256 devices in a mesh: lat: 8 (over x_lo, y), lon: 32 (over x_hi, z, core).
Axes of the slice: x: 4 (x_hi: 2, x_lo: 2; x = x_hi * 2 + x_lo), y: 4, z: 8, core: 2. Of those that a mesh axis runs over, the one named last changes fastest.
Arguments:
- tokens: bfloat16 [2, 48, 384, 512], P(None, 'lat', 'lon'), may hold values from -6 to 6
- coarse: bfloat16 [2, 24, 192, 1024], P(None, 'lat', 'lon'), may hold values from -6 to 6
- output_cotangent: bfloat16 [2, 48, 384, 512], P(None, 'lat', 'lon'), may hold values from -6 to 6
- token_class: int32 [2, 48, 384], P(None, 'lat', 'lon'), may hold values 0 or 1
- relative_index: int32 [144, 144], replicated, may hold values from 0 to 758
- encoder_gain: float32 [512], replicated, may hold values from 0.1 to 1.9
- encoder_offset: float32 [512], replicated, may hold values from -3 to 3
- encoder_projection: bfloat16 [512, 1536], replicated, may hold values from -0.25 to 0.25
- encoder_projection_bias: float32 [1536], replicated, may hold values from -3 to 3
- encoder_output_weight: bfloat16 [512, 512], replicated, may hold values from -0.25 to 0.25
- encoder_output_bias: float32 [512], replicated, may hold values from -3 to 3
- encoder_table: float32 [8, 759], replicated, may hold values from -6 to 323, as said below
- decoder_gain: float32 [512], replicated, may hold values from 0.1 to 1.9
- decoder_offset: float32 [512], replicated, may hold values from -3 to 3
- decoder_projection: bfloat16 [512, 1536], replicated, may hold values from -0.25 to 0.25
- decoder_projection_bias: float32 [1536], replicated, may hold values from -3 to 3
- decoder_output_weight: bfloat16 [512, 512], replicated, may hold values from -0.25 to 0.25
- decoder_output_bias: float32 [512], replicated, may hold values from -3 to 3
- decoder_table: float32 [8, 759], replicated, may hold values from -6 to 323, as said below
- split_weight: bfloat16 [1024, 2048], replicated, may hold values from -0.1875 to 0.1875
- split_bias: float32 [2048], replicated, may hold values from -3 to 3
Outputs:
- decoded: bfloat16 [2, 48, 384, 512], P(None, 'lat', 'lon')
- tokens_gradient: bfloat16 [2, 48, 384, 512], P(None, 'lat', 'lon')
- coarse_gradient: bfloat16 [2, 24, 192, 1024], P(None, 'lat', 'lon')
The draws below stay inside these ranges and needn't reach their ends.
Inputs may be any that keep to these rules, and one draw needn't show every extreme that they name: `encoder_table`: learned relative-position biases. `decoder_table`: learned relative-position biases.
All inputs are finite; a program needn't handle non-finite values. No bound on the sum of `token_class` on one device may be relied on, other than what follows from the above.
Results may differ from the reference program's by a relative error of at most 0.025.
Values may be sent and summed in bfloat16 or wider, within the bound.
No kernel may reach another device: no remote copies, remote signals or barrier semaphores. Data moves between devices by JAX's collectives and lax.ppermute only.
A program may use at most 64 MiB of HBM per device.

```python
import jax
import jax.numpy as jnp
from jax import lax

D = 512
HEADS = 8
LEVELS = 2
WIN_LAT = 6
WIN_LON = 12
SPAN = 144
RELATIVE = 759
NLAT = 48
NLON = 384


def bias_table(key):
    first, second = jax.random.split(key, 2)
    base = jnp.clip(jax.random.normal(first, (HEADS, RELATIVE), jnp.float32), -6.0, 6.0)
    picked = jax.random.uniform(second, (HEADS, RELATIVE)) < 0.05
    return jnp.where(picked, base, base)


def draw_encoder_table(key, part):
    key = jax.random.fold_in(key, 17)
    return bias_table(key)


def draw_decoder_table(key, part):
    key = jax.random.fold_in(key, 29)
    return bias_table(key)


def with_ends(entries, stream_key, smallest, largest):
    dims = entries.shape
    spot = [jax.random.randint(jax.random.fold_in(stream_key, axis), (), 0, dims[axis]) for axis in range(len(dims))]
    entries = entries.at[tuple(spot)].set(smallest)
    longest = dims.index(max(dims))
    spot[longest] = (spot[longest] + 1) % dims[longest]
    return entries.at[tuple(spot)].set(largest)


def shard_levels(own_key, dims, pieces, least, high):
    level, own = 1.0, jax.random.fold_in(own_key, 6)
    for dim, shards_of in pieces:
        steps = jnp.exp(jax.random.uniform(jax.random.fold_in(own, dim), (shards_of,), jnp.float32, least / len(pieces), high / len(pieces)))
        level = level * jnp.repeat(steps, dims[dim] // shards_of).reshape([-1 if axis == dim else 1 for axis in range(len(dims))])
    return level


def normal_values(key, extent, scale, reach, cuts=(), dtype=jnp.bfloat16):
    values = jax.random.normal(key, extent, jnp.float32) * scale
    if len(cuts) > 0:
        values = shard_levels(key, extent, cuts, -0.22, 0.18) * values
    return jnp.clip(values, min=-reach, max=reach).astype(dtype)


def setup_inputs(seed: int = 0) -> dict:
    key_list = jax.random.split(jax.random.key(seed), 22)
    return {
        "tokens": normal_values(key_list[0], (LEVELS, NLAT, NLON, D), 1.0, 6.0, ((1, 8), (2, 32))),
        "coarse": normal_values(key_list[1], (LEVELS, NLAT // 2, NLON // 2, 2 * D), 1.0, 6.0, ((1, 8), (2, 32))),
        "output_cotangent": normal_values(key_list[2], (LEVELS, NLAT, NLON, D), 1.0, 6.0, ((1, 8), (2, 32))),
        "token_class": with_ends((jax.random.randint(key_list[3], (LEVELS, NLAT, NLON), 0, 2) < 1).astype(jnp.int32), jax.random.fold_in(key_list[3], 1), 0, 1),
        "relative_index": with_ends(jax.random.randint(key_list[4], (SPAN, SPAN), 0, RELATIVE), jax.random.fold_in(key_list[4], 1), 0, RELATIVE - 1).astype(jnp.int32),
        "encoder_gain": jnp.clip(1.0 + 0.18 * jax.random.normal(key_list[5], (D,), jnp.float32), 0.1, 1.9),
        "encoder_offset": normal_values(key_list[6], (D,), 0.3, 3.0, (), jnp.float32),
        "encoder_projection": normal_values(key_list[7], (D, 3 * D), D ** -0.5, 0.25),
        "encoder_projection_bias": normal_values(key_list[8], (3 * D,), 0.5, 3.0, (), jnp.float32),
        "encoder_output_weight": normal_values(key_list[9], (D, D), D ** -0.5, 0.25),
        "encoder_output_bias": normal_values(key_list[10], (D,), 0.3, 3.0, (), jnp.float32),
        "encoder_table": draw_encoder_table(jax.random.fold_in(key_list[21], 71), 0),
        "decoder_gain": jnp.clip(1.0 + 0.18 * jax.random.normal(key_list[12], (D,), jnp.float32), 0.1, 1.9),
        "decoder_offset": normal_values(key_list[13], (D,), 0.3, 3.0, (), jnp.float32),
        "decoder_projection": normal_values(key_list[14], (D, 3 * D), D ** -0.5, 0.25),
        "decoder_projection_bias": normal_values(key_list[15], (3 * D,), 0.5, 3.0, (), jnp.float32),
        "decoder_output_weight": normal_values(key_list[16], (D, D), D ** -0.5, 0.25),
        "decoder_output_bias": normal_values(key_list[17], (D,), 0.3, 3.0, (), jnp.float32),
        "decoder_table": draw_decoder_table(jax.random.fold_in(key_list[21], 71), 0),
        "split_weight": normal_values(key_list[19], (2 * D, 4 * D), (2 * D) ** -0.5, 0.1875),
        "split_bias": normal_values(key_list[20], (4 * D,), 0.3, 3.0, (), jnp.float32),
    }


eps = 1e-05

def layer_norm(values, gain, offset):
    widened = values.astype(jnp.float32)
    centred = widened - lax.optimization_barrier(jnp.mean(widened, axis=-1, keepdims=True))
    variance = lax.optimization_barrier(jnp.mean(centred * centred, axis=-1, keepdims=True))
    return centred * lax.rsqrt(variance + eps) * gain + offset

def project(values, gain, offset, weight, bias):
    normed = layer_norm(values, gain, offset).astype(jnp.bfloat16)
    flat = normed.reshape(-1, normed.shape[-1])
    mixed = jnp.dot(flat, weight, preferred_element_type=jnp.float32) + bias
    return mixed.astype(jnp.bfloat16).reshape(values.shape[:-1] + (weight.shape[1],))

def to_windows(grid):
    levels, height, breadth, features = grid.shape
    split = grid.reshape(levels, height // WIN_LAT, WIN_LAT, breadth // WIN_LON, WIN_LON, features)
    split = split.transpose(1, 3, 0, 2, 4, 5)
    return split.reshape(height // WIN_LAT * (breadth // WIN_LON), levels * WIN_LAT * WIN_LON, features)

def from_windows(windows, height, breadth):
    features = windows.shape[-1]
    split = windows.reshape(height // WIN_LAT, breadth // WIN_LON, LEVELS, WIN_LAT, WIN_LON, features)
    return split.transpose(2, 0, 3, 1, 4, 5).reshape(LEVELS, height, breadth, features)

def attend_windows(projected, allowed, bias_full):
    count, span, triple = projected.shape
    features = triple // 3
    head_size = features // HEADS
    queries = projected[..., :features].reshape(count, span, HEADS, head_size).astype(jnp.float32)
    keys_part = projected[..., features:2 * features].reshape(count, span, HEADS, head_size).astype(jnp.float32)
    values_part = projected[..., 2 * features:].reshape(count, span, HEADS, head_size).astype(jnp.float32)
    scores = jnp.einsum('wqhd,wkhd->whqk', queries, keys_part) * head_size ** (-0.5) + bias_full[None]
    scores = jnp.where(allowed[:, None], scores, -1e+30)
    probs = jax.nn.softmax(scores, axis=-1).astype(jnp.bfloat16)
    mixed = jnp.einsum('whqk,wkhd->wqhd', probs.astype(jnp.float32), values_part)
    return mixed.reshape(count, span, features).astype(jnp.bfloat16)

def swin_block(grid, token_class, gain, offset, weight, bias, out_weight, out_bias, bias_full):
    height, breadth, features = (grid.shape[1], grid.shape[2], grid.shape[3])
    half_lat = WIN_LAT // 2
    half_lon = WIN_LON // 2
    projected = project(grid, gain, offset, weight, bias)
    rolled = jnp.roll(projected, (-half_lat, -half_lon), axis=(1, 2))
    classes_rolled = jnp.roll(token_class, (-half_lat, -half_lon), axis=(1, 2))
    seam_flag = (jnp.arange(height) >= height - half_lat).astype(jnp.int32)
    labels = classes_rolled * 2 + seam_flag[None, :, None]
    window_labels = to_windows(labels[..., None])[..., 0]
    allowed = window_labels[:, :, None] == window_labels[:, None, :]
    window_proj = to_windows(rolled)
    groups = height // WIN_LAT
    per_group = breadth // WIN_LON
    span = window_proj.shape[1]
    mixed = lax.map(lambda window_pair: attend_windows(window_pair[0], window_pair[1], bias_full), (window_proj.reshape(groups, per_group, span, 3 * features), allowed.reshape(groups, per_group, span, span)))
    heads_out = from_windows(mixed.reshape(groups * per_group, span, features), height, breadth)
    heads_out = jnp.roll(heads_out, (half_lat, half_lon), axis=(1, 2))
    attended = jnp.dot(heads_out.reshape(-1, features), out_weight, preferred_element_type=jnp.float32) + out_bias
    return (grid.astype(jnp.float32) + attended.reshape(grid.shape)).astype(jnp.bfloat16)

def expand(coarse, weight, bias):
    levels, height, breadth, features = coarse.shape
    flat = jnp.dot(coarse.reshape(-1, features), weight, preferred_element_type=jnp.float32) + bias
    fine = flat.reshape(levels, height, breadth, 2, 2, features // 2)
    return fine.transpose(0, 1, 3, 2, 4, 5).reshape(levels, 2 * height, 2 * breadth, features // 2)

def reference(tokens, coarse, output_cotangent, token_class, relative_index, encoder_gain, encoder_offset, encoder_projection, encoder_projection_bias, encoder_output_weight, encoder_output_bias, encoder_table, decoder_gain, decoder_offset, decoder_projection, decoder_projection_bias, decoder_output_weight, decoder_output_bias, decoder_table, split_weight, split_bias):
    encoder_bias = encoder_table[:, relative_index]
    decoder_bias = decoder_table[:, relative_index]

    def forward(inputs, lowres):
        encoded = swin_block(inputs, token_class, encoder_gain, encoder_offset, encoder_projection, encoder_projection_bias, encoder_output_weight, encoder_output_bias, encoder_bias)
        joined = (encoded.astype(jnp.float32) + expand(lowres, split_weight, split_bias)).astype(jnp.bfloat16)
        return swin_block(joined, token_class, decoder_gain, decoder_offset, decoder_projection, decoder_projection_bias, decoder_output_weight, decoder_output_bias, decoder_bias)
    decoded, pullback = jax.vjp(forward, tokens, coarse)
    tokens_gradient, coarse_gradient = pullback(output_cotangent)
    return (decoded, tokens_gradient, coarse_gradient)
```

```python
import functools

import jax
import jax.numpy as jnp
from jax import lax
from jax.experimental import pallas as pl
from jax.experimental.pallas import tpu as pltpu
from jax.sharding import PartitionSpec as P

HEADS = 8
LEVELS = 2
WIN_LAT = 6
WIN_LON = 12
SPAN = LEVELS * WIN_LAT * WIN_LON
D = 512
HEAD = D // HEADS
WIDE = 256
HL, HN = WIN_LAT // 2, WIN_LON // 2
PAIRS = HL * HN
GROUP = 4
BLANK = -1e30
eps = 1e-05

f32, bf16 = jnp.float32, jnp.bfloat16
NT = (((1,), (1,)), ((), ()))
TN = (((0,), (0,)), ((), ()))


def dot(a, b):
    return jnp.dot(a, b, preferred_element_type=f32)


def dot_nt(a, b):
    return lax.dot_general(a, b, NT, preferred_element_type=f32)


def dot_tn(a, b):
    return lax.dot_general(a, b, TN, preferred_element_type=f32)


def gather_quadrants(refs, base, scratch):
    for q, ref in enumerate(refs):
        for t in range(PAIRS):
            scratch[pl.ds(2 * (q * PAIRS + t), 2), :] = ref[base + t].astype(f32)


def scatter_quadrants(scratch, refs, base):
    for q, ref in enumerate(refs):
        for t in range(PAIRS):
            ref[base + t] = scratch[pl.ds(2 * (q * PAIRS + t), 2), :].astype(bf16)


def token_place(t):
    rest = t % (2 * PAIRS)
    return t // (2 * PAIRS), rest // (2 * HN), rest % (2 * HN) // 2, rest % 2


def normalise(x):
    centred = x - jnp.mean(x, axis=-1, keepdims=True)
    variance = jnp.mean(centred * centred, axis=-1, keepdims=True)
    rstd = lax.rsqrt(variance + eps)
    return centred * rstd, rstd


def head_masks(dtype):
    lane = lax.broadcasted_iota(jnp.int32, (1, GROUP * HEAD), 1) // HEAD
    return [(lane == h).astype(dtype) for h in range(GROUP)]


def stack_heads(x):
    return jnp.concatenate([x * m for m in head_masks(x.dtype)], axis=0)


def merge_heads(y):
    masks = head_masks(f32)
    total = y[:SPAN] * masks[0]
    for h in range(1, GROUP):
        total = total + y[h * SPAN : (h + 1) * SPAN] * masks[h]
    return total


def mask_bias(refs, is_last):
    token = lax.broadcasted_iota(jnp.int32, (1, WIDE), 1)
    quadrant, r, c, level = token_place(token)
    lane = HN * (1 - quadrant % 2) + c
    hot = lax.broadcasted_iota(jnp.int32, (128, WIDE), 0) == lane
    rows = jnp.concatenate([ref[CLASS_AT + r, :, :128].astype(f32) for ref in refs for r in range(HL)], axis=0)
    spread = dot(rows.astype(bf16), hot.astype(f32).astype(bf16))
    mine = lax.broadcasted_iota(jnp.int32, (4 * HL * LEVELS, WIDE), 0) == (quadrant * HL + r) * LEVELS + level
    seam = (quadrant // 2).astype(f32) * is_last.astype(f32)
    label = 2.0 * jnp.sum(jnp.where(mine, spread, 0.0), axis=0, keepdims=True) + seam
    label = jnp.where(token < SPAN, label, 9.0)
    eye = lax.broadcasted_iota(jnp.int32, (SPAN, WIDE), 0) == lax.broadcasted_iota(jnp.int32, (SPAN, WIDE), 1)
    column = jnp.sum(jnp.where(eye, label, 0.0), axis=1, keepdims=True)
    return jnp.where(column == label, 0.0, BLANK)


def pad_keys(x):
    return jnp.concatenate([x, jnp.zeros((WIDE - SPAN, x.shape[1]), x.dtype)], axis=0)


def block_forward(x, blank, bias_of, gain, offset, weight, bias, out_weight, out_bias, qkv_ref, probs_ref):
    xhat, _ = normalise(x)
    normed = (xhat * gain + offset).astype(bf16)
    queries = (dot(normed, weight[:, :D]) + bias[:, :D]).astype(bf16) * jnp.array(HEAD**-0.5, bf16)
    qkv_ref[:, :D] = queries
    qkv_ref[:, D:] = (dot(normed, weight[:, D:]) + bias[:, D:]).astype(bf16)
    mixed = []
    for g in range(HEADS // GROUP):
        lanes = pl.ds(g * GROUP * HEAD, GROUP * HEAD)
        q4 = stack_heads(qkv_ref[:, pl.ds(g * 256, 256)])
        k4 = pad_keys(qkv_ref[:, pl.ds(D + g * 256, 256)])
        v4 = pad_keys(qkv_ref[:, pl.ds(2 * D + g * 256, 256)])
        scores = dot_nt(q4, k4)
        for h in range(GROUP):
            s = scores[h * SPAN : (h + 1) * SPAN] + bias_of(g * GROUP + h) + blank
            e = jnp.exp(s - jnp.max(s, axis=-1, keepdims=True))
            p = e * (1.0 / jnp.sum(e, axis=-1, keepdims=True))
            probs_ref[pl.ds((g * GROUP + h) * SPAN, SPAN), :] = p.astype(bf16)
        p4 = probs_ref[pl.ds(g * GROUP * SPAN, GROUP * SPAN), :]
        mixed.append(merge_heads(dot(p4, v4)))
    heads_out = jnp.concatenate(mixed, axis=1).astype(bf16)
    return x + dot(heads_out, out_weight) + out_bias


def block_backward(grad, x, gain, weight, out_weight, qkv_ref, probs_ref, dqkv_ref):
    dheads = dot_nt(grad, out_weight).astype(bf16)
    for g in range(HEADS // GROUP):
        q4 = stack_heads(qkv_ref[:, pl.ds(g * 256, 256)])
        k4 = pad_keys(qkv_ref[:, pl.ds(D + g * 256, 256)])
        v4 = pad_keys(qkv_ref[:, pl.ds(2 * D + g * 256, 256)])
        do4 = stack_heads(dheads[:, g * 256 : (g + 1) * 256])
        p4 = probs_ref[pl.ds(g * GROUP * SPAN, GROUP * SPAN), :]
        dprobs = dot_nt(do4, v4)
        pf = p4.astype(f32)
        weighted = pf * dprobs
        ds = (weighted - pf * jnp.sum(weighted, axis=-1, keepdims=True)).astype(bf16)
        dq = merge_heads(dot(ds, k4)) * HEAD**-0.5
        dk = dot_tn(ds[:, :SPAN], q4)
        dv = dot_tn(p4[:, :SPAN], do4)
        dqkv_ref[:, pl.ds(g * 256, 256)] = dq.astype(bf16)
        dqkv_ref[:, pl.ds(D + g * 256, 256)] = dk.astype(bf16)
        dqkv_ref[:, pl.ds(2 * D + g * 256, 256)] = dv.astype(bf16)
    dnormed = dot_nt(dqkv_ref[...], weight).astype(bf16).astype(f32)
    xhat, rstd = normalise(x)
    dxhat = dnormed * gain
    dx = rstd * (
        dxhat
        - jnp.mean(dxhat, axis=-1, keepdims=True)
        - xhat * jnp.mean(dxhat * xhat, axis=-1, keepdims=True)
    )
    return grad.astype(f32) + dx.astype(bf16).astype(f32)


COARSE_ROWS, COARSE_COLS = HL // 2 + 1, HN // 2
POINTS = COARSE_ROWS * COARSE_COLS
COTANGENT_AT = PAIRS
COARSE_AT = 2 * PAIRS
CLASS_AT = 2 * PAIRS + 2 * POINTS


TILES = CLASS_AT + HL


def pack_kernel(tokens, cotangent, coarse, classes, o0, o1, o2, o3, kinds, tiles, sems, first_sem):
    outs = (o0, o1, o2, o3)
    fetch = pltpu.make_async_copy(classes, kinds, first_sem)
    fetch.start()
    copies = []

    def send(src, dst):
        copy = pltpu.make_async_copy(src, dst, sems.at[len(copies)])
        copy.start()
        copies.append(copy)

    for q in (3, 2, 1, 0):
        qr, qc = divmod(q, 2)
        lat, lon = HL * (1 - qr), HN * (1 - qc)
        low_lat = (coarse.shape[0] - COARSE_ROWS) * (1 - qr)
        for r in range(HL):
            send(tokens.at[lat + r, pl.ds(lon, HN)], outs[q].at[pl.ds(r * HN, HN)])
            send(cotangent.at[lat + r, pl.ds(lon, HN)], outs[q].at[pl.ds(COTANGENT_AT + r * HN, HN)])
        for r in range(COARSE_ROWS):
            for half in range(2):
                send(
                    coarse.at[low_lat + r, pl.ds(COARSE_COLS * (1 - qc), COARSE_COLS), :, pl.ds(D * half, D)],
                    outs[q].at[pl.ds(COARSE_AT + POINTS * half + r * COARSE_COLS, COARSE_COLS)],
                )
    tiles[...] = jnp.zeros_like(tiles)
    fetch.wait()
    for r in range(WIN_LAT):
        tiles[r, :, pl.ds(0, WIN_LON)] = kinds[r].astype(f32).astype(bf16)
    for q in (3, 2, 1, 0):
        send(tiles.at[pl.ds(HL * (1 - q // 2), HL)], outs[q].at[pl.ds(CLASS_AT, HL)])
    for copy in copies:
        copy.wait()


def lookup_kernel(inputs_ref, out_ref, rest_ref, low, high, packed_low, packed_high, parts):
    token = lax.broadcasted_iota(jnp.int32, (SPAN, 1), 0)
    quadrant, r, c, level = token_place(token)
    old = level * (WIN_LAT * WIN_LON) + (quadrant // 2 * HL + r) * WIN_LON + quadrant % 2 * HN + c
    order = (lax.broadcasted_iota(jnp.int32, (SPAN, SPAN), 1) == old).astype(f32).astype(bf16)
    index = inputs_ref[:SPAN, :SPAN].astype(jnp.int32)
    rest = SPAN - 128

    lane = lax.broadcasted_iota(jnp.int32, (rest, WIDE), 1)
    spread = (lane % rest == lax.broadcasted_iota(jnp.int32, (rest, WIDE), 0)).astype(f32).astype(bf16)
    own = (
        lax.broadcasted_iota(jnp.int32, (SPAN, WIDE), 1) // rest
        == lax.broadcasted_iota(jnp.int32, (SPAN, WIDE), 0) % rest
    )
    for part, full, packed in ((index % WIDE, low, packed_low), (index // WIDE, high, packed_high)):
        moved = dot_nt(dot(order, part.astype(f32).astype(bf16)).astype(bf16), order)
        full[...] = moved[:, :128]
        tail = jnp.where(own, dot(moved[:, 128:].astype(bf16), spread), 0.0)
        for g in range(SPAN // rest):
            packed[pl.ds(g, 1), :] = jnp.sum(tail[rest * g : rest * (g + 1)], axis=0, keepdims=True)

    left = inputs_ref[SPAN:]
    blocks = left.shape[1] // WIDE
    for k in range(3):
        piece = left.astype(bf16)
        left = left - piece.astype(f32)
        for b in range(blocks):
            parts[pl.ds((b * 3 + k) * 2 * HEADS, 2 * HEADS), :] = piece[:, b * WIDE : (b + 1) * WIDE]
    entries = parts[...]
    ids = lax.broadcasted_iota(jnp.int32, (16, WIDE), 0).astype(f32)
    ids = [(ids + 16 * n).astype(bf16) for n in range(WIDE // 16)]
    one, zero = jnp.ones((16, WIDE), bf16), jnp.zeros((16, WIDE), bf16)

    def look(low_row, high_row):
        wanted = jnp.broadcast_to(low_row, (16, WIDE)).astype(bf16)
        hot = jnp.concatenate([jnp.where(wanted == i, one, zero) for i in ids], axis=0)
        found = dot(entries, hot)
        sums = []
        for b in range(blocks):
            at = [found[(b * 3 + k) * 2 * HEADS : (b * 3 + k + 1) * 2 * HEADS] for k in range(3)]
            sums.append(at[0] + at[1] + at[2])
        result = sums[0]
        for b in range(1, blocks):
            result = jnp.where(high_row == b, sums[b], result)
        return result

    def two_rows(i):
        def pair(ref):
            return jnp.concatenate([ref[pl.ds(i, 1), :], ref[pl.ds(i + 1, 1), :]], axis=1)

        result = look(pair(low), pair(high))
        for n in range(2):
            for half in range(2):
                out_ref[pl.ds(half * HEADS * SPAN + i + n, HEADS, stride=SPAN), :] = result[
                    half * HEADS : (half + 1) * HEADS, n * 128 : (n + 1) * 128
                ]

    @pl.loop(0, SPAN // 8)
    def _(step):
        for n in range(4):
            two_rows(8 * step + 2 * n)

    for g in range(SPAN // rest):
        result = look(packed_low[pl.ds(g, 1), :], packed_high[pl.ds(g, 1), :])
        for n in range(rest):
            first = n * rest // 128 * 128
            for half in range(2):
                rest_ref[pl.ds(half * HEADS * SPAN + rest * g + n, HEADS, stride=SPAN), :] = pltpu.roll(
                    result[half * HEADS : (half + 1) * HEADS, first : first + 128], (first - n * rest) % 128, axis=1
                )


def lookup(relative_index, encoder_table, decoder_table):
    blocks = -(-encoder_table.shape[1] // WIDE)

    def widen(rows):
        return jnp.pad(rows, ((0, 0), (0, blocks * WIDE - rows.shape[1])))

    inputs = jnp.concatenate([widen(relative_index.astype(f32)), widen(encoder_table), widen(decoder_table)], axis=0)
    return pl.pallas_call(
        lookup_kernel,
        out_shape=[jax.ShapeDtypeStruct((2 * HEADS * SPAN, 128), f32)] * 2,
        scratch_shapes=[
            pltpu.VMEM((SPAN, 128), f32),
            pltpu.VMEM((SPAN, 128), f32),
            pltpu.VMEM((16, WIDE), f32),
            pltpu.VMEM((16, WIDE), f32),
            pltpu.VMEM((blocks * 3 * 2 * HEADS, WIDE), bf16),
        ],
        compiler_params=pltpu.CompilerParams(vmem_limit_bytes=32 * 2**20),
        cost_estimate=pl.CostEstimate(flops=3_000_000_000, bytes_accessed=4_000_000, transcendentals=0),
        name="lookup",
    )(inputs)


def main_kernel(
    b0, b1, b2, b3, bias_main, bias_rest, is_last,
    e_gain, e_offset, e_bias, e_out_bias, d_gain, d_offset, d_bias, d_out_bias, split_bias,
    e_weight, e_out_weight, d_weight, d_out_weight, split,
    o0, o1, o2, o3, joined_grad, tokens, e_qkv, e_probs,
    scratch, coarse, fine, d_qkv, d_probs, dqkv,
):
    def bias_rows(h):
        rows = pl.ds(h * SPAN, SPAN)
        return jnp.concatenate([bias_main[rows, :], bias_rest[rows, :]], axis=1)

    parts = (b0, b1, b2, b3)
    gather_quadrants(parts, 0, scratch)
    x = scratch[...]
    tokens[...] = x.astype(bf16)
    blank = mask_bias(parts, is_last[0])
    encoded = block_forward(
        x, blank, lambda h: bias_rows(h), e_gain[...], e_offset[...], e_weight,
        e_bias[...].reshape(1, -1), e_out_weight[...], e_out_bias[...], e_qkv, e_probs,
    ).astype(bf16)

    for q, ref in enumerate(parts):
        qr, qc = divmod(q, 2)
        for r in range(COARSE_ROWS):
            for c in range(COARSE_COLS):
                at = (qr * COARSE_ROWS + r) * 2 * COARSE_COLS + qc * COARSE_COLS + c
                for half in range(2):
                    coarse[pl.ds(2 * at, 2), pl.ds(D * half, D)] = ref[
                        COARSE_AT + POINTS * half + r * COARSE_COLS + c
                    ].astype(f32)
    lowres = coarse[...].astype(bf16)
    fine[...] = dot(lowres, split[...]) + split_bias[...]
    for q in range(4):
        qr, qc = divmod(q, 2)
        for r in range(HL):
            for c in range(HN):
                row, column = qr * HL + r + HL % 2, qc * HN + c + HN % 2
                at = (row // 2) * 2 * COARSE_COLS + column // 2
                kind = (row % 2) * 2 + column % 2
                scratch[pl.ds(2 * (q * PAIRS + r * HN + c), 2), :] = fine[pl.ds(2 * at, 2), pl.ds(kind * D, D)]
    x = (encoded.astype(f32) + scratch[...]).astype(bf16).astype(f32)
    decoded = block_forward(
        x, blank, lambda h: bias_rows(HEADS + h), d_gain[...], d_offset[...], d_weight,
        d_bias[...].reshape(1, -1), d_out_weight[...], d_out_bias[...], d_qkv, d_probs,
    )
    outs = (o0, o1, o2, o3)
    scratch[...] = decoded
    scatter_quadrants(scratch, outs, 0)
    gather_quadrants(parts, COTANGENT_AT, scratch)
    grad = scratch[...].astype(bf16)
    dx = block_backward(grad, x, d_gain[...], d_weight[...], d_out_weight[...], d_qkv, d_probs, dqkv)
    scratch[...] = dx
    joined_grad[...] = dx.astype(bf16)
    scatter_quadrants(scratch, outs, PAIRS)


def encoder_back_kernel(grad, tokens, qkv, probs, gain, weight, out_weight, t0, t1, t2, t3, scratch, dqkv):
    x = tokens[...].astype(f32)
    scratch[...] = block_backward(grad[...], x, gain[...], weight[...], out_weight[...], qkv, probs, dqkv)
    scatter_quadrants(scratch, (t0, t1, t2, t3), 0)


def coarse_kernel(j0, j1, j2, j3, split, out, decoded, fine, result, sems):
    copies = []
    for q, ref in enumerate((j0, j1, j2, j3)):
        for r in range(HL):
            copy = pltpu.make_async_copy(
                ref.at[pl.ds(r * HN, HN)],
                decoded.at[q // 2 * HL + r, pl.ds(q % 2 * HN, HN)],
                sems.at[len(copies)],
            )
            copy.start()
            copies.append(copy)
    columns = WIN_LON // 2
    for q, ref in enumerate((j0, j1, j2, j3)):
        qr, qc = divmod(q, 2)
        for r in range(HL):
            for c in range(HN):
                row, column = qr * HL + r, qc * HN + c
                at = (row // 2) * columns + column // 2
                kind = (row % 2) * 2 + column % 2
                fine[pl.ds(2 * at, 2), pl.ds(kind * D, D)] = ref[PAIRS + r * HN + c].astype(f32)
    result[...] = dot_nt(fine[...].astype(bf16), split[...])
    for t in range(out.shape[0]):
        out[t] = result[pl.ds(2 * t, 2), :].astype(bf16)
    for copy in copies:
        copy.wait()


VM = pl.BlockSpec(memory_space=pltpu.VMEM)


ANY = pl.BlockSpec(memory_space=pl.ANY)


def call(kernel, name, inputs, outs, scratch, flops, in_specs=None, out_specs=None, vmem=32):
    return pl.pallas_call(
        kernel,
        out_shape=outs,
        in_specs=in_specs or [VM] * len(inputs),
        out_specs=out_specs or [VM] * len(outs),
        scratch_shapes=scratch,
        compiler_params=pltpu.CompilerParams(vmem_limit_bytes=vmem * 2**20),
        cost_estimate=pl.CostEstimate(flops=flops, bytes_accessed=flops // 1000, transcendentals=0),
        name=name,
    )(*inputs)


def shift_pairs(lat, lon, lats, lons):
    return [
        (i * lons + j, ((i + lat) % lats) * lons + (j + lon) % lons) for i in range(lats) for j in range(lons)
    ]


def exchange(pieces, steps, lats, lons):
    out = [pieces[0]]
    for q in range(1, 4):
        qr, qc = divmod(q, 2)
        out.append(lax.ppermute(pieces[q], ("lat", "lon"), shift_pairs(qr * steps, qc * steps, lats, lons)))
    return out


def per_device(
    lats, lons,
    tokens, coarse, output_cotangent, token_class, relative_index,
    encoder_gain, encoder_offset, encoder_projection, encoder_projection_bias,
    encoder_output_weight, encoder_output_bias, encoder_table,
    decoder_gain, decoder_offset, decoder_projection, decoder_projection_bias,
    decoder_output_weight, decoder_output_bias, decoder_table,
    split_weight, split_bias,
):
    def row(v):
        return v.reshape(1, -1)

    s = jax.ShapeDtypeStruct
    packed = call(
        pack_kernel,
        "pack",
        [
            jnp.transpose(tokens, (1, 2, 0, 3)),
            jnp.transpose(output_cotangent, (1, 2, 0, 3)),
            jnp.transpose(coarse, (1, 2, 0, 3)),
            jnp.transpose(token_class, (1, 0, 2)),
        ],
        [s((TILES, LEVELS, D), bf16)] * 4,
        [
            pltpu.VMEM((WIN_LAT, LEVELS, WIN_LON), jnp.int32),
            pltpu.VMEM((WIN_LAT, LEVELS, D), bf16),
            pltpu.SemaphoreType.DMA((4 * (2 * HL + 2 * COARSE_ROWS + 1),)),
            pltpu.SemaphoreType.DMA(()),
        ],
        100_000_000,
        [ANY] * 4,
        [ANY] * 4,
        60,
    )
    parts = exchange(packed, -1, lats, lons)
    biases = lookup(relative_index, encoder_table, decoder_table)
    is_last = (lax.axis_index("lat") == lats - 1).astype(jnp.int32).reshape(1)
    half = s((2 * PAIRS, LEVELS, D), bf16)
    quarter = s((PAIRS, LEVELS, D), bf16)
    points = 4 * LEVELS * POINTS
    outs = call(
        main_kernel,
        "main",
        [
            *parts, *biases, is_last,
            row(encoder_gain), row(encoder_offset), encoder_projection_bias, row(encoder_output_bias),
            row(decoder_gain), row(decoder_offset), decoder_projection_bias, row(decoder_output_bias),
            row(split_bias),
            encoder_projection, encoder_output_weight, decoder_projection, decoder_output_weight, split_weight,
        ],
        [half] * 4
        + [s((SPAN, D), bf16), s((SPAN, D), bf16), s((SPAN, 3 * D), bf16), s((HEADS * SPAN, WIDE), bf16)],
        [
            pltpu.VMEM((SPAN, D), f32),
            pltpu.VMEM((points, 2 * D), f32),
            pltpu.VMEM((points, 4 * D), f32),
            pltpu.VMEM((SPAN, 3 * D), bf16),
            pltpu.VMEM((HEADS * SPAN, WIDE), bf16),
            pltpu.VMEM((SPAN, 3 * D), bf16),
        ],
        5_000_000_000,
        [VM] * 6 + [pl.BlockSpec(memory_space=pltpu.SMEM)] + [VM] * 14,
    )
    home = exchange(outs[:4], 1, lats, lons)
    joined_grad, kept_tokens, qkv, probs = outs[4:]
    token_grads = call(
        encoder_back_kernel,
        "encoder_back",
        [joined_grad, kept_tokens, qkv, probs, row(encoder_gain), encoder_projection, encoder_output_weight],
        [quarter] * 4,
        [pltpu.VMEM((SPAN, D), f32), pltpu.VMEM((SPAN, 3 * D), bf16)],
        3_000_000_000,
    )
    home, token_grads = lax.optimization_barrier((home, token_grads))
    home_tokens = exchange(token_grads, 1, lats, lons)
    low_tokens = SPAN // 4
    coarse_gradient, decoded = call(
        coarse_kernel,
        "coarse_back",
        [home[3 - q] for q in range(4)] + [split_weight],
        [s((low_tokens // LEVELS, LEVELS, 2 * D), bf16), s((WIN_LAT, WIN_LON, LEVELS, D), bf16)],
        [
            pltpu.VMEM((low_tokens, 4 * D), f32),
            pltpu.VMEM((low_tokens, 2 * D), f32),
            pltpu.SemaphoreType.DMA((4 * HL,)),
        ],
        1_000_000,
        None,
        [VM, ANY],
    )
    coarse_gradient = jnp.transpose(
        coarse_gradient.reshape(WIN_LAT // 2, WIN_LON // 2, LEVELS, 2 * D), (2, 0, 1, 3)
    )

    def assemble(parts):
        parts = [p.reshape(HL, HN, LEVELS, D) for p in parts]
        upper = jnp.concatenate([parts[3], parts[2]], axis=1)
        lower = jnp.concatenate([parts[1], parts[0]], axis=1)
        return jnp.transpose(jnp.concatenate([upper, lower], axis=0), (2, 0, 1, 3))

    return jnp.transpose(decoded, (2, 0, 1, 3)), assemble(home_tokens), coarse_gradient


def solution(mesh):
    cut = P(None, "lat", "lon", None)
    in_specs = (cut, cut, cut, P(None, "lat", "lon")) + (P(),) * 17
    return jax.shard_map(
        functools.partial(per_device, mesh.shape["lat"], mesh.shape["lon"]),
        mesh=mesh,
        in_specs=in_specs,
        out_specs=(cut, cut, cut),
        check_vma=False,
    )
```

```python
import functools

import jax
import jax.numpy as jnp
from jax import lax
from jax.experimental import pallas as pl
from jax.experimental.pallas import tpu as pltpu
from jax.sharding import PartitionSpec as P

HEADS = 8
LEVELS = 2
WIN_LAT = 6
WIN_LON = 12
SPAN = LEVELS * WIN_LAT * WIN_LON
D = 512
HEAD = D // HEADS
WIDE = 256
HL, HN = WIN_LAT // 2, WIN_LON // 2
PAIRS = HL * HN
GROUP = 4
BLANK = -1e30
eps = 1e-05

f32, bf16 = jnp.float32, jnp.bfloat16
NT = (((1,), (1,)), ((), ()))
TN = (((0,), (0,)), ((), ()))


def dot(a, b):
    return jnp.dot(a, b, preferred_element_type=f32)


def dot_nt(a, b):
    return lax.dot_general(a, b, NT, preferred_element_type=f32)


def dot_tn(a, b):
    return lax.dot_general(a, b, TN, preferred_element_type=f32)


def gather_quadrants(refs, base, scratch):
    for q, ref in enumerate(refs):
        for t in range(PAIRS):
            scratch[pl.ds(2 * (q * PAIRS + t), 2), :] = ref[base + t].astype(f32)


def scatter_quadrants(scratch, refs, base):
    for q, ref in enumerate(refs):
        for t in range(PAIRS):
            ref[base + t] = scratch[pl.ds(2 * (q * PAIRS + t), 2), :].astype(bf16)


def token_place(t):
    rest = t % (2 * PAIRS)
    return t // (2 * PAIRS), rest // (2 * HN), rest % (2 * HN) // 2, rest % 2


def normalise(x):
    centred = x - jnp.mean(x, axis=-1, keepdims=True)
    variance = jnp.mean(centred * centred, axis=-1, keepdims=True)
    rstd = lax.rsqrt(variance + eps)
    return centred * rstd, rstd


def head_masks(dtype):
    lane = lax.broadcasted_iota(jnp.int32, (1, GROUP * HEAD), 1) // HEAD
    return [(lane == h).astype(dtype) for h in range(GROUP)]


def stack_heads(x):
    return jnp.concatenate([x * m for m in head_masks(x.dtype)], axis=0)


def merge_heads(y):
    masks = head_masks(f32)
    total = y[:SPAN] * masks[0]
    for h in range(1, GROUP):
        total = total + y[h * SPAN : (h + 1) * SPAN] * masks[h]
    return total


def mask_bias(refs, lats):
    token = lax.broadcasted_iota(jnp.int32, (1, WIDE), 1)
    quadrant, r, c, level = token_place(token)
    lane = HN * (1 - quadrant % 2) + c
    hot = lax.broadcasted_iota(jnp.int32, (128, WIDE), 0) == lane
    rows = jnp.concatenate([ref[CLASS_AT + r, :, :128].astype(f32) for ref in refs for r in range(HL)], axis=0)
    spread = dot(rows.astype(bf16), hot.astype(f32).astype(bf16))
    mine = lax.broadcasted_iota(jnp.int32, (4 * HL * LEVELS, WIDE), 0) == (quadrant * HL + r) * LEVELS + level
    seam = jnp.where(lax.axis_index("lat") == lats - 1, (quadrant // 2).astype(f32), 0.0)
    label = 2.0 * jnp.sum(jnp.where(mine, spread, 0.0), axis=0, keepdims=True) + seam
    label = jnp.where(token < SPAN, label, 9.0)
    eye = lax.broadcasted_iota(jnp.int32, (SPAN, WIDE), 0) == lax.broadcasted_iota(jnp.int32, (SPAN, WIDE), 1)
    column = jnp.sum(jnp.where(eye, label, 0.0), axis=1, keepdims=True)
    return jnp.where(column == label, 0.0, BLANK)


def pad_keys(x):
    return jnp.concatenate([x, jnp.zeros((WIDE - SPAN, x.shape[1]), x.dtype)], axis=0)


def block_forward(x, blank, bias_of, gain, offset, weight, bias, out_weight, out_bias, qkv_ref, probs_ref):
    xhat, _ = normalise(x)
    normed = (xhat * gain + offset).astype(bf16)
    queries = (dot(normed, weight[:, :D]) + bias[:, :D]).astype(bf16) * jnp.array(HEAD**-0.5, bf16)
    qkv_ref[:, :D] = queries
    qkv_ref[:, D:] = (dot(normed, weight[:, D:]) + bias[:, D:]).astype(bf16)
    mixed = []
    for g in range(HEADS // GROUP):
        lanes = pl.ds(g * GROUP * HEAD, GROUP * HEAD)
        q4 = stack_heads(qkv_ref[:, pl.ds(g * 256, 256)])
        k4 = pad_keys(qkv_ref[:, pl.ds(D + g * 256, 256)])
        v4 = pad_keys(qkv_ref[:, pl.ds(2 * D + g * 256, 256)])
        scores = dot_nt(q4, k4)
        for h in range(GROUP):
            s = scores[h * SPAN : (h + 1) * SPAN] + bias_of(g * GROUP + h) + blank
            e = jnp.exp(s - jnp.max(s, axis=-1, keepdims=True))
            p = e * (1.0 / jnp.sum(e, axis=-1, keepdims=True))
            probs_ref[pl.ds((g * GROUP + h) * SPAN, SPAN), :] = p.astype(bf16)
        p4 = probs_ref[pl.ds(g * GROUP * SPAN, GROUP * SPAN), :]
        mixed.append(merge_heads(dot(p4, v4)))
    heads_out = jnp.concatenate(mixed, axis=1).astype(bf16)
    return x + dot(heads_out, out_weight) + out_bias


def block_backward(grad, x, gain, weight, out_weight, qkv_ref, probs_ref, dqkv_ref):
    dheads = dot_nt(grad, out_weight).astype(bf16)
    for g in range(HEADS // GROUP):
        q4 = stack_heads(qkv_ref[:, pl.ds(g * 256, 256)])
        k4 = pad_keys(qkv_ref[:, pl.ds(D + g * 256, 256)])
        v4 = pad_keys(qkv_ref[:, pl.ds(2 * D + g * 256, 256)])
        do4 = stack_heads(dheads[:, g * 256 : (g + 1) * 256])
        p4 = probs_ref[pl.ds(g * GROUP * SPAN, GROUP * SPAN), :]
        dprobs = dot_nt(do4, v4)
        pf = p4.astype(f32)
        weighted = pf * dprobs
        ds = (weighted - pf * jnp.sum(weighted, axis=-1, keepdims=True)).astype(bf16)
        dq = merge_heads(dot(ds, k4)) * HEAD**-0.5
        dk = dot_tn(ds[:, :SPAN], q4)
        dv = dot_tn(p4[:, :SPAN], do4)
        dqkv_ref[:, pl.ds(g * 256, 256)] = dq.astype(bf16)
        dqkv_ref[:, pl.ds(D + g * 256, 256)] = dk.astype(bf16)
        dqkv_ref[:, pl.ds(2 * D + g * 256, 256)] = dv.astype(bf16)
    dnormed = dot_nt(dqkv_ref[...], weight).astype(bf16).astype(f32)
    xhat, rstd = normalise(x)
    dxhat = dnormed * gain
    dx = rstd * (
        dxhat
        - jnp.mean(dxhat, axis=-1, keepdims=True)
        - xhat * jnp.mean(dxhat * xhat, axis=-1, keepdims=True)
    )
    return grad.astype(f32) + dx.astype(bf16).astype(f32)


COARSE_ROWS, COARSE_COLS = HL // 2 + 1, HN // 2
POINTS = COARSE_ROWS * COARSE_COLS
COTANGENT_AT = PAIRS
COARSE_AT = 2 * PAIRS
CLASS_AT = 2 * PAIRS + 2 * POINTS


TILES = CLASS_AT + HL


def pack_kernel(
    tokens_hbm, cotangent_hbm, coarse_hbm, classes_hbm, o0, o1, o2, o3,
    tokens, cotangent, coarse, classes, buffers, in_sems, out_sems,
):
    arrivals = [
        pltpu.make_async_copy(src, dst, in_sems.at[n])
        for n, (src, dst) in enumerate(
            ((tokens_hbm, tokens), (cotangent_hbm, cotangent), (coarse_hbm, coarse), (classes_hbm, classes))
        )
    ]
    for copy in arrivals:
        copy.start()
    buffers[:, pl.ds(CLASS_AT, HL)] = jnp.zeros((4, HL, LEVELS, D), bf16)
    for copy in arrivals:
        copy.wait()
    departures = []
    for q in (3, 2, 1, 0):
        qr, qc = divmod(q, 2)
        lat, lon = HL * (1 - qr), HN * (1 - qc)
        low_lat, low_lon = (coarse.shape[0] - COARSE_ROWS) * (1 - qr), COARSE_COLS * (1 - qc)
        for r in range(HL):
            buffers[q, pl.ds(r * HN, HN)] = tokens[lat + r, pl.ds(lon, HN)]
            buffers[q, pl.ds(COTANGENT_AT + r * HN, HN)] = cotangent[lat + r, pl.ds(lon, HN)]
            buffers[q, CLASS_AT + r, :, pl.ds(0, WIN_LON)] = classes[lat + r].astype(f32).astype(bf16)
        for r in range(COARSE_ROWS):
            for half in range(2):
                buffers[q, pl.ds(COARSE_AT + POINTS * half + r * COARSE_COLS, COARSE_COLS)] = coarse[
                    low_lat + r, pl.ds(low_lon, COARSE_COLS), :, pl.ds(D * half, D)
                ]
        copy = pltpu.make_async_copy(buffers.at[q], (o0, o1, o2, o3)[q], out_sems.at[q])
        copy.start()
        departures.append(copy)
    for copy in departures:
        copy.wait()


def lookup_kernel(inputs_ref, out_ref, rest_ref, low, high, packed_low, packed_high, parts):
    token = lax.broadcasted_iota(jnp.int32, (SPAN, 1), 0)
    quadrant, r, c, level = token_place(token)
    old = level * (WIN_LAT * WIN_LON) + (quadrant // 2 * HL + r) * WIN_LON + quadrant % 2 * HN + c
    order = (lax.broadcasted_iota(jnp.int32, (SPAN, SPAN), 1) == old).astype(f32).astype(bf16)
    index = inputs_ref[:SPAN, :SPAN].astype(jnp.int32)
    rest = SPAN - 128

    lane = lax.broadcasted_iota(jnp.int32, (rest, WIDE), 1)
    spread = (lane % rest == lax.broadcasted_iota(jnp.int32, (rest, WIDE), 0)).astype(f32).astype(bf16)
    own = (
        lax.broadcasted_iota(jnp.int32, (SPAN, WIDE), 1) // rest
        == lax.broadcasted_iota(jnp.int32, (SPAN, WIDE), 0) % rest
    )
    for part, full, packed in ((index % WIDE, low, packed_low), (index // WIDE, high, packed_high)):
        moved = dot_nt(dot(order, part.astype(f32).astype(bf16)).astype(bf16), order)
        full[...] = moved[:, :128]
        tail = jnp.where(own, dot(moved[:, 128:].astype(bf16), spread), 0.0)
        for g in range(SPAN // rest):
            packed[pl.ds(g, 1), :] = jnp.sum(tail[rest * g : rest * (g + 1)], axis=0, keepdims=True)

    left = inputs_ref[SPAN:]
    blocks = left.shape[1] // WIDE
    for k in range(3):
        piece = left.astype(bf16)
        left = left - piece.astype(f32)
        for b in range(blocks):
            parts[pl.ds((b * 3 + k) * 2 * HEADS, 2 * HEADS), :] = piece[:, b * WIDE : (b + 1) * WIDE]
    entries = parts[...]
    ids = lax.broadcasted_iota(jnp.int32, (16, WIDE), 0).astype(f32)
    ids = [(ids + 16 * n).astype(bf16) for n in range(WIDE // 16)]
    one, zero = jnp.ones((16, WIDE), bf16), jnp.zeros((16, WIDE), bf16)

    def look(low_row, high_row):
        wanted = jnp.broadcast_to(low_row, (16, WIDE)).astype(bf16)
        hot = jnp.concatenate([jnp.where(wanted == i, one, zero) for i in ids], axis=0)
        found = dot(entries, hot)
        sums = []
        for b in range(blocks):
            at = [found[(b * 3 + k) * 2 * HEADS : (b * 3 + k + 1) * 2 * HEADS] for k in range(3)]
            sums.append(at[0] + at[1] + at[2])
        result = sums[0]
        for b in range(1, blocks):
            result = jnp.where(high_row == b, sums[b], result)
        return result

    def two_rows(i):
        def pair(ref):
            return jnp.concatenate([ref[pl.ds(i, 1), :], ref[pl.ds(i + 1, 1), :]], axis=1)

        result = look(pair(low), pair(high))
        for n in range(2):
            for half in range(2):
                out_ref[pl.ds(half * HEADS * SPAN + i + n, HEADS, stride=SPAN), :] = result[
                    half * HEADS : (half + 1) * HEADS, n * 128 : (n + 1) * 128
                ]

    @pl.loop(0, SPAN // 16)
    def _(step):
        for n in range(8):
            two_rows(16 * step + 2 * n)

    for g in range(SPAN // rest):
        result = look(packed_low[pl.ds(g, 1), :], packed_high[pl.ds(g, 1), :])
        for n in range(rest):
            first = n * rest // 128 * 128
            for half in range(2):
                rest_ref[pl.ds(half * HEADS * SPAN + rest * g + n, HEADS, stride=SPAN), :] = pltpu.roll(
                    result[half * HEADS : (half + 1) * HEADS, first : first + 128], (first - n * rest) % 128, axis=1
                )


def lookup(relative_index, encoder_table, decoder_table):
    blocks = -(-encoder_table.shape[1] // WIDE)

    def widen(rows):
        return jnp.pad(rows, ((0, 0), (0, blocks * WIDE - rows.shape[1])))

    inputs = jnp.concatenate([widen(relative_index.astype(f32)), widen(encoder_table), widen(decoder_table)], axis=0)
    return pl.pallas_call(
        lookup_kernel,
        out_shape=[jax.ShapeDtypeStruct((2 * HEADS * SPAN, 128), f32)] * 2,
        scratch_shapes=[
            pltpu.VMEM((SPAN, 128), f32),
            pltpu.VMEM((SPAN, 128), f32),
            pltpu.VMEM((16, WIDE), f32),
            pltpu.VMEM((16, WIDE), f32),
            pltpu.VMEM((blocks * 3 * 2 * HEADS, WIDE), bf16),
        ],
        compiler_params=pltpu.CompilerParams(vmem_limit_bytes=32 * 2**20),
        cost_estimate=pl.CostEstimate(flops=3_000_000_000, bytes_accessed=4_000_000, transcendentals=0),
        name="lookup",
    )(inputs)


def coarse_points(q):
    qr, qc = divmod(q, 2)
    return [
        (qr * COARSE_ROWS + r) * 2 * COARSE_COLS + qc * COARSE_COLS + c
        for r in range(COARSE_ROWS)
        for c in range(COARSE_COLS)
    ]


def coarse_places():
    places = []
    for q in range(4):
        qr, qc = divmod(q, 2)
        for r in range(HL):
            for c in range(HN):
                row, column = qr * HL + r + HL % 2, qc * HN + c + HN % 2
                at = (row // 2) * 2 * COARSE_COLS + column // 2
                places.append((q * PAIRS + r * HN + c, at, (row % 2) * 2 + column % 2))
    return places


def main_kernel(
    lats, b0, b1, b2, b3, bias_main, bias_rest,
    e_gain, e_offset, e_bias, e_out_bias, d_gain, d_offset, d_bias, d_out_bias, split_bias,
    e_weight, e_out_weight, d_weight, d_out_weight, split,
    o0, o1, o2, o3,
    scratch, coarse, fine, tokens, e_qkv, e_probs, d_qkv, d_probs, dqkv,
):
    def bias_rows(h):
        rows = pl.ds(h * SPAN, SPAN)
        return jnp.concatenate([bias_main[rows, :], bias_rest[rows, :]], axis=1)

    parts = (b0, b1, b2, b3)
    gather_quadrants(parts, 0, scratch)
    x = scratch[...]
    tokens[...] = x.astype(bf16)
    blank = mask_bias(parts, lats)
    encoded = block_forward(
        x, blank, lambda h: bias_rows(h), e_gain[...], e_offset[...], e_weight,
        e_bias[...].reshape(1, -1), e_out_weight[...], e_out_bias[...], e_qkv, e_probs,
    ).astype(bf16)

    for q, ref in enumerate(parts):
        for n, at in enumerate(coarse_points(q)):
            for half in range(2):
                coarse[pl.ds(2 * at, 2), pl.ds(D * half, D)] = ref[COARSE_AT + POINTS * half + n].astype(f32)
    lowres = coarse[...].astype(bf16)
    fine[...] = dot(lowres, split[...]) + split_bias[...]
    for t, at, kind in coarse_places():
        scratch[pl.ds(2 * t, 2), :] = fine[pl.ds(2 * at, 2), pl.ds(kind * D, D)]
    x = (encoded.astype(f32) + scratch[...]).astype(bf16).astype(f32)
    decoded = block_forward(
        x, blank, lambda h: bias_rows(HEADS + h), d_gain[...], d_offset[...], d_weight,
        d_bias[...].reshape(1, -1), d_out_weight[...], d_out_bias[...], d_qkv, d_probs,
    )
    outs = (o0, o1, o2, o3)
    scratch[...] = decoded
    scatter_quadrants(scratch, outs, 0)
    gather_quadrants(parts, COTANGENT_AT, scratch)
    grad = scratch[...].astype(bf16)
    dx = block_backward(grad, x, d_gain[...], d_weight[...], d_out_weight[...], d_qkv, d_probs, dqkv)
    grad = dx.astype(bf16)

    scratch[...] = dx
    fine[...] = jnp.zeros_like(fine)
    for t, at, kind in coarse_places():
        fine[pl.ds(2 * at, 2), pl.ds(kind * D, D)] = scratch[pl.ds(2 * t, 2), :]
    coarse[...] = dot_nt(fine[...].astype(bf16), split[...])
    for q, ref in enumerate(outs):
        for n, at in enumerate(coarse_points(q)):
            for half in range(2):
                ref[COARSE_AT + POINTS * half + n] = coarse[pl.ds(2 * at, 2), pl.ds(D * half, D)].astype(bf16)

    scratch[...] = block_backward(
        grad, tokens[...].astype(f32), e_gain[...], e_weight[...], e_out_weight[...], e_qkv, e_probs, dqkv
    )
    scatter_quadrants(scratch, outs, PAIRS)


def home_kernel(h0, h1, h2, h3, decoded, tokens_gradient, coarse_gradient, sems):
    copies = []
    for q, ref in enumerate((h0, h1, h2, h3)):
        for n, out in enumerate((decoded, tokens_gradient)):
            for r in range(HL):
                copy = pltpu.make_async_copy(
                    ref.at[pl.ds(PAIRS * n + r * HN, HN)],
                    out.at[q // 2 * HL + r, pl.ds(q % 2 * HN, HN)],
                    sems.at[len(copies)],
                )
                copy.start()
                copies.append(copy)
    for qc, (upper, lower) in enumerate(((h0, h2), (h1, h3))):
        for half in range(2):
            for c in range(COARSE_COLS):
                at = COARSE_AT + POINTS * half + c
                lanes = pl.ds(D * half, D)
                column = qc * COARSE_COLS + c
                coarse_gradient[0, column, :, lanes] = upper[at]
                both = upper[at + COARSE_COLS].astype(f32) + lower[at].astype(f32)
                coarse_gradient[1, column, :, lanes] = both.astype(bf16)
                coarse_gradient[2, column, :, lanes] = lower[at + COARSE_COLS]
    for copy in copies:
        copy.wait()


VM = pl.BlockSpec(memory_space=pltpu.VMEM)


ANY = pl.BlockSpec(memory_space=pl.ANY)


def call(kernel, name, inputs, outs, scratch, flops, in_specs=None, out_specs=None, vmem=32):
    return pl.pallas_call(
        kernel,
        out_shape=outs,
        in_specs=in_specs or [VM] * len(inputs),
        out_specs=out_specs or [VM] * len(outs),
        scratch_shapes=scratch,
        compiler_params=pltpu.CompilerParams(vmem_limit_bytes=vmem * 2**20),
        cost_estimate=pl.CostEstimate(flops=flops, bytes_accessed=flops // 1000, transcendentals=0),
        name=name,
    )(*inputs)


def shift_pairs(lat, lon, lats, lons):
    return [
        (i * lons + j, ((i + lat) % lats) * lons + (j + lon) % lons) for i in range(lats) for j in range(lons)
    ]


def exchange(pieces, steps, lats, lons):
    out = [pieces[0]]
    for q in range(1, 4):
        qr, qc = divmod(q, 2)
        out.append(lax.ppermute(pieces[q], ("lat", "lon"), shift_pairs(qr * steps, qc * steps, lats, lons)))
    return out


def per_device(
    lats, lons,
    tokens, coarse, output_cotangent, token_class, relative_index,
    encoder_gain, encoder_offset, encoder_projection, encoder_projection_bias,
    encoder_output_weight, encoder_output_bias, encoder_table,
    decoder_gain, decoder_offset, decoder_projection, decoder_projection_bias,
    decoder_output_weight, decoder_output_bias, decoder_table,
    split_weight, split_bias,
):
    def row(v):
        return v.reshape(1, -1)

    s = jax.ShapeDtypeStruct
    packed = call(
        pack_kernel,
        "pack",
        [
            jnp.transpose(tokens, (1, 2, 0, 3)),
            jnp.transpose(output_cotangent, (1, 2, 0, 3)),
            jnp.transpose(coarse, (1, 2, 0, 3)),
            jnp.transpose(token_class, (1, 0, 2)),
        ],
        [s((TILES, LEVELS, D), bf16)] * 4,
        [
            pltpu.VMEM((WIN_LAT, WIN_LON, LEVELS, D), bf16),
            pltpu.VMEM((WIN_LAT, WIN_LON, LEVELS, D), bf16),
            pltpu.VMEM((WIN_LAT // 2, WIN_LON // 2, LEVELS, 2 * D), bf16),
            pltpu.VMEM((WIN_LAT, LEVELS, WIN_LON), jnp.int32),
            pltpu.VMEM((4, TILES, LEVELS, D), bf16),
            pltpu.SemaphoreType.DMA((4,)),
            pltpu.SemaphoreType.DMA((4,)),
        ],
        100_000_000,
        [ANY] * 4,
        [ANY] * 4,
        60,
    )
    parts = exchange(packed, -1, lats, lons)
    biases = lookup(relative_index, encoder_table, decoder_table)
    points = 4 * LEVELS * POINTS
    outs = call(
        functools.partial(main_kernel, lats),
        "main",
        [
            *parts, *biases,
            row(encoder_gain), row(encoder_offset), encoder_projection_bias, row(encoder_output_bias),
            row(decoder_gain), row(decoder_offset), decoder_projection_bias, row(decoder_output_bias),
            row(split_bias),
            encoder_projection, encoder_output_weight, decoder_projection, decoder_output_weight, split_weight,
        ],
        [s((CLASS_AT, LEVELS, D), bf16)] * 4,
        [
            pltpu.VMEM((SPAN, D), f32),
            pltpu.VMEM((points, 2 * D), f32),
            pltpu.VMEM((points, 4 * D), f32),
            pltpu.VMEM((SPAN, D), bf16),
            pltpu.VMEM((SPAN, 3 * D), bf16),
            pltpu.VMEM((HEADS * SPAN, WIDE), bf16),
            pltpu.VMEM((SPAN, 3 * D), bf16),
            pltpu.VMEM((HEADS * SPAN, WIDE), bf16),
            pltpu.VMEM((SPAN, 3 * D), bf16),
        ],
        8_000_000_000,
    )
    home = exchange(outs, 1, lats, lons)
    grid = s((WIN_LAT, WIN_LON, LEVELS, D), bf16)
    low = s((WIN_LAT // 2, WIN_LON // 2, LEVELS, 2 * D), bf16)
    results = call(
        home_kernel,
        "home",
        [home[3 - q] for q in range(4)],
        [grid, grid, low],
        [pltpu.SemaphoreType.DMA((4 * 2 * HL,))],
        1_000_000,
        None,
        [ANY, ANY, VM],
    )
    return tuple(jnp.transpose(r, (2, 0, 1, 3)) for r in results)


def solution(mesh):
    cut = P(None, "lat", "lon", None)
    in_specs = (cut, cut, cut, P(None, "lat", "lon")) + (P(),) * 17
    return jax.shard_map(
        functools.partial(per_device, mesh.shape["lat"], mesh.shape["lon"]),
        mesh=mesh,
        in_specs=in_specs,
        out_specs=(cut, cut, cut),
        check_vma=False,
    )
```

```python
import functools

import jax
import jax.numpy as jnp
from jax import lax
from jax.experimental import pallas as pl
from jax.experimental.pallas import tpu as pltpu
from jax.sharding import PartitionSpec as P

HEADS = 8
LEVELS = 2
WIN_LAT = 6
WIN_LON = 12
SPAN = LEVELS * WIN_LAT * WIN_LON
D = 512
HEAD = D // HEADS
WIDE = 256
HL, HN = WIN_LAT // 2, WIN_LON // 2
PAIRS = HL * HN
GROUP = 4
BLANK = -1e30
eps = 1e-05

f32, bf16 = jnp.float32, jnp.bfloat16
NT = (((1,), (1,)), ((), ()))
TN = (((0,), (0,)), ((), ()))


def dot(a, b):
    return jnp.dot(a, b, preferred_element_type=f32)


def dot_nt(a, b):
    return lax.dot_general(a, b, NT, preferred_element_type=f32)


def dot_tn(a, b):
    return lax.dot_general(a, b, TN, preferred_element_type=f32)


def column_parity():
    return lax.axis_index("lon") % 2


def swapped(m, parity):
    return m + parity * (1 - 2 * m)


def gather_quadrants(refs, base, scratch, parity):
    for q, ref in enumerate(refs):
        m, qc = divmod(q, 2)
        half = swapped(m, parity)
        for t in range(PAIRS):
            scratch[half, pl.ds(2 * (qc * PAIRS + t), 2), :] = ref[base + t].astype(f32)


def scatter_quadrants(scratch, refs, base, parity):
    for q, ref in enumerate(refs):
        m, qc = divmod(q, 2)
        half = swapped(m, parity)
        for t in range(PAIRS):
            ref[base + t] = scratch[half, pl.ds(2 * (qc * PAIRS + t), 2), :].astype(bf16)


def whole(scratch):
    return scratch[...].reshape(-1, scratch.shape[-1])


def fill(scratch, value):
    scratch[...] = value.reshape(scratch.shape)


def token_place(t):
    rest = t % (2 * PAIRS)
    return t // (2 * PAIRS), rest // (2 * HN), rest % (2 * HN) // 2, rest % 2


def normalise(x):
    centred = x - jnp.mean(x, axis=-1, keepdims=True)
    variance = jnp.mean(centred * centred, axis=-1, keepdims=True)
    rstd = lax.rsqrt(variance + eps)
    return centred * rstd, rstd


def head_masks(dtype):
    lane = lax.broadcasted_iota(jnp.int32, (1, GROUP * HEAD), 1) // HEAD
    return [(lane == h).astype(dtype) for h in range(GROUP)]


def stack_heads(x):
    return jnp.concatenate([x * m for m in head_masks(x.dtype)], axis=0)


def merge_heads(y):
    masks = head_masks(f32)
    total = y[:SPAN] * masks[0]
    for h in range(1, GROUP):
        total = total + y[h * SPAN : (h + 1) * SPAN] * masks[h]
    return total


def mask_bias(refs, lats, parity):
    token = lax.broadcasted_iota(jnp.int32, (1, WIDE), 1)
    quadrant, r, c, level = token_place(token)
    lane = HN * (1 - quadrant % 2) + c
    hot = lax.broadcasted_iota(jnp.int32, (128, WIDE), 0) == lane
    rows = jnp.concatenate([ref[CLASS_AT + r, :, :128].astype(f32) for ref in refs for r in range(HL)], axis=0)
    spread = dot(rows.astype(bf16), hot.astype(f32).astype(bf16))
    piece = swapped(quadrant // 2, parity) * 2 + quadrant % 2
    mine = lax.broadcasted_iota(jnp.int32, (4 * HL * LEVELS, WIDE), 0) == (piece * HL + r) * LEVELS + level
    last = lax.axis_index("lat") == jnp.where(parity == 0, lats - 1, 0)
    seam = jnp.where(last, (quadrant // 2).astype(f32), 0.0)
    label = 2.0 * jnp.sum(jnp.where(mine, spread, 0.0), axis=0, keepdims=True) + seam
    label = jnp.where(token < SPAN, label, 9.0)
    eye = lax.broadcasted_iota(jnp.int32, (SPAN, WIDE), 0) == lax.broadcasted_iota(jnp.int32, (SPAN, WIDE), 1)
    column = jnp.sum(jnp.where(eye, label, 0.0), axis=1, keepdims=True)
    return jnp.where(column == label, 0.0, BLANK)


def pad_keys(x):
    return jnp.concatenate([x, jnp.zeros((WIDE - SPAN, x.shape[1]), x.dtype)], axis=0)


def block_forward(x, blank, bias_of, gain, offset, weight, bias, out_weight, out_bias, qkv_ref, probs_ref):
    xhat, _ = normalise(x)
    normed = (xhat * gain + offset).astype(bf16)
    queries = (dot(normed, weight[:, :D]) + bias[:, :D]).astype(bf16) * jnp.array(HEAD**-0.5, bf16)
    qkv_ref[:, :D] = queries
    qkv_ref[:, D:] = (dot(normed, weight[:, D:]) + bias[:, D:]).astype(bf16)
    mixed = []
    for g in range(HEADS // GROUP):
        lanes = pl.ds(g * GROUP * HEAD, GROUP * HEAD)
        q4 = stack_heads(qkv_ref[:, pl.ds(g * 256, 256)])
        k4 = pad_keys(qkv_ref[:, pl.ds(D + g * 256, 256)])
        v4 = pad_keys(qkv_ref[:, pl.ds(2 * D + g * 256, 256)])
        scores = dot_nt(q4, k4)
        for h in range(GROUP):
            s = scores[h * SPAN : (h + 1) * SPAN] + bias_of(g * GROUP + h) + blank
            e = jnp.exp(s - jnp.max(s, axis=-1, keepdims=True))
            p = e * (1.0 / jnp.sum(e, axis=-1, keepdims=True))
            probs_ref[pl.ds((g * GROUP + h) * SPAN, SPAN), :] = p.astype(bf16)
        p4 = probs_ref[pl.ds(g * GROUP * SPAN, GROUP * SPAN), :]
        mixed.append(merge_heads(dot(p4, v4)))
    heads_out = jnp.concatenate(mixed, axis=1).astype(bf16)
    return x + dot(heads_out, out_weight) + out_bias


def block_backward(grad, x, gain, weight, out_weight, qkv_ref, probs_ref, dqkv_ref):
    dheads = dot_nt(grad, out_weight).astype(bf16)
    for g in range(HEADS // GROUP):
        q4 = stack_heads(qkv_ref[:, pl.ds(g * 256, 256)])
        k4 = pad_keys(qkv_ref[:, pl.ds(D + g * 256, 256)])
        v4 = pad_keys(qkv_ref[:, pl.ds(2 * D + g * 256, 256)])
        do4 = stack_heads(dheads[:, g * 256 : (g + 1) * 256])
        p4 = probs_ref[pl.ds(g * GROUP * SPAN, GROUP * SPAN), :]
        dprobs = dot_nt(do4, v4)
        pf = p4.astype(f32)
        weighted = pf * dprobs
        ds = (weighted - pf * jnp.sum(weighted, axis=-1, keepdims=True)).astype(bf16)
        dq = merge_heads(dot(ds, k4)) * HEAD**-0.5
        dk = dot_tn(ds[:, :SPAN], q4)
        dv = dot_tn(p4[:, :SPAN], do4)
        dqkv_ref[:, pl.ds(g * 256, 256)] = dq.astype(bf16)
        dqkv_ref[:, pl.ds(D + g * 256, 256)] = dk.astype(bf16)
        dqkv_ref[:, pl.ds(2 * D + g * 256, 256)] = dv.astype(bf16)
    dnormed = dot_nt(dqkv_ref[...], weight).astype(bf16).astype(f32)
    xhat, rstd = normalise(x)
    dxhat = dnormed * gain
    dx = rstd * (
        dxhat
        - jnp.mean(dxhat, axis=-1, keepdims=True)
        - xhat * jnp.mean(dxhat * xhat, axis=-1, keepdims=True)
    )
    return grad.astype(f32) + dx.astype(bf16).astype(f32)


COARSE_ROWS, COARSE_COLS = HL // 2 + 1, HN // 2
POINTS = COARSE_ROWS * COARSE_COLS
COTANGENT_AT = PAIRS
COARSE_AT = 2 * PAIRS
CLASS_AT = 2 * PAIRS + 2 * POINTS


TILES = CLASS_AT + HL


def pack_kernel(
    tokens_hbm, cotangent_hbm, coarse_hbm, classes_hbm, o0, o1, o2, o3,
    tokens, cotangent, coarse, classes, buffers, in_sems, out_sems,
):
    arrivals = [
        pltpu.make_async_copy(src, dst, in_sems.at[n])
        for n, (src, dst) in enumerate(
            ((tokens_hbm, tokens), (cotangent_hbm, cotangent), (coarse_hbm, coarse), (classes_hbm, classes))
        )
    ]
    for copy in arrivals:
        copy.start()
    buffers[:, pl.ds(CLASS_AT, HL)] = jnp.zeros((4, HL, LEVELS, D), bf16)
    for copy in arrivals:
        copy.wait()
    departures = []
    parity = column_parity()
    for q in (3, 2, 1, 0):
        m, qc = divmod(q, 2)
        later = swapped(swapped(1 - m, qc), parity)
        lat, lon = HL * later, HN * (1 - qc)
        low_lat, low_lon = (coarse.shape[0] - COARSE_ROWS) * later, COARSE_COLS * (1 - qc)
        for r in range(HL):
            buffers[q, pl.ds(r * HN, HN)] = tokens[lat + r, pl.ds(lon, HN)]
            buffers[q, pl.ds(COTANGENT_AT + r * HN, HN)] = cotangent[lat + r, pl.ds(lon, HN)]
            buffers[q, CLASS_AT + r, :, pl.ds(0, WIN_LON)] = classes[lat + r].astype(f32).astype(bf16)
        for r in range(COARSE_ROWS):
            for half in range(2):
                buffers[q, pl.ds(COARSE_AT + POINTS * half + r * COARSE_COLS, COARSE_COLS)] = coarse[
                    low_lat + r, pl.ds(low_lon, COARSE_COLS), :, pl.ds(D * half, D)
                ]
        copy = pltpu.make_async_copy(buffers.at[q], (o0, o1, o2, o3)[q], out_sems.at[q])
        copy.start()
        departures.append(copy)
    for copy in departures:
        copy.wait()


def lookup_kernel(inputs_ref, out_ref, rest_ref, low, high, packed_low, packed_high, parts):
    token = lax.broadcasted_iota(jnp.int32, (SPAN, 1), 0)
    quadrant, r, c, level = token_place(token)
    old = level * (WIN_LAT * WIN_LON) + (quadrant // 2 * HL + r) * WIN_LON + quadrant % 2 * HN + c
    order = (lax.broadcasted_iota(jnp.int32, (SPAN, SPAN), 1) == old).astype(f32).astype(bf16)
    index = inputs_ref[:SPAN, :SPAN].astype(jnp.int32)
    rest = SPAN - 128

    lane = lax.broadcasted_iota(jnp.int32, (rest, WIDE), 1)
    spread = (lane % rest == lax.broadcasted_iota(jnp.int32, (rest, WIDE), 0)).astype(f32).astype(bf16)
    own = (
        lax.broadcasted_iota(jnp.int32, (SPAN, WIDE), 1) // rest
        == lax.broadcasted_iota(jnp.int32, (SPAN, WIDE), 0) % rest
    )
    for part, full, packed in ((index % WIDE, low, packed_low), (index // WIDE, high, packed_high)):
        moved = dot_nt(dot(order, part.astype(f32).astype(bf16)).astype(bf16), order)
        full[...] = moved[:, :128]
        tail = jnp.where(own, dot(moved[:, 128:].astype(bf16), spread), 0.0)
        for g in range(SPAN // rest):
            packed[pl.ds(g, 1), :] = jnp.sum(tail[rest * g : rest * (g + 1)], axis=0, keepdims=True)

    left = inputs_ref[SPAN:]
    blocks = left.shape[1] // WIDE
    for k in range(3):
        piece = left.astype(bf16)
        left = left - piece.astype(f32)
        for b in range(blocks):
            parts[pl.ds((b * 3 + k) * 2 * HEADS, 2 * HEADS), :] = piece[:, b * WIDE : (b + 1) * WIDE]
    entries = parts[...]
    ids = lax.broadcasted_iota(jnp.int32, (16, WIDE), 0).astype(f32)
    ids = [(ids + 16 * n).astype(bf16) for n in range(WIDE // 16)]
    one, zero = jnp.ones((16, WIDE), bf16), jnp.zeros((16, WIDE), bf16)

    def look(low_row, high_row):
        wanted = jnp.broadcast_to(low_row, (16, WIDE)).astype(bf16)
        hot = jnp.concatenate([jnp.where(wanted == i, one, zero) for i in ids], axis=0)
        found = dot(entries, hot)
        sums = []
        for b in range(blocks):
            at = [found[(b * 3 + k) * 2 * HEADS : (b * 3 + k + 1) * 2 * HEADS] for k in range(3)]
            sums.append(at[0] + at[1] + at[2])
        result = sums[0]
        for b in range(1, blocks):
            result = jnp.where(high_row == b, sums[b], result)
        return result

    def two_rows(i):
        def pair(ref):
            return jnp.concatenate([ref[pl.ds(i, 1), :], ref[pl.ds(i + 1, 1), :]], axis=1)

        result = look(pair(low), pair(high))
        for n in range(2):
            for half in range(2):
                out_ref[pl.ds(half * HEADS * SPAN + i + n, HEADS, stride=SPAN), :] = result[
                    half * HEADS : (half + 1) * HEADS, n * 128 : (n + 1) * 128
                ]

    @pl.loop(0, SPAN // 48)
    def _(step):
        for n in range(24):
            two_rows(48 * step + 2 * n)

    for g in range(SPAN // rest):
        result = look(packed_low[pl.ds(g, 1), :], packed_high[pl.ds(g, 1), :])
        for n in range(rest):
            first = n * rest // 128 * 128
            for half in range(2):
                rest_ref[pl.ds(half * HEADS * SPAN + rest * g + n, HEADS, stride=SPAN), :] = pltpu.roll(
                    result[half * HEADS : (half + 1) * HEADS, first : first + 128], (first - n * rest) % 128, axis=1
                )


def lookup(relative_index, encoder_table, decoder_table):
    blocks = -(-encoder_table.shape[1] // WIDE)

    def widen(rows):
        return jnp.pad(rows, ((0, 0), (0, blocks * WIDE - rows.shape[1])))

    inputs = jnp.concatenate([widen(relative_index.astype(f32)), widen(encoder_table), widen(decoder_table)], axis=0)
    return pl.pallas_call(
        lookup_kernel,
        out_shape=[jax.ShapeDtypeStruct((2 * HEADS * SPAN, 128), f32)] * 2,
        scratch_shapes=[
            pltpu.VMEM((SPAN, 128), f32),
            pltpu.VMEM((SPAN, 128), f32),
            pltpu.VMEM((16, WIDE), f32),
            pltpu.VMEM((16, WIDE), f32),
            pltpu.VMEM((blocks * 3 * 2 * HEADS, WIDE), bf16),
        ],
        compiler_params=pltpu.CompilerParams(vmem_limit_bytes=32 * 2**20),
        cost_estimate=pl.CostEstimate(flops=3_000_000_000, bytes_accessed=4_000_000, transcendentals=0),
        name="lookup",
    )(inputs)


def coarse_points(qc):
    return [r * 2 * COARSE_COLS + qc * COARSE_COLS + c for r in range(COARSE_ROWS) for c in range(COARSE_COLS)]


def coarse_places():
    places = []
    for q in range(4):
        qr, qc = divmod(q, 2)
        for r in range(HL):
            for c in range(HN):
                row, column = qr * HL + r + HL % 2, qc * HN + c + HN % 2
                at = (row // 2) * 2 * COARSE_COLS + column // 2
                places.append((q * PAIRS + r * HN + c, at, (row % 2) * 2 + column % 2))
    return places


def main_kernel(
    lats, b0, b1, b2, b3, bias_main, bias_rest,
    e_gain, e_offset, e_bias, e_out_bias, d_gain, d_offset, d_bias, d_out_bias, split_bias,
    e_weight, e_out_weight, d_weight, d_out_weight, split,
    o0, o1, o2, o3,
    scratch, coarse, fine, tokens, e_qkv, e_probs, d_qkv, d_probs, dqkv,
):
    def bias_rows(h):
        rows = pl.ds(h * SPAN, SPAN)
        return jnp.concatenate([bias_main[rows, :], bias_rest[rows, :]], axis=1)

    parity = column_parity()
    parts = (b0, b1, b2, b3)
    gather_quadrants(parts, 0, scratch, parity)
    x = whole(scratch)
    tokens[...] = x.astype(bf16)
    blank = mask_bias(parts, lats, parity)
    encoded = block_forward(
        x, blank, lambda h: bias_rows(h), e_gain[...], e_offset[...], e_weight,
        e_bias[...].reshape(1, -1), e_out_weight[...], e_out_bias[...], e_qkv, e_probs,
    ).astype(bf16)

    for q, ref in enumerate(parts):
        part = swapped(q // 2, parity)
        for n, at in enumerate(coarse_points(q % 2)):
            for half in range(2):
                coarse[part, pl.ds(2 * at, 2), pl.ds(D * half, D)] = ref[COARSE_AT + POINTS * half + n].astype(f32)
    lowres = whole(coarse).astype(bf16)
    fine[...] = dot(lowres, split[...]) + split_bias[...]
    for t, at, kind in coarse_places():
        scratch[t // (2 * PAIRS), pl.ds(2 * (t % (2 * PAIRS)), 2), :] = fine[pl.ds(2 * at, 2), pl.ds(kind * D, D)]
    x = (encoded.astype(f32) + whole(scratch)).astype(bf16).astype(f32)
    decoded = block_forward(
        x, blank, lambda h: bias_rows(HEADS + h), d_gain[...], d_offset[...], d_weight,
        d_bias[...].reshape(1, -1), d_out_weight[...], d_out_bias[...], d_qkv, d_probs,
    )
    outs = (o0, o1, o2, o3)
    fill(scratch, decoded)
    scatter_quadrants(scratch, outs, 0, parity)
    gather_quadrants(parts, COTANGENT_AT, scratch, parity)
    grad = whole(scratch).astype(bf16)
    dx = block_backward(grad, x, d_gain[...], d_weight[...], d_out_weight[...], d_qkv, d_probs, dqkv)
    grad = dx.astype(bf16)

    fill(scratch, dx)
    fine[...] = jnp.zeros_like(fine)
    for t, at, kind in coarse_places():
        fine[pl.ds(2 * at, 2), pl.ds(kind * D, D)] = scratch[t // (2 * PAIRS), pl.ds(2 * (t % (2 * PAIRS)), 2), :]
    fill(coarse, dot_nt(fine[...].astype(bf16), split[...]))
    for q, ref in enumerate(outs):
        part = swapped(q // 2, parity)
        for n, at in enumerate(coarse_points(q % 2)):
            for half in range(2):
                ref[COARSE_AT + POINTS * half + n] = coarse[part, pl.ds(2 * at, 2), pl.ds(D * half, D)].astype(bf16)

    dx = block_backward(
        grad, tokens[...].astype(f32), e_gain[...], e_weight[...], e_out_weight[...], e_qkv, e_probs, dqkv
    )
    fill(scratch, dx)
    scatter_quadrants(scratch, outs, PAIRS, parity)


def home_kernel(h0, h1, h2, h3, decoded, tokens_gradient, coarse_gradient, sems):
    parity = column_parity()
    refs = (h0, h1, h2, h3)
    copies = []
    for q, ref in enumerate(refs):
        m, qc = divmod(q, 2)
        later = swapped(swapped(1 - m, qc), parity)
        for n, out in enumerate((decoded, tokens_gradient)):
            for r in range(HL):
                copy = pltpu.make_async_copy(
                    ref.at[pl.ds(PAIRS * n + r * HN, HN)],
                    out.at[HL * later + r, pl.ds(HN * (1 - qc), HN)],
                    sems.at[len(copies)],
                )
                copy.start()
                copies.append(copy)
    for qc in range(2):
        begins = swapped(qc, parity) == 0
        own, other = refs[qc], refs[2 + qc]
        for half in range(2):
            for c in range(COARSE_COLS):
                at = COARSE_AT + POINTS * half + c
                a0, a1, b0, b1 = (r[at + k].astype(f32) for r in (own, other) for k in (0, COARSE_COLS))
                rows = (jnp.where(begins, b0, a0), jnp.where(begins, b1 + a0, a1 + b0), jnp.where(begins, a1, b1))
                for n, row in enumerate(rows):
                    coarse_gradient[n, (1 - qc) * COARSE_COLS + c, :, pl.ds(D * half, D)] = row.astype(bf16)
    for copy in copies:
        copy.wait()


VM = pl.BlockSpec(memory_space=pltpu.VMEM)


ANY = pl.BlockSpec(memory_space=pl.ANY)


def call(kernel, name, inputs, outs, scratch, flops, in_specs=None, out_specs=None, vmem=32):
    return pl.pallas_call(
        kernel,
        out_shape=outs,
        in_specs=in_specs or [VM] * len(inputs),
        out_specs=out_specs or [VM] * len(outs),
        scratch_shapes=scratch,
        compiler_params=pltpu.CompilerParams(vmem_limit_bytes=vmem * 2**20),
        cost_estimate=pl.CostEstimate(flops=flops, bytes_accessed=flops // 1000, transcendentals=0),
        name=name,
    )(*inputs)


def exchange(pieces, lats, lons, back):
    out = [pieces[0]]
    for q in range(1, 4):
        m, qc = divmod(q, 2)
        pairs = []
        for i in range(lats):
            for j in range(lons):
                to = (j - qc) % lons
                step = m * (1 if to % 2 else -1)
                pairs.append((i * lons + j, (i + step) % lats * lons + to))
        if back:
            pairs = [(target, source) for source, target in pairs]
        out.append(lax.ppermute(pieces[q], ("lat", "lon"), pairs))
    return out


def per_device(
    lats, lons,
    tokens, coarse, output_cotangent, token_class, relative_index,
    encoder_gain, encoder_offset, encoder_projection, encoder_projection_bias,
    encoder_output_weight, encoder_output_bias, encoder_table,
    decoder_gain, decoder_offset, decoder_projection, decoder_projection_bias,
    decoder_output_weight, decoder_output_bias, decoder_table,
    split_weight, split_bias,
):
    def row(v):
        return v.reshape(1, -1)

    s = jax.ShapeDtypeStruct
    packed = call(
        pack_kernel,
        "pack",
        [
            jnp.transpose(tokens, (1, 2, 0, 3)),
            jnp.transpose(output_cotangent, (1, 2, 0, 3)),
            jnp.transpose(coarse, (1, 2, 0, 3)),
            jnp.transpose(token_class, (1, 0, 2)),
        ],
        [s((TILES, LEVELS, D), bf16)] * 4,
        [
            pltpu.VMEM((WIN_LAT, WIN_LON, LEVELS, D), bf16),
            pltpu.VMEM((WIN_LAT, WIN_LON, LEVELS, D), bf16),
            pltpu.VMEM((WIN_LAT // 2, WIN_LON // 2, LEVELS, 2 * D), bf16),
            pltpu.VMEM((WIN_LAT, LEVELS, WIN_LON), jnp.int32),
            pltpu.VMEM((4, TILES, LEVELS, D), bf16),
            pltpu.SemaphoreType.DMA((4,)),
            pltpu.SemaphoreType.DMA((4,)),
        ],
        100_000_000,
        [ANY] * 4,
        [ANY] * 4,
        60,
    )
    parts = exchange(packed, lats, lons, False)
    biases = lookup(relative_index, encoder_table, decoder_table)
    points = 4 * LEVELS * POINTS
    outs = call(
        functools.partial(main_kernel, lats),
        "main",
        [
            *parts, *biases,
            row(encoder_gain), row(encoder_offset), encoder_projection_bias, row(encoder_output_bias),
            row(decoder_gain), row(decoder_offset), decoder_projection_bias, row(decoder_output_bias),
            row(split_bias),
            encoder_projection, encoder_output_weight, decoder_projection, decoder_output_weight, split_weight,
        ],
        [s((CLASS_AT, LEVELS, D), bf16)] * 4,
        [
            pltpu.VMEM((2, SPAN // 2, D), f32),
            pltpu.VMEM((2, points // 2, 2 * D), f32),
            pltpu.VMEM((points, 4 * D), f32),
            pltpu.VMEM((SPAN, D), bf16),
            pltpu.VMEM((SPAN, 3 * D), bf16),
            pltpu.VMEM((HEADS * SPAN, WIDE), bf16),
            pltpu.VMEM((SPAN, 3 * D), bf16),
            pltpu.VMEM((HEADS * SPAN, WIDE), bf16),
            pltpu.VMEM((SPAN, 3 * D), bf16),
        ],
        8_000_000_000,
    )
    home = exchange(outs, lats, lons, True)
    grid = s((WIN_LAT, WIN_LON, LEVELS, D), bf16)
    low = s((WIN_LAT // 2, WIN_LON // 2, LEVELS, 2 * D), bf16)
    results = call(
        home_kernel,
        "home",
        home,
        [grid, grid, low],
        [pltpu.SemaphoreType.DMA((4 * 2 * HL,))],
        1_000_000,
        None,
        [ANY, ANY, VM],
    )
    return tuple(jnp.transpose(r, (2, 0, 1, 3)) for r in results)


def solution(mesh):
    cut = P(None, "lat", "lon", None)
    in_specs = (cut, cut, cut, P(None, "lat", "lon")) + (P(),) * 17
    return jax.shard_map(
        functools.partial(per_device, mesh.shape["lat"], mesh.shape["lon"]),
        mesh=mesh,
        in_specs=in_specs,
        out_specs=(cut, cut, cut),
        check_vma=False,
    )
```

```python
import functools

import jax
import jax.numpy as jnp
from jax import lax
from jax.experimental import pallas as pl
from jax.experimental.pallas import tpu as pltpu
from jax.sharding import PartitionSpec as P

HEADS = 8
LEVELS = 2
WIN_LAT = 6
WIN_LON = 12
SPAN = LEVELS * WIN_LAT * WIN_LON
D = 512
HEAD = D // HEADS
WIDE = 256
HL, HN = WIN_LAT // 2, WIN_LON // 2
PAIRS = HL * HN
GROUP = 4
BLANK = -1e30
eps = 1e-05

f32, bf16 = jnp.float32, jnp.bfloat16
NT = (((1,), (1,)), ((), ()))
TN = (((0,), (0,)), ((), ()))


def dot(a, b):
    return jnp.dot(a, b, preferred_element_type=f32)


def dot_nt(a, b):
    return lax.dot_general(a, b, NT, preferred_element_type=f32)


def dot_tn(a, b):
    return lax.dot_general(a, b, TN, preferred_element_type=f32)


def column_parity():
    return lax.axis_index("lon") % 2


def swapped(m, parity):
    return m + parity * (1 - 2 * m)


def turned(window_row, lats):
    return (window_row % lats + lats) % lats // (lats // 2)


def own_turned(lats):
    return turned(lax.axis_index("lat") - column_parity(), lats)


def piece_cut(m, n, lats):
    target = swapped(n, column_parity())
    window_row = lax.axis_index("lat") - (1 - target if m else target)
    return swapped(1 - m, target), swapped(1 - n, turned(window_row, lats))


def gather_quadrants(refs, base, scratch, parity):
    for q, ref in enumerate(refs):
        m, qc = divmod(q, 2)
        half = swapped(m, parity)
        for t in range(PAIRS):
            scratch[half, pl.ds(2 * (qc * PAIRS + t), 2), :] = ref[base + t].astype(f32)


def scatter_quadrants(scratch, refs, base, parity):
    for q, ref in enumerate(refs):
        m, qc = divmod(q, 2)
        half = swapped(m, parity)
        for t in range(PAIRS):
            ref[base + t] = scratch[half, pl.ds(2 * (qc * PAIRS + t), 2), :].astype(bf16)


def whole(scratch):
    return scratch[...].reshape(-1, scratch.shape[-1])


def fill(scratch, value):
    scratch[...] = value.reshape(scratch.shape)


def token_place(t):
    rest = t % (2 * PAIRS)
    return t // (2 * PAIRS), rest // (2 * HN), rest % (2 * HN) // 2, rest % 2


def normalise(x):
    centred = x - jnp.mean(x, axis=-1, keepdims=True)
    variance = jnp.mean(centred * centred, axis=-1, keepdims=True)
    rstd = lax.rsqrt(variance + eps)
    return centred * rstd, rstd


def head_masks(dtype):
    lane = lax.broadcasted_iota(jnp.int32, (1, GROUP * HEAD), 1) // HEAD
    return [(lane == h).astype(dtype) for h in range(GROUP)]


def stack_heads(x):
    return jnp.concatenate([x * m for m in head_masks(x.dtype)], axis=0)


def merge_heads(y):
    masks = head_masks(f32)
    total = y[:SPAN] * masks[0]
    for h in range(1, GROUP):
        total = total + y[h * SPAN : (h + 1) * SPAN] * masks[h]
    return total


def mask_bias(refs, lats, parity):
    token = lax.broadcasted_iota(jnp.int32, (1, WIDE), 1)
    quadrant, r, c, level = token_place(token)
    lane = HN * swapped(1 - quadrant % 2, own_turned(lats)) + c
    hot = lax.broadcasted_iota(jnp.int32, (128, WIDE), 0) == lane
    rows = jnp.concatenate([ref[CLASS_AT + r, :, :128].astype(f32) for ref in refs for r in range(HL)], axis=0)
    spread = dot(rows.astype(bf16), hot.astype(f32).astype(bf16))
    piece = swapped(quadrant // 2, parity) * 2 + quadrant % 2
    mine = lax.broadcasted_iota(jnp.int32, (4 * HL * LEVELS, WIDE), 0) == (piece * HL + r) * LEVELS + level
    last = lax.axis_index("lat") == jnp.where(parity == 0, lats - 1, 0)
    seam = jnp.where(last, (quadrant // 2).astype(f32), 0.0)
    label = 2.0 * jnp.sum(jnp.where(mine, spread, 0.0), axis=0, keepdims=True) + seam
    label = jnp.where(token < SPAN, label, 9.0)
    eye = lax.broadcasted_iota(jnp.int32, (SPAN, WIDE), 0) == lax.broadcasted_iota(jnp.int32, (SPAN, WIDE), 1)
    column = jnp.sum(jnp.where(eye, label, 0.0), axis=1, keepdims=True)
    return jnp.where(column == label, 0.0, BLANK)


def pad_keys(x):
    return jnp.concatenate([x, jnp.zeros((WIDE - SPAN, x.shape[1]), x.dtype)], axis=0)


def block_forward(x, blank, bias_of, gain, offset, weight, bias, out_weight, out_bias, qkv_ref, probs_ref):
    xhat, _ = normalise(x)
    normed = (xhat * gain + offset).astype(bf16)
    queries = (dot(normed, weight[:, :D]) + bias[:, :D]).astype(bf16) * jnp.array(HEAD**-0.5, bf16)
    qkv_ref[:, :D] = queries
    qkv_ref[:, D:] = (dot(normed, weight[:, D:]) + bias[:, D:]).astype(bf16)
    mixed = []
    for g in range(HEADS // GROUP):
        lanes = pl.ds(g * GROUP * HEAD, GROUP * HEAD)
        q4 = stack_heads(qkv_ref[:, pl.ds(g * 256, 256)])
        k4 = pad_keys(qkv_ref[:, pl.ds(D + g * 256, 256)])
        v4 = pad_keys(qkv_ref[:, pl.ds(2 * D + g * 256, 256)])
        scores = dot_nt(q4, k4)
        for h in range(GROUP):
            s = scores[h * SPAN : (h + 1) * SPAN] + bias_of(g * GROUP + h) + blank
            e = jnp.exp(s - jnp.max(s, axis=-1, keepdims=True))
            p = e * (1.0 / jnp.sum(e, axis=-1, keepdims=True))
            probs_ref[pl.ds((g * GROUP + h) * SPAN, SPAN), :] = p.astype(bf16)
        p4 = probs_ref[pl.ds(g * GROUP * SPAN, GROUP * SPAN), :]
        mixed.append(merge_heads(dot(p4, v4)))
    heads_out = jnp.concatenate(mixed, axis=1).astype(bf16)
    return x + dot(heads_out, out_weight) + out_bias


def block_backward(grad, x, gain, weight, out_weight, qkv_ref, probs_ref, dqkv_ref):
    dheads = dot_nt(grad, out_weight).astype(bf16)
    for g in range(HEADS // GROUP):
        q4 = stack_heads(qkv_ref[:, pl.ds(g * 256, 256)])
        k4 = pad_keys(qkv_ref[:, pl.ds(D + g * 256, 256)])
        v4 = pad_keys(qkv_ref[:, pl.ds(2 * D + g * 256, 256)])
        do4 = stack_heads(dheads[:, g * 256 : (g + 1) * 256])
        p4 = probs_ref[pl.ds(g * GROUP * SPAN, GROUP * SPAN), :]
        dprobs = dot_nt(do4, v4)
        pf = p4.astype(f32)
        weighted = pf * dprobs
        ds = (weighted - pf * jnp.sum(weighted, axis=-1, keepdims=True)).astype(bf16)
        dq = merge_heads(dot(ds, k4)) * HEAD**-0.5
        dk = dot_tn(ds[:, :SPAN], q4)
        dv = dot_tn(p4[:, :SPAN], do4)
        dqkv_ref[:, pl.ds(g * 256, 256)] = dq.astype(bf16)
        dqkv_ref[:, pl.ds(D + g * 256, 256)] = dk.astype(bf16)
        dqkv_ref[:, pl.ds(2 * D + g * 256, 256)] = dv.astype(bf16)
    dnormed = dot_nt(dqkv_ref[...], weight).astype(bf16).astype(f32)
    xhat, rstd = normalise(x)
    dxhat = dnormed * gain
    dx = rstd * (
        dxhat
        - jnp.mean(dxhat, axis=-1, keepdims=True)
        - xhat * jnp.mean(dxhat * xhat, axis=-1, keepdims=True)
    )
    return grad.astype(f32) + dx.astype(bf16).astype(f32)


COARSE_ROWS, COARSE_COLS = HL // 2 + 1, HN // 2
POINTS = COARSE_ROWS * COARSE_COLS
COTANGENT_AT = PAIRS
COARSE_AT = 2 * PAIRS
CLASS_AT = 2 * PAIRS + 2 * POINTS


TILES = CLASS_AT + HL


def pack_kernel(
    lats, tokens_hbm, cotangent_hbm, coarse_hbm, classes_hbm, o0, o1, o2, o3,
    tokens, cotangent, coarse, classes, buffers, in_sems, out_sems,
):
    arrivals = [
        pltpu.make_async_copy(src, dst, in_sems.at[n])
        for n, (src, dst) in enumerate(
            ((tokens_hbm, tokens), (cotangent_hbm, cotangent), (coarse_hbm, coarse), (classes_hbm, classes))
        )
    ]
    for copy in arrivals:
        copy.start()
    buffers[:, pl.ds(CLASS_AT, HL)] = jnp.zeros((4, HL, LEVELS, D), bf16)
    for copy in arrivals:
        copy.wait()
    departures = []
    for q in (2, 1, 3, 0):
        later, right = piece_cut(*divmod(q, 2), lats)
        lat, lon = HL * later, HN * right
        low_lat, low_lon = (coarse.shape[0] - COARSE_ROWS) * later, COARSE_COLS * right
        for r in range(HL):
            buffers[q, pl.ds(r * HN, HN)] = tokens[lat + r, pl.ds(lon, HN)]
            buffers[q, pl.ds(COTANGENT_AT + r * HN, HN)] = cotangent[lat + r, pl.ds(lon, HN)]
            buffers[q, CLASS_AT + r, :, pl.ds(0, WIN_LON)] = classes[lat + r].astype(f32).astype(bf16)
        for r in range(COARSE_ROWS):
            for half in range(2):
                buffers[q, pl.ds(COARSE_AT + POINTS * half + r * COARSE_COLS, COARSE_COLS)] = coarse[
                    low_lat + r, pl.ds(low_lon, COARSE_COLS), :, pl.ds(D * half, D)
                ]
        copy = pltpu.make_async_copy(buffers.at[q], (o0, o1, o2, o3)[q], out_sems.at[q])
        copy.start()
        departures.append(copy)
    for copy in departures:
        copy.wait()


def lookup_kernel(lats, inputs_ref, out_ref, rest_ref, low, high, packed_low, packed_high, parts):
    token = lax.broadcasted_iota(jnp.int32, (SPAN, 1), 0)
    quadrant, r, c, level = token_place(token)
    right = swapped(quadrant % 2, own_turned(lats))
    old = level * (WIN_LAT * WIN_LON) + (quadrant // 2 * HL + r) * WIN_LON + right * HN + c
    order = (lax.broadcasted_iota(jnp.int32, (SPAN, SPAN), 1) == old).astype(f32).astype(bf16)
    index = inputs_ref[:SPAN, :SPAN].astype(jnp.int32)
    rest = SPAN - 128

    lane = lax.broadcasted_iota(jnp.int32, (rest, WIDE), 1)
    spread = (lane % rest == lax.broadcasted_iota(jnp.int32, (rest, WIDE), 0)).astype(f32).astype(bf16)
    own = (
        lax.broadcasted_iota(jnp.int32, (SPAN, WIDE), 1) // rest
        == lax.broadcasted_iota(jnp.int32, (SPAN, WIDE), 0) % rest
    )
    for part, full, packed in ((index % WIDE, low, packed_low), (index // WIDE, high, packed_high)):
        moved = dot_nt(dot(order, part.astype(f32).astype(bf16)).astype(bf16), order)
        full[...] = moved[:, :128]
        tail = jnp.where(own, dot(moved[:, 128:].astype(bf16), spread), 0.0)
        for g in range(SPAN // rest):
            packed[pl.ds(g, 1), :] = jnp.sum(tail[rest * g : rest * (g + 1)], axis=0, keepdims=True)

    left = inputs_ref[SPAN:]
    blocks = left.shape[1] // WIDE
    for k in range(3):
        piece = left.astype(bf16)
        left = left - piece.astype(f32)
        for b in range(blocks):
            parts[pl.ds((b * 3 + k) * 2 * HEADS, 2 * HEADS), :] = piece[:, b * WIDE : (b + 1) * WIDE]
    entries = parts[...]
    ids = lax.broadcasted_iota(jnp.int32, (16, WIDE), 0).astype(f32)
    ids = [(ids + 16 * n).astype(bf16) for n in range(WIDE // 16)]
    one, zero = jnp.ones((16, WIDE), bf16), jnp.zeros((16, WIDE), bf16)

    def look(low_row, high_row):
        wanted = jnp.broadcast_to(low_row, (16, WIDE)).astype(bf16)
        hot = jnp.concatenate([jnp.where(wanted == i, one, zero) for i in ids], axis=0)
        found = dot(entries, hot)
        sums = []
        for b in range(blocks):
            at = [found[(b * 3 + k) * 2 * HEADS : (b * 3 + k + 1) * 2 * HEADS] for k in range(3)]
            sums.append(at[0] + at[1] + at[2])
        result = sums[0]
        for b in range(1, blocks):
            result = jnp.where(high_row == b, sums[b], result)
        return result

    def two_rows(i):
        def pair(ref):
            return jnp.concatenate([ref[pl.ds(i, 1), :], ref[pl.ds(i + 1, 1), :]], axis=1)

        result = look(pair(low), pair(high))
        for n in range(2):
            for half in range(2):
                out_ref[pl.ds(half * HEADS * SPAN + i + n, HEADS, stride=SPAN), :] = result[
                    half * HEADS : (half + 1) * HEADS, n * 128 : (n + 1) * 128
                ]

    @pl.loop(0, SPAN // 48)
    def _(step):
        for n in range(24):
            two_rows(48 * step + 2 * n)

    for g in range(SPAN // rest):
        result = look(packed_low[pl.ds(g, 1), :], packed_high[pl.ds(g, 1), :])
        for n in range(rest):
            first = n * rest // 128 * 128
            for half in range(2):
                rest_ref[pl.ds(half * HEADS * SPAN + rest * g + n, HEADS, stride=SPAN), :] = pltpu.roll(
                    result[half * HEADS : (half + 1) * HEADS, first : first + 128], (first - n * rest) % 128, axis=1
                )


def lookup(lats, relative_index, encoder_table, decoder_table):
    blocks = -(-encoder_table.shape[1] // WIDE)

    def widen(rows):
        return jnp.pad(rows, ((0, 0), (0, blocks * WIDE - rows.shape[1])))

    inputs = jnp.concatenate([widen(relative_index.astype(f32)), widen(encoder_table), widen(decoder_table)], axis=0)
    return pl.pallas_call(
        functools.partial(lookup_kernel, lats),
        out_shape=[jax.ShapeDtypeStruct((2 * HEADS * SPAN, 128), f32)] * 2,
        scratch_shapes=[
            pltpu.VMEM((SPAN, 128), f32),
            pltpu.VMEM((SPAN, 128), f32),
            pltpu.VMEM((16, WIDE), f32),
            pltpu.VMEM((16, WIDE), f32),
            pltpu.VMEM((blocks * 3 * 2 * HEADS, WIDE), bf16),
        ],
        compiler_params=pltpu.CompilerParams(vmem_limit_bytes=32 * 2**20),
        cost_estimate=pl.CostEstimate(flops=3_000_000_000, bytes_accessed=4_000_000, transcendentals=0),
        name="lookup",
    )(inputs)


def coarse_points(qc):
    return [r * 2 * COARSE_COLS + qc * COARSE_COLS + c for r in range(COARSE_ROWS) for c in range(COARSE_COLS)]


def coarse_places():
    places = []
    for q in range(4):
        qr, qc = divmod(q, 2)
        for r in range(HL):
            for c in range(HN):
                row, column = qr * HL + r + HL % 2, qc * HN + c + HN % 2
                at = (row // 2) * 2 * COARSE_COLS + column // 2
                places.append((q * PAIRS + r * HN + c, at, (row % 2) * 2 + column % 2))
    return places


def main_kernel(
    lats, b0, b2, b1, b3, bias_main, bias_rest,
    e_gain, e_offset, e_bias, e_out_bias, d_gain, d_offset, d_bias, d_out_bias, split_bias,
    e_weight, e_out_weight, d_weight, d_out_weight, split,
    o0, o1, o2, o3,
    scratch, coarse, fine, tokens, e_qkv, e_probs, d_qkv, d_probs, dqkv,
):
    def bias_rows(h):
        rows = pl.ds(h * SPAN, SPAN)
        return jnp.concatenate([bias_main[rows, :], bias_rest[rows, :]], axis=1)

    parity = column_parity()
    parts = (b0, b1, b2, b3)
    gather_quadrants(parts, 0, scratch, parity)
    x = whole(scratch)
    tokens[...] = x.astype(bf16)
    blank = mask_bias(parts, lats, parity)
    encoded = block_forward(
        x, blank, lambda h: bias_rows(h), e_gain[...], e_offset[...], e_weight,
        e_bias[...].reshape(1, -1), e_out_weight[...], e_out_bias[...], e_qkv, e_probs,
    ).astype(bf16)

    for q, ref in enumerate(parts):
        part = swapped(q // 2, parity)
        for n, at in enumerate(coarse_points(q % 2)):
            for half in range(2):
                coarse[part, pl.ds(2 * at, 2), pl.ds(D * half, D)] = ref[COARSE_AT + POINTS * half + n].astype(f32)
    lowres = whole(coarse).astype(bf16)
    fine[...] = dot(lowres, split[...]) + split_bias[...]
    for t, at, kind in coarse_places():
        scratch[t // (2 * PAIRS), pl.ds(2 * (t % (2 * PAIRS)), 2), :] = fine[pl.ds(2 * at, 2), pl.ds(kind * D, D)]
    x = (encoded.astype(f32) + whole(scratch)).astype(bf16).astype(f32)
    decoded = block_forward(
        x, blank, lambda h: bias_rows(HEADS + h), d_gain[...], d_offset[...], d_weight,
        d_bias[...].reshape(1, -1), d_out_weight[...], d_out_bias[...], d_qkv, d_probs,
    )
    outs = (o0, o1, o2, o3)
    fill(scratch, decoded)
    scatter_quadrants(scratch, outs, 0, parity)
    gather_quadrants(parts, COTANGENT_AT, scratch, parity)
    grad = whole(scratch).astype(bf16)
    dx = block_backward(grad, x, d_gain[...], d_weight[...], d_out_weight[...], d_qkv, d_probs, dqkv)
    grad = dx.astype(bf16)

    fill(scratch, dx)
    fine[...] = jnp.zeros_like(fine)
    for t, at, kind in coarse_places():
        fine[pl.ds(2 * at, 2), pl.ds(kind * D, D)] = scratch[t // (2 * PAIRS), pl.ds(2 * (t % (2 * PAIRS)), 2), :]
    fill(coarse, dot_nt(fine[...].astype(bf16), split[...]))
    for q, ref in enumerate(outs):
        part = swapped(q // 2, parity)
        for n, at in enumerate(coarse_points(q % 2)):
            for half in range(2):
                ref[COARSE_AT + POINTS * half + n] = coarse[part, pl.ds(2 * at, 2), pl.ds(D * half, D)].astype(bf16)

    dx = block_backward(
        grad, tokens[...].astype(f32), e_gain[...], e_weight[...], e_out_weight[...], e_qkv, e_probs, dqkv
    )
    fill(scratch, dx)
    scatter_quadrants(scratch, outs, PAIRS, parity)


def home_kernel(lats, h0, h2, h1, h3, decoded, tokens_gradient, coarse_gradient, total, sems):
    copies = []
    total[...] = jnp.zeros_like(total)
    for q, ref in enumerate((h0, h1, h2, h3)):
        later, right = piece_cut(*divmod(q, 2), lats)
        for n, out in enumerate((decoded, tokens_gradient)):
            for r in range(HL):
                copy = pltpu.make_async_copy(
                    ref.at[pl.ds(PAIRS * n + r * HN, HN)],
                    out.at[HL * later + r, pl.ds(HN * right, HN)],
                    sems.at[len(copies)],
                )
                copy.start()
                copies.append(copy)
        for half in range(2):
            for r in range(COARSE_ROWS):
                for c in range(COARSE_COLS):
                    part = ref[COARSE_AT + POINTS * half + r * COARSE_COLS + c].astype(f32)
                    total[later + r, COARSE_COLS * right + c, :, pl.ds(D * half, D)] += part
    coarse_gradient[...] = total[...].astype(bf16)
    for copy in copies:
        copy.wait()


VM = pl.BlockSpec(memory_space=pltpu.VMEM)


ANY = pl.BlockSpec(memory_space=pl.ANY)


def call(kernel, name, inputs, outs, scratch, flops, in_specs=None, out_specs=None, vmem=32):
    return pl.pallas_call(
        kernel,
        out_shape=outs,
        in_specs=in_specs or [VM] * len(inputs),
        out_specs=out_specs or [VM] * len(outs),
        scratch_shapes=scratch,
        compiler_params=pltpu.CompilerParams(vmem_limit_bytes=vmem * 2**20),
        cost_estimate=pl.CostEstimate(flops=flops, bytes_accessed=flops // 1000, transcendentals=0),
        name=name,
    )(*inputs)


def exchange(pieces, lats, lons, back):
    out = list(pieces)
    for q in (2, 1, 3):
        m, n = divmod(q, 2)
        pairs = []
        for i in range(lats):
            for j in range(lons):
                target = (j + n) % 2
                turn = turned(i - (1 - target if m else target), lats)
                to = (i + m * (2 * target - 1)) % lats, (j + n * (2 * turn - 1)) % lons
                pairs.append((i * lons + j, to[0] * lons + to[1]))
        if back:
            pairs = [(target, source) for source, target in pairs]
        out[q] = lax.ppermute(pieces[q], ("lat", "lon"), pairs)
    return out


def per_device(
    lats, lons,
    tokens, coarse, output_cotangent, token_class, relative_index,
    encoder_gain, encoder_offset, encoder_projection, encoder_projection_bias,
    encoder_output_weight, encoder_output_bias, encoder_table,
    decoder_gain, decoder_offset, decoder_projection, decoder_projection_bias,
    decoder_output_weight, decoder_output_bias, decoder_table,
    split_weight, split_bias,
):
    def row(v):
        return v.reshape(1, -1)

    s = jax.ShapeDtypeStruct
    packed = call(
        functools.partial(pack_kernel, lats),
        "pack",
        [
            jnp.transpose(tokens, (1, 2, 0, 3)),
            jnp.transpose(output_cotangent, (1, 2, 0, 3)),
            jnp.transpose(coarse, (1, 2, 0, 3)),
            jnp.transpose(token_class, (1, 0, 2)),
        ],
        [s((TILES, LEVELS, D), bf16)] * 4,
        [
            pltpu.VMEM((WIN_LAT, WIN_LON, LEVELS, D), bf16),
            pltpu.VMEM((WIN_LAT, WIN_LON, LEVELS, D), bf16),
            pltpu.VMEM((WIN_LAT // 2, WIN_LON // 2, LEVELS, 2 * D), bf16),
            pltpu.VMEM((WIN_LAT, LEVELS, WIN_LON), jnp.int32),
            pltpu.VMEM((4, TILES, LEVELS, D), bf16),
            pltpu.SemaphoreType.DMA((4,)),
            pltpu.SemaphoreType.DMA((4,)),
        ],
        100_000_000,
        [ANY] * 4,
        [ANY] * 4,
        60,
    )
    parts = exchange(packed, lats, lons, False)
    biases = lookup(lats, relative_index, encoder_table, decoder_table)
    points = 4 * LEVELS * POINTS
    outs = call(
        functools.partial(main_kernel, lats),
        "main",
        [
            parts[0], parts[2], parts[1], parts[3], *biases,
            row(encoder_gain), row(encoder_offset), encoder_projection_bias, row(encoder_output_bias),
            row(decoder_gain), row(decoder_offset), decoder_projection_bias, row(decoder_output_bias),
            row(split_bias),
            encoder_projection, encoder_output_weight, decoder_projection, decoder_output_weight, split_weight,
        ],
        [s((CLASS_AT, LEVELS, D), bf16)] * 4,
        [
            pltpu.VMEM((2, SPAN // 2, D), f32),
            pltpu.VMEM((2, points // 2, 2 * D), f32),
            pltpu.VMEM((points, 4 * D), f32),
            pltpu.VMEM((SPAN, D), bf16),
            pltpu.VMEM((SPAN, 3 * D), bf16),
            pltpu.VMEM((HEADS * SPAN, WIDE), bf16),
            pltpu.VMEM((SPAN, 3 * D), bf16),
            pltpu.VMEM((HEADS * SPAN, WIDE), bf16),
            pltpu.VMEM((SPAN, 3 * D), bf16),
        ],
        8_000_000_000,
    )
    home = exchange(outs, lats, lons, True)
    grid = s((WIN_LAT, WIN_LON, LEVELS, D), bf16)
    low = s((WIN_LAT // 2, WIN_LON // 2, LEVELS, 2 * D), bf16)
    results = call(
        functools.partial(home_kernel, lats),
        "home",
        [home[0], home[2], home[1], home[3]],
        [grid, grid, low],
        [
            pltpu.VMEM((WIN_LAT // 2, WIN_LON // 2, LEVELS, 2 * D), f32),
            pltpu.SemaphoreType.DMA((4 * 2 * HL,)),
        ],
        1_000_000,
        None,
        [ANY, ANY, VM],
    )
    return tuple(jnp.transpose(r, (2, 0, 1, 3)) for r in results)


def solution(mesh):
    cut = P(None, "lat", "lon", None)
    in_specs = (cut, cut, cut, P(None, "lat", "lon")) + (P(),) * 17
    return jax.shard_map(
        functools.partial(per_device, mesh.shape["lat"], mesh.shape["lon"]),
        mesh=mesh,
        in_specs=in_specs,
        out_specs=(cut, cut, cut),
        check_vma=False,
    )
```

```python
import functools

import jax
import jax.numpy as jnp
from jax import lax
from jax.experimental import pallas as pl
from jax.experimental.pallas import tpu as pltpu
from jax.sharding import PartitionSpec as P

HEADS = 8
LEVELS = 2
WIN_LAT = 6
WIN_LON = 12
SPAN = LEVELS * WIN_LAT * WIN_LON
D = 512
HEAD = D // HEADS
WIDE = 256
FIRST = 128
REST = SPAN - FIRST
HL, HN = WIN_LAT // 2, WIN_LON // 2
PAIRS = HL * HN
GROUP = 4
BLANK = -1e30
eps = 1e-05

f32, bf16 = jnp.float32, jnp.bfloat16
NT = (((1,), (1,)), ((), ()))
TN = (((0,), (0,)), ((), ()))


def dot(a, b):
    return jnp.dot(a, b, preferred_element_type=f32)


def dot_nt(a, b):
    return lax.dot_general(a, b, NT, preferred_element_type=f32)


def dot_tn(a, b):
    return lax.dot_general(a, b, TN, preferred_element_type=f32)


def column_parity():
    return lax.axis_index("lon") % 2


def swapped(m, parity):
    return m + parity * (1 - 2 * m)


def turned(window_row, lats):
    return (window_row % lats + lats) % lats // (lats // 2)


def own_turned(lats):
    return turned(lax.axis_index("lat") - column_parity(), lats)


def piece_cut(m, n, lats):
    target = swapped(n, column_parity())
    window_row = lax.axis_index("lat") - (1 - target if m else target)
    return swapped(1 - m, target), swapped(1 - n, turned(window_row, lats))


def gather_quadrants(refs, base, scratch, parity):
    for q, ref in enumerate(refs):
        m, qc = divmod(q, 2)
        half = swapped(m, parity)
        for t in range(PAIRS):
            scratch[half, pl.ds(2 * (qc * PAIRS + t), 2), :] = ref[base + t].astype(f32)


def scatter_quadrants(scratch, refs, base, parity):
    for q, ref in enumerate(refs):
        m, qc = divmod(q, 2)
        half = swapped(m, parity)
        for t in range(PAIRS):
            ref[base + t] = scratch[half, pl.ds(2 * (qc * PAIRS + t), 2), :].astype(bf16)


def whole(scratch):
    return scratch[...].reshape(-1, scratch.shape[-1])


def fill(scratch, value):
    scratch[...] = value.reshape(scratch.shape)


def token_place(t):
    rest = t % (2 * PAIRS)
    return t // (2 * PAIRS), rest // (2 * HN), rest % (2 * HN) // 2, rest % 2


def normalise(x):
    centred = x - jnp.mean(x, axis=-1, keepdims=True)
    variance = jnp.mean(centred * centred, axis=-1, keepdims=True)
    rstd = lax.rsqrt(variance + eps)
    return centred * rstd, rstd


def head_of(lanes):
    return lax.broadcasted_iota(jnp.int32, (1, lanes), 1) // HEAD


def stack(x):
    lanes = x.shape[1]
    return jnp.concatenate([x * (head_of(lanes) == h).astype(x.dtype) for h in range(lanes // HEAD)], axis=0)


def unstack(y):
    lanes = y.shape[1]
    rows = y.shape[0] // (lanes // HEAD)
    total = y[:rows]
    for h in range(1, lanes // HEAD):
        total = jnp.where(head_of(lanes) == h, y[h * rows : (h + 1) * rows], total)
    return total


def main_lanes(g):
    return pl.ds(g * GROUP * HEAD, GROUP * HEAD)


def columns_of(g):
    return slice(g * GROUP * FIRST, (g + 1) * GROUP * FIRST)


def mask_bias(refs, lats, parity):
    lane = lax.broadcasted_iota(jnp.int32, (1, WIDE + FIRST), 1)
    token = jnp.where(lane < WIDE, lane, FIRST + lane % REST)
    quadrant, r, c, level = token_place(token)
    place = HN * swapped(1 - quadrant % 2, own_turned(lats)) + c
    hot = lax.broadcasted_iota(jnp.int32, (128, WIDE + FIRST), 0) == place
    rows = jnp.concatenate([ref[CLASS_AT + r, :, :128].astype(f32) for ref in refs for r in range(HL)], axis=0)
    spread = dot(rows.astype(bf16), hot.astype(f32).astype(bf16))
    piece = swapped(quadrant // 2, parity) * 2 + quadrant % 2
    row = lax.broadcasted_iota(jnp.int32, (4 * HL * LEVELS, WIDE + FIRST), 0)
    mine = row == (piece * HL + r) * LEVELS + level
    last = lax.axis_index("lat") == jnp.where(parity == 0, lats - 1, 0)
    seam = jnp.where(last, (quadrant // 2).astype(f32), 0.0)
    label = 2.0 * jnp.sum(jnp.where(mine, spread, 0.0), axis=0, keepdims=True) + seam
    eye = lax.broadcasted_iota(jnp.int32, (SPAN, WIDE), 0) == lax.broadcasted_iota(jnp.int32, (SPAN, WIDE), 1)
    column = jnp.sum(jnp.where(eye, label[:, :WIDE], 0.0), axis=1, keepdims=True)
    return [jnp.where(column == queries, 0.0, BLANK) for queries in (label[:, :FIRST], label[:, WIDE:])]


def block_forward(x, blank, bias_of, gain, offset, weight, bias, out_weight, out_bias, qkv_ref, probs_ref):
    xhat, _ = normalise(x)
    normed = (xhat * gain + offset).astype(bf16)
    queries = (dot(normed, weight[:, :D]) + bias[:, :D]).astype(bf16) * jnp.array(HEAD**-0.5, bf16)
    qkv_ref[:, :D] = queries
    qkv_ref[:, D:] = (dot(normed, weight[:, D:]) + bias[:, D:]).astype(bf16)
    keys, values = qkv_ref[:, D : 2 * D], qkv_ref[:, 2 * D :]

    def soften(s, tile):
        s = s + bias_of(tile) + blank[tile // HEADS]
        e = jnp.exp(s - jnp.max(s, axis=0, keepdims=True))
        p = e * (1.0 / jnp.sum(e, axis=0, keepdims=True))
        probs_ref[:, pl.ds(tile * FIRST, FIRST)] = p.astype(bf16)

    for g in range(HEADS // GROUP):
        scores = dot_nt(keys[:, g * 256 : (g + 1) * 256], stack(qkv_ref[:FIRST, main_lanes(g)]))
        for h in range(GROUP):
            soften(scores[:, h * FIRST : (h + 1) * FIRST], g * GROUP + h)
    soften(dot_nt(keys, stack(qkv_ref[FIRST:, :D])), HEADS)
    first = [
        unstack(dot_tn(probs_ref[:, columns_of(g)], values[:, g * 256 : (g + 1) * 256])) for g in range(HEADS // GROUP)
    ]
    rest = unstack(dot_tn(probs_ref[:, HEADS * FIRST :], values))
    heads_out = jnp.concatenate([jnp.concatenate(first, axis=1).astype(bf16), rest.astype(bf16)], axis=0)
    return x + dot(heads_out, out_weight) + out_bias


def block_backward(grad, x, gain, weight, out_weight, qkv_ref, probs_ref, dqkv_ref):
    dheads = dot_nt(grad, out_weight).astype(bf16)
    keys, values = qkv_ref[:, D : 2 * D], qkv_ref[:, 2 * D :]

    def harden(dprobs, columns):
        pf = probs_ref[:, columns].astype(f32)
        weighted = pf * dprobs
        return (weighted - pf * jnp.sum(weighted, axis=0, keepdims=True)).astype(bf16)

    last = slice(HEADS * FIRST, HEADS * FIRST + HEADS * REST)
    q_rest, do_rest = stack(qkv_ref[FIRST:, :D]), stack(dheads[FIRST:])
    ds_rest = harden(dot_nt(values, do_rest), last)
    dqkv_ref[FIRST:, :D] = (unstack(dot_tn(ds_rest, keys)) * HEAD**-0.5).astype(bf16)
    dk_rest, dv_rest = dot(ds_rest, q_rest), dot(probs_ref[:, last], do_rest)
    for g in range(HEADS // GROUP):
        lanes = slice(g * 256, (g + 1) * 256)
        q4, do4 = stack(qkv_ref[:FIRST, main_lanes(g)]), stack(dheads[:FIRST, lanes])
        ds = harden(dot_nt(values[:, lanes], do4), columns_of(g))
        dq = unstack(dot_tn(ds, keys[:, lanes])) * HEAD**-0.5
        dqkv_ref[:FIRST, lanes] = dq.astype(bf16)
        dqkv_ref[:, pl.ds(D + g * 256, 256)] = (dot(ds, q4) + dk_rest[:, lanes]).astype(bf16)
        dv = dot(probs_ref[:, columns_of(g)], do4) + dv_rest[:, lanes]
        dqkv_ref[:, pl.ds(2 * D + g * 256, 256)] = dv.astype(bf16)
    dnormed = dot_nt(dqkv_ref[...], weight)
    xhat, rstd = normalise(x)
    dxhat = dnormed * gain
    dx = rstd * (
        dxhat
        - jnp.mean(dxhat, axis=-1, keepdims=True)
        - xhat * jnp.mean(dxhat * xhat, axis=-1, keepdims=True)
    )
    return grad.astype(f32) + dx


COARSE_ROWS, COARSE_COLS = HL // 2 + 1, HN // 2
POINTS = COARSE_ROWS * COARSE_COLS
COTANGENT_AT = PAIRS
COARSE_AT = 2 * PAIRS
CLASS_AT = 2 * PAIRS + 2 * POINTS


TILES = CLASS_AT + HL


def pack_kernel(
    lats, tokens_hbm, cotangent_hbm, coarse_hbm, classes_hbm, o0, o1, o2, o3,
    tokens, cotangent, coarse, classes, buffers, in_sems, out_sems,
):
    arrivals = [
        pltpu.make_async_copy(src, dst, in_sems.at[n])
        for n, (src, dst) in enumerate(
            ((tokens_hbm, tokens), (cotangent_hbm, cotangent), (coarse_hbm, coarse), (classes_hbm, classes))
        )
    ]
    for copy in arrivals:
        copy.start()
    buffers[:, pl.ds(CLASS_AT, HL)] = jnp.zeros((4, HL, LEVELS, D), bf16)
    for copy in arrivals:
        copy.wait()
    departures = []
    for q in (2, 1, 3, 0):
        later, right = piece_cut(*divmod(q, 2), lats)
        lat, lon = HL * later, HN * right
        low_lat, low_lon = (coarse.shape[0] - COARSE_ROWS) * later, COARSE_COLS * right
        for r in range(HL):
            buffers[q, pl.ds(r * HN, HN)] = tokens[lat + r, pl.ds(lon, HN)]
            buffers[q, pl.ds(COTANGENT_AT + r * HN, HN)] = cotangent[lat + r, pl.ds(lon, HN)]
            buffers[q, CLASS_AT + r, :, pl.ds(0, WIN_LON)] = classes[lat + r].astype(f32).astype(bf16)
        for r in range(COARSE_ROWS):
            for half in range(2):
                buffers[q, pl.ds(COARSE_AT + POINTS * half + r * COARSE_COLS, COARSE_COLS)] = coarse[
                    low_lat + r, pl.ds(low_lon, COARSE_COLS), :, pl.ds(D * half, D)
                ]
        copy = pltpu.make_async_copy(buffers.at[q], (o0, o1, o2, o3)[q], out_sems.at[q])
        copy.start()
        departures.append(copy)
    for copy in departures:
        copy.wait()


def lookup_kernel(lats, inputs_ref, out_ref, rest_ref, low, high, packed_low, packed_high, parts, spots):
    token = lax.broadcasted_iota(jnp.int32, (SPAN, 1), 0)
    quadrant, r, c, level = token_place(token)
    right = swapped(quadrant % 2, own_turned(lats))
    old = level * (WIN_LAT * WIN_LON) + (quadrant // 2 * HL + r) * WIN_LON + right * HN + c
    order = (lax.broadcasted_iota(jnp.int32, (SPAN, SPAN), 1) == old).astype(f32).astype(bf16)
    index = inputs_ref[:SPAN, :SPAN].astype(jnp.int32)
    rest = SPAN - 128

    lane = lax.broadcasted_iota(jnp.int32, (rest, WIDE), 1)
    spread = (lane % rest == lax.broadcasted_iota(jnp.int32, (rest, WIDE), 0)).astype(f32).astype(bf16)
    own = (
        lax.broadcasted_iota(jnp.int32, (SPAN, WIDE), 1) // rest
        == lax.broadcasted_iota(jnp.int32, (SPAN, WIDE), 0) % rest
    )
    for part, full, packed in ((index % WIDE, low, packed_low), (index // WIDE, high, packed_high)):
        moved = dot_nt(dot_nt(order, part.astype(f32).astype(bf16)).astype(bf16), order)
        full[...] = moved[:, :128]
        tail = jnp.where(own, dot(moved[:, 128:].astype(bf16), spread), 0.0)
        for g in range(SPAN // rest):
            packed[pl.ds(g, 1), :] = jnp.sum(tail[rest * g : rest * (g + 1)], axis=0, keepdims=True)

    left = inputs_ref[SPAN:]
    blocks = left.shape[1] // WIDE
    for k in range(3):
        piece = left.astype(bf16)
        left = left - piece.astype(f32)
        for b in range(blocks):
            parts[pl.ds((b * 3 + k) * 2 * HEADS, 2 * HEADS), :] = piece[:, b * WIDE : (b + 1) * WIDE]
    entries = parts[...]
    ids = lax.broadcasted_iota(jnp.int32, (16, WIDE), 0).astype(f32)
    ids = [(ids + 16 * n).astype(bf16) for n in range(WIDE // 16)]
    one, zero = jnp.ones((16, WIDE), bf16), jnp.zeros((16, WIDE), bf16)

    def look(low_row, high_row):
        wanted = jnp.broadcast_to(low_row, (16, WIDE)).astype(bf16)
        hot = jnp.concatenate([jnp.where(wanted == i, one, zero) for i in ids], axis=0)
        found = dot(entries, hot)
        sums = []
        for b in range(blocks):
            at = [found[(b * 3 + k) * 2 * HEADS : (b * 3 + k + 1) * 2 * HEADS] for k in range(3)]
            sums.append(at[0] + at[1] + at[2])
        result = sums[0]
        for b in range(1, blocks):
            result = jnp.where(high_row == b, sums[b], result)
        return result

    def two_rows(i):
        def pair(ref):
            return jnp.concatenate([ref[pl.ds(i, 1), :], ref[pl.ds(i + 1, 1), :]], axis=1)

        result = look(pair(low), pair(high))
        for n in range(2):
            for half in range(2):
                out_ref[pl.ds(half * HEADS * SPAN + i + n, HEADS, stride=SPAN), :] = result[
                    half * HEADS : (half + 1) * HEADS, n * 128 : (n + 1) * 128
                ]

    @pl.loop(0, SPAN // 48)
    def _(step):
        for n in range(24):
            two_rows(48 * step + 2 * n)

    block = lax.broadcasted_iota(jnp.int32, (HEADS, 128), 1) // rest
    head = lax.broadcasted_iota(jnp.int32, (HEADS, 128), 0)
    for g in range(SPAN // rest):
        result = look(packed_low[pl.ds(g, 1), :], packed_high[pl.ds(g, 1), :])
        for first in range(0, WIDE, 128):
            for half in range(2):
                rows = result[half * HEADS : (half + 1) * HEADS, first : first + 128]
                rows = pltpu.roll(rows, 0, axis=1, stride=rest, stride_axis=0)
                for n in range(128 // rest):
                    at = half * HEADS * SPAN + rest * g + first // rest + n
                    spots[pl.ds(at, HEADS, stride=SPAN), :] = jnp.where(block == (head + n) % HEADS, rows, 0.0)
    lane = lax.broadcasted_iota(jnp.int32, (8, 128), 1)
    turn = (lane + rest * lax.broadcasted_iota(jnp.int32, (8, 128), 0)) % 128
    for half in range(2):
        for k in range(0, SPAN, 8):
            total = spots[pl.ds(half * HEADS * SPAN + k, 8), :]
            for h in range(1, HEADS):
                total = total + spots[pl.ds((half * HEADS + h) * SPAN + k, 8), :]
            rest_ref[pl.ds(half * SPAN + k, 8), :] = jnp.take_along_axis(
                total, turn, axis=1, mode="promise_in_bounds"
            )


def lookup(lats, relative_index, encoder_table, decoder_table):
    blocks = -(-encoder_table.shape[1] // WIDE)

    def widen(rows):
        return jnp.pad(rows, ((0, 0), (0, blocks * WIDE - rows.shape[1])))

    inputs = jnp.concatenate([widen(relative_index.astype(f32)), widen(encoder_table), widen(decoder_table)], axis=0)
    return pl.pallas_call(
        functools.partial(lookup_kernel, lats),
        out_shape=[
            jax.ShapeDtypeStruct((2 * HEADS * SPAN, FIRST), f32),
            jax.ShapeDtypeStruct((2 * SPAN, HEADS * REST), f32),
        ],
        scratch_shapes=[
            pltpu.VMEM((SPAN, 128), f32),
            pltpu.VMEM((SPAN, 128), f32),
            pltpu.VMEM((16, WIDE), f32),
            pltpu.VMEM((16, WIDE), f32),
            pltpu.VMEM((blocks * 3 * 2 * HEADS, WIDE), bf16),
            pltpu.VMEM((2 * HEADS * SPAN, 128), f32),
        ],
        compiler_params=pltpu.CompilerParams(vmem_limit_bytes=32 * 2**20),
        cost_estimate=pl.CostEstimate(flops=3_000_000_000, bytes_accessed=4_000_000, transcendentals=0),
        name="lookup",
    )(inputs)


def coarse_points(qc):
    return [r * 2 * COARSE_COLS + qc * COARSE_COLS + c for r in range(COARSE_ROWS) for c in range(COARSE_COLS)]


def coarse_places():
    places = []
    for q in range(4):
        qr, qc = divmod(q, 2)
        for r in range(HL):
            for c in range(HN):
                row, column = qr * HL + r + HL % 2, qc * HN + c + HN % 2
                at = (row // 2) * 2 * COARSE_COLS + column // 2
                places.append((q * PAIRS + r * HN + c, at, (row % 2) * 2 + column % 2))
    return places


def main_kernel(
    lats, b0, b2, b1, b3, bias_main, bias_rest,
    e_gain, e_offset, e_bias, e_out_bias, d_gain, d_offset, d_bias, d_out_bias, split_bias,
    e_weight, e_out_weight, d_weight, d_out_weight, split,
    o0, o1, o2, o3,
    scratch, coarse, fine, tokens, e_qkv, e_probs, d_qkv, d_probs, dqkv,
):
    def bias_tiles(block):
        def tile(h):
            if h == HEADS:
                return bias_rest[pl.ds(block * SPAN, SPAN), :]
            return bias_main[pl.ds((block * HEADS + h) * SPAN, SPAN), :]

        return tile

    parity = column_parity()
    parts = (b0, b1, b2, b3)
    gather_quadrants(parts, 0, scratch, parity)
    x = whole(scratch)
    tokens[...] = x.astype(bf16)
    blank = mask_bias(parts, lats, parity)
    encoded = block_forward(
        x, blank, bias_tiles(0), e_gain[...], e_offset[...], e_weight,
        e_bias[...].reshape(1, -1), e_out_weight[...], e_out_bias[...], e_qkv, e_probs,
    ).astype(bf16)

    for q, ref in enumerate(parts):
        part = swapped(q // 2, parity)
        for n, at in enumerate(coarse_points(q % 2)):
            for half in range(2):
                coarse[part, pl.ds(2 * at, 2), pl.ds(D * half, D)] = ref[COARSE_AT + POINTS * half + n].astype(f32)
    lowres = whole(coarse).astype(bf16)
    fine[...] = dot(lowres, split[...]) + split_bias[...]
    for t, at, kind in coarse_places():
        scratch[t // (2 * PAIRS), pl.ds(2 * (t % (2 * PAIRS)), 2), :] = fine[pl.ds(2 * at, 2), pl.ds(kind * D, D)]
    x = (encoded.astype(f32) + whole(scratch)).astype(bf16).astype(f32)
    decoded = block_forward(
        x, blank, bias_tiles(1), d_gain[...], d_offset[...], d_weight,
        d_bias[...].reshape(1, -1), d_out_weight[...], d_out_bias[...], d_qkv, d_probs,
    )
    outs = (o0, o1, o2, o3)
    fill(scratch, decoded)
    scatter_quadrants(scratch, outs, 0, parity)
    gather_quadrants(parts, COTANGENT_AT, scratch, parity)
    grad = whole(scratch).astype(bf16)
    dx = block_backward(grad, x, d_gain[...], d_weight[...], d_out_weight[...], d_qkv, d_probs, dqkv)
    grad = dx.astype(bf16)

    fill(scratch, dx)
    fine[...] = jnp.zeros_like(fine)
    for t, at, kind in coarse_places():
        fine[pl.ds(2 * at, 2), pl.ds(kind * D, D)] = scratch[t // (2 * PAIRS), pl.ds(2 * (t % (2 * PAIRS)), 2), :]
    fill(coarse, dot_nt(fine[...].astype(bf16), split[...]))
    for q, ref in enumerate(outs):
        part = swapped(q // 2, parity)
        for n, at in enumerate(coarse_points(q % 2)):
            for half in range(2):
                ref[COARSE_AT + POINTS * half + n] = coarse[part, pl.ds(2 * at, 2), pl.ds(D * half, D)].astype(bf16)

    dx = block_backward(
        grad, tokens[...].astype(f32), e_gain[...], e_weight[...], e_out_weight[...], e_qkv, e_probs, dqkv
    )
    fill(scratch, dx)
    scatter_quadrants(scratch, outs, PAIRS, parity)


def home_kernel(lats, h0, h2, h1, h3, decoded, tokens_gradient, coarse_gradient, total, sems):
    copies = []
    total[...] = jnp.zeros_like(total)
    for q, ref in enumerate((h0, h1, h2, h3)):
        later, right = piece_cut(*divmod(q, 2), lats)
        for n, out in enumerate((decoded, tokens_gradient)):
            for r in range(HL):
                copy = pltpu.make_async_copy(
                    ref.at[pl.ds(PAIRS * n + r * HN, HN)],
                    out.at[HL * later + r, pl.ds(HN * right, HN)],
                    sems.at[len(copies)],
                )
                copy.start()
                copies.append(copy)
        for half in range(2):
            for r in range(COARSE_ROWS):
                for c in range(COARSE_COLS):
                    part = ref[COARSE_AT + POINTS * half + r * COARSE_COLS + c].astype(f32)
                    total[later + r, COARSE_COLS * right + c, :, pl.ds(D * half, D)] += part
    coarse_gradient[...] = total[...].astype(bf16)
    for copy in copies:
        copy.wait()


VM = pl.BlockSpec(memory_space=pltpu.VMEM)


ANY = pl.BlockSpec(memory_space=pl.ANY)


def call(kernel, name, inputs, outs, scratch, flops, in_specs=None, out_specs=None, vmem=32):
    return pl.pallas_call(
        kernel,
        out_shape=outs,
        in_specs=in_specs or [VM] * len(inputs),
        out_specs=out_specs or [VM] * len(outs),
        scratch_shapes=scratch,
        compiler_params=pltpu.CompilerParams(vmem_limit_bytes=vmem * 2**20),
        cost_estimate=pl.CostEstimate(flops=flops, bytes_accessed=flops // 1000, transcendentals=0),
        name=name,
    )(*inputs)


def exchange(pieces, lats, lons, back):
    out = list(pieces)
    for q in (2, 1, 3):
        m, n = divmod(q, 2)
        pairs = []
        for i in range(lats):
            for j in range(lons):
                target = (j + n) % 2
                turn = turned(i - (1 - target if m else target), lats)
                to = (i + m * (2 * target - 1)) % lats, (j + n * (2 * turn - 1)) % lons
                pairs.append((i * lons + j, to[0] * lons + to[1]))
        if back:
            pairs = [(target, source) for source, target in pairs]
        out[q] = lax.ppermute(pieces[q], ("lat", "lon"), pairs)
    return out


def per_device(
    lats, lons,
    tokens, coarse, output_cotangent, token_class, relative_index,
    encoder_gain, encoder_offset, encoder_projection, encoder_projection_bias,
    encoder_output_weight, encoder_output_bias, encoder_table,
    decoder_gain, decoder_offset, decoder_projection, decoder_projection_bias,
    decoder_output_weight, decoder_output_bias, decoder_table,
    split_weight, split_bias,
):
    def row(v):
        return v.reshape(1, -1)

    s = jax.ShapeDtypeStruct
    packed = call(
        functools.partial(pack_kernel, lats),
        "pack",
        [
            jnp.transpose(tokens, (1, 2, 0, 3)),
            jnp.transpose(output_cotangent, (1, 2, 0, 3)),
            jnp.transpose(coarse, (1, 2, 0, 3)),
            jnp.transpose(token_class, (1, 0, 2)),
        ],
        [s((TILES, LEVELS, D), bf16)] * 4,
        [
            pltpu.VMEM((WIN_LAT, WIN_LON, LEVELS, D), bf16),
            pltpu.VMEM((WIN_LAT, WIN_LON, LEVELS, D), bf16),
            pltpu.VMEM((WIN_LAT // 2, WIN_LON // 2, LEVELS, 2 * D), bf16),
            pltpu.VMEM((WIN_LAT, LEVELS, WIN_LON), jnp.int32),
            pltpu.VMEM((4, TILES, LEVELS, D), bf16),
            pltpu.SemaphoreType.DMA((4,)),
            pltpu.SemaphoreType.DMA((4,)),
        ],
        100_000_000,
        [ANY] * 4,
        [ANY] * 4,
        60,
    )
    parts = exchange(packed, lats, lons, False)
    biases = lookup(lats, relative_index, encoder_table, decoder_table)
    points = 4 * LEVELS * POINTS
    outs = call(
        functools.partial(main_kernel, lats),
        "main",
        [
            parts[0], parts[2], parts[1], parts[3], *biases,
            row(encoder_gain), row(encoder_offset), encoder_projection_bias, row(encoder_output_bias),
            row(decoder_gain), row(decoder_offset), decoder_projection_bias, row(decoder_output_bias),
            row(split_bias),
            encoder_projection, encoder_output_weight, decoder_projection, decoder_output_weight, split_weight,
        ],
        [s((CLASS_AT, LEVELS, D), bf16)] * 4,
        [
            pltpu.VMEM((2, SPAN // 2, D), f32),
            pltpu.VMEM((2, points // 2, 2 * D), f32),
            pltpu.VMEM((points, 4 * D), f32),
            pltpu.VMEM((SPAN, D), bf16),
            pltpu.VMEM((SPAN, 3 * D), bf16),
            pltpu.VMEM((SPAN, HEADS * SPAN), bf16),
            pltpu.VMEM((SPAN, 3 * D), bf16),
            pltpu.VMEM((SPAN, HEADS * SPAN), bf16),
            pltpu.VMEM((SPAN, 3 * D), bf16),
        ],
        8_000_000_000,
    )
    home = exchange(outs, lats, lons, True)
    grid = s((WIN_LAT, WIN_LON, LEVELS, D), bf16)
    low = s((WIN_LAT // 2, WIN_LON // 2, LEVELS, 2 * D), bf16)
    results = call(
        functools.partial(home_kernel, lats),
        "home",
        [home[0], home[2], home[1], home[3]],
        [grid, grid, low],
        [
            pltpu.VMEM((WIN_LAT // 2, WIN_LON // 2, LEVELS, 2 * D), f32),
            pltpu.SemaphoreType.DMA((4 * 2 * HL,)),
        ],
        1_000_000,
        None,
        [ANY, ANY, VM],
    )
    return tuple(jnp.transpose(r, (2, 0, 1, 3)) for r in results)


def solution(mesh):
    cut = P(None, "lat", "lon", None)
    in_specs = (cut, cut, cut, P(None, "lat", "lon")) + (P(),) * 17
    return jax.shard_map(
        functools.partial(per_device, mesh.shape["lat"], mesh.shape["lon"]),
        mesh=mesh,
        in_specs=in_specs,
        out_specs=(cut, cut, cut),
        check_vma=False,
    )
```

```python
import functools

import jax
import jax.numpy as jnp
from jax import lax
from jax.experimental import pallas as pl
from jax.experimental.pallas import tpu as pltpu
from jax.sharding import PartitionSpec as P

HEADS = 8
LEVELS = 2
WIN_LAT = 6
WIN_LON = 12
SPAN = LEVELS * WIN_LAT * WIN_LON
D = 512
HEAD = D // HEADS
WIDE = 256
FIRST = 128
REST = SPAN - FIRST
HL, HN = WIN_LAT // 2, WIN_LON // 2
PAIRS = HL * HN
GROUP = 4
BLANK = -1e30
eps = 1e-05

f32, bf16 = jnp.float32, jnp.bfloat16
NT = (((1,), (1,)), ((), ()))
TN = (((0,), (0,)), ((), ()))


def dot(a, b):
    return jnp.dot(a, b, preferred_element_type=f32)


def dot_nt(a, b):
    return lax.dot_general(a, b, NT, preferred_element_type=f32)


def dot_tn(a, b):
    return lax.dot_general(a, b, TN, preferred_element_type=f32)


def column_parity():
    return lax.axis_index("lon") % 2


def swapped(m, parity):
    return m + parity * (1 - 2 * m)


def piece_cut(m, n):
    return swapped(1 - m, swapped(n, column_parity())), 1 - n


def gather_quadrants(refs, base, scratch, parity):
    for q, ref in enumerate(refs):
        m, qc = divmod(q, 2)
        half = swapped(m, parity)
        for t in range(PAIRS):
            scratch[half, pl.ds(2 * (qc * PAIRS + t), 2), :] = ref[base + t].astype(f32)


def scatter_quadrants(scratch, refs, base, parity):
    for q, ref in enumerate(refs):
        m, qc = divmod(q, 2)
        half = swapped(m, parity)
        for t in range(PAIRS):
            ref[base + t] = scratch[half, pl.ds(2 * (qc * PAIRS + t), 2), :].astype(bf16)


def whole(scratch):
    return scratch[...].reshape(-1, scratch.shape[-1])


def fill(scratch, value):
    scratch[...] = value.reshape(scratch.shape)


def token_place(t):
    rest = t % (2 * PAIRS)
    return t // (2 * PAIRS), rest // (2 * HN), rest % (2 * HN) // 2, rest % 2


def normalise(x):
    centred = x - jnp.mean(x, axis=-1, keepdims=True)
    variance = jnp.mean(centred * centred, axis=-1, keepdims=True)
    rstd = lax.rsqrt(variance + eps)
    return centred * rstd, rstd


def head_of(lanes):
    return lax.broadcasted_iota(jnp.int32, (1, lanes), 1) // HEAD


def stack(x):
    lanes = x.shape[1]
    return jnp.concatenate([x * (head_of(lanes) == h).astype(x.dtype) for h in range(lanes // HEAD)], axis=0)


def unstack(y):
    lanes = y.shape[1]
    rows = y.shape[0] // (lanes // HEAD)
    total = y[:rows]
    for h in range(1, lanes // HEAD):
        total = jnp.where(head_of(lanes) == h, y[h * rows : (h + 1) * rows], total)
    return total


def main_lanes(g):
    return pl.ds(g * GROUP * HEAD, GROUP * HEAD)


def columns_of(g):
    return slice(g * GROUP * FIRST, (g + 1) * GROUP * FIRST)


def mask_bias(refs, lats, parity):
    lane = lax.broadcasted_iota(jnp.int32, (1, WIDE + FIRST), 1)
    token = jnp.where(lane < WIDE, lane, FIRST + lane % REST)
    quadrant, r, c, level = token_place(token)
    place = HN * (1 - quadrant % 2) + c
    hot = lax.broadcasted_iota(jnp.int32, (128, WIDE + FIRST), 0) == place
    rows = jnp.concatenate([ref[CLASS_AT + r, :, :128].astype(f32) for ref in refs for r in range(HL)], axis=0)
    spread = dot(rows.astype(bf16), hot.astype(f32).astype(bf16))
    piece = swapped(quadrant // 2, parity) * 2 + quadrant % 2
    row = lax.broadcasted_iota(jnp.int32, (4 * HL * LEVELS, WIDE + FIRST), 0)
    mine = row == (piece * HL + r) * LEVELS + level
    last = lax.axis_index("lat") == jnp.where(parity == 0, lats - 1, 0)
    seam = jnp.where(last, (quadrant // 2).astype(f32), 0.0)
    label = 2.0 * jnp.sum(jnp.where(mine, spread, 0.0), axis=0, keepdims=True) + seam
    eye = lax.broadcasted_iota(jnp.int32, (SPAN, WIDE), 0) == lax.broadcasted_iota(jnp.int32, (SPAN, WIDE), 1)
    column = jnp.sum(jnp.where(eye, label[:, :WIDE], 0.0), axis=1, keepdims=True)
    return [jnp.where(column == queries, 0.0, BLANK) for queries in (label[:, :FIRST], label[:, WIDE:])]


def block_forward(x, blank, bias_of, gain, offset, weight, bias, out_weight, out_bias, qkv_ref, probs_ref):
    xhat, _ = normalise(x)
    normed = (xhat * gain + offset).astype(bf16)
    queries = (dot(normed, weight[:, :D]) + bias[:, :D]).astype(bf16) * jnp.array(HEAD**-0.5, bf16)
    qkv_ref[:, :D] = queries
    qkv_ref[:, D:] = (dot(normed, weight[:, D:]) + bias[:, D:]).astype(bf16)
    keys, values = qkv_ref[:, D : 2 * D], qkv_ref[:, 2 * D :]

    def soften(s, tile):
        s = s + bias_of(tile) + blank[tile // HEADS]
        e = jnp.exp(s - jnp.max(s, axis=0, keepdims=True))
        p = e * (1.0 / jnp.sum(e, axis=0, keepdims=True))
        probs_ref[:, pl.ds(tile * FIRST, FIRST)] = p.astype(bf16)

    for g in range(HEADS // GROUP):
        scores = dot_nt(keys[:, g * 256 : (g + 1) * 256], stack(qkv_ref[:FIRST, main_lanes(g)]))
        for h in range(GROUP):
            soften(scores[:, h * FIRST : (h + 1) * FIRST], g * GROUP + h)
    soften(dot_nt(keys, stack(qkv_ref[FIRST:, :D])), HEADS)
    first = [
        unstack(dot_tn(probs_ref[:, columns_of(g)], values[:, g * 256 : (g + 1) * 256])) for g in range(HEADS // GROUP)
    ]
    rest = unstack(dot_tn(probs_ref[:, HEADS * FIRST :], values))
    heads_out = jnp.concatenate([jnp.concatenate(first, axis=1).astype(bf16), rest.astype(bf16)], axis=0)
    return x + dot(heads_out, out_weight) + out_bias


def block_backward(grad, x, gain, weight, out_weight, qkv_ref, probs_ref, dqkv_ref):
    dheads = dot_nt(grad, out_weight).astype(bf16)
    keys, values = qkv_ref[:, D : 2 * D], qkv_ref[:, 2 * D :]

    def harden(dprobs, columns):
        pf = probs_ref[:, columns].astype(f32)
        weighted = pf * dprobs
        return (weighted - pf * jnp.sum(weighted, axis=0, keepdims=True)).astype(bf16)

    last = slice(HEADS * FIRST, HEADS * FIRST + HEADS * REST)
    q_rest, do_rest = stack(qkv_ref[FIRST:, :D]), stack(dheads[FIRST:])
    ds_rest = harden(dot_nt(values, do_rest), last)
    dqkv_ref[FIRST:, :D] = (unstack(dot_tn(ds_rest, keys)) * HEAD**-0.5).astype(bf16)
    dk_rest, dv_rest = dot(ds_rest, q_rest), dot(probs_ref[:, last], do_rest)
    for g in range(HEADS // GROUP):
        lanes = slice(g * 256, (g + 1) * 256)
        q4, do4 = stack(qkv_ref[:FIRST, main_lanes(g)]), stack(dheads[:FIRST, lanes])
        ds = harden(dot_nt(values[:, lanes], do4), columns_of(g))
        dq = unstack(dot_tn(ds, keys[:, lanes])) * HEAD**-0.5
        dqkv_ref[:FIRST, lanes] = dq.astype(bf16)
        dqkv_ref[:, pl.ds(D + g * 256, 256)] = (dot(ds, q4) + dk_rest[:, lanes]).astype(bf16)
        dv = dot(probs_ref[:, columns_of(g)], do4) + dv_rest[:, lanes]
        dqkv_ref[:, pl.ds(2 * D + g * 256, 256)] = dv.astype(bf16)
    dnormed = dot_nt(dqkv_ref[...], weight)
    xhat, rstd = normalise(x)
    dxhat = dnormed * gain
    dx = rstd * (
        dxhat
        - jnp.mean(dxhat, axis=-1, keepdims=True)
        - xhat * jnp.mean(dxhat * xhat, axis=-1, keepdims=True)
    )
    return grad.astype(f32) + dx


COARSE_ROWS, COARSE_COLS = HL // 2 + 1, HN // 2
POINTS = COARSE_ROWS * COARSE_COLS
COTANGENT_AT = PAIRS
COARSE_AT = 2 * PAIRS
CLASS_AT = 2 * PAIRS + 2 * POINTS


TILES = CLASS_AT + HL


def pack_kernel(
    tokens_hbm, cotangent_hbm, coarse_hbm, classes_hbm, o0, o1, o2, o3,
    tokens, cotangent, coarse, classes, buffers, in_sems, out_sems,
):
    arrivals = [
        pltpu.make_async_copy(src, dst, in_sems.at[n])
        for n, (src, dst) in enumerate(
            ((tokens_hbm, tokens), (cotangent_hbm, cotangent), (coarse_hbm, coarse), (classes_hbm, classes))
        )
    ]
    for copy in arrivals:
        copy.start()
    buffers[:, pl.ds(CLASS_AT, HL)] = jnp.zeros((4, HL, LEVELS, D), bf16)
    for copy in arrivals:
        copy.wait()
    departures = []
    for q in (1, 3, 2, 0):
        later, right = piece_cut(*divmod(q, 2))
        lat, lon = HL * later, HN * right
        low_lat, low_lon = (coarse.shape[0] - COARSE_ROWS) * later, COARSE_COLS * right
        for r in range(HL):
            buffers[q, pl.ds(r * HN, HN)] = tokens[lat + r, pl.ds(lon, HN)]
            buffers[q, pl.ds(COTANGENT_AT + r * HN, HN)] = cotangent[lat + r, pl.ds(lon, HN)]
            buffers[q, CLASS_AT + r, :, pl.ds(0, WIN_LON)] = classes[lat + r].astype(f32).astype(bf16)
        for r in range(COARSE_ROWS):
            for half in range(2):
                buffers[q, pl.ds(COARSE_AT + POINTS * half + r * COARSE_COLS, COARSE_COLS)] = coarse[
                    low_lat + r, pl.ds(low_lon, COARSE_COLS), :, pl.ds(D * half, D)
                ]
        copy = pltpu.make_async_copy(buffers.at[q], (o0, o1, o2, o3)[q], out_sems.at[q])
        copy.start()
        departures.append(copy)
    for copy in departures:
        copy.wait()


def lookup_kernel(inputs_ref, out_ref, rest_ref, low, high, packed_low, packed_high, parts, spots):
    token = lax.broadcasted_iota(jnp.int32, (SPAN, 1), 0)
    quadrant, r, c, level = token_place(token)
    old = level * (WIN_LAT * WIN_LON) + (quadrant // 2 * HL + r) * WIN_LON + quadrant % 2 * HN + c
    order = (lax.broadcasted_iota(jnp.int32, (SPAN, SPAN), 1) == old).astype(f32).astype(bf16)
    index = inputs_ref[:SPAN, :SPAN].astype(jnp.int32)
    rest = SPAN - 128

    lane = lax.broadcasted_iota(jnp.int32, (rest, WIDE), 1)
    spread = (lane % rest == lax.broadcasted_iota(jnp.int32, (rest, WIDE), 0)).astype(f32).astype(bf16)
    own = (
        lax.broadcasted_iota(jnp.int32, (SPAN, WIDE), 1) // rest
        == lax.broadcasted_iota(jnp.int32, (SPAN, WIDE), 0) % rest
    )
    for part, full, packed in ((index % WIDE, low, packed_low), (index // WIDE, high, packed_high)):
        moved = dot_nt(dot_nt(order, part.astype(f32).astype(bf16)).astype(bf16), order)
        full[...] = moved[:, :128]
        tail = jnp.where(own, dot(moved[:, 128:].astype(bf16), spread), 0.0)
        for g in range(SPAN // rest):
            packed[pl.ds(g, 1), :] = jnp.sum(tail[rest * g : rest * (g + 1)], axis=0, keepdims=True)

    left = inputs_ref[SPAN:]
    blocks = left.shape[1] // WIDE
    for k in range(3):
        piece = left.astype(bf16)
        left = left - piece.astype(f32)
        for b in range(blocks):
            parts[pl.ds((b * 3 + k) * 2 * HEADS, 2 * HEADS), :] = piece[:, b * WIDE : (b + 1) * WIDE]
    entries = parts[...]
    ids = lax.broadcasted_iota(jnp.int32, (16, WIDE), 0).astype(f32)
    ids = [(ids + 16 * n).astype(bf16) for n in range(WIDE // 16)]
    one, zero = jnp.ones((16, WIDE), bf16), jnp.zeros((16, WIDE), bf16)

    def look(low_row, high_row):
        wanted = jnp.broadcast_to(low_row, (16, WIDE)).astype(bf16)
        hot = jnp.concatenate([jnp.where(wanted == i, one, zero) for i in ids], axis=0)
        found = dot(entries, hot)
        sums = []
        for b in range(blocks):
            at = [found[(b * 3 + k) * 2 * HEADS : (b * 3 + k + 1) * 2 * HEADS] for k in range(3)]
            sums.append(at[0] + at[1] + at[2])
        result = sums[0]
        for b in range(1, blocks):
            result = jnp.where(high_row == b, sums[b], result)
        return result

    def two_rows(i):
        def pair(ref):
            return jnp.concatenate([ref[pl.ds(i, 1), :], ref[pl.ds(i + 1, 1), :]], axis=1)

        result = look(pair(low), pair(high))
        for n in range(2):
            for half in range(2):
                out_ref[pl.ds(half * HEADS * SPAN + i + n, HEADS, stride=SPAN), :] = result[
                    half * HEADS : (half + 1) * HEADS, n * 128 : (n + 1) * 128
                ]

    @pl.loop(0, SPAN // 48)
    def _(step):
        for n in range(24):
            two_rows(48 * step + 2 * n)

    block = lax.broadcasted_iota(jnp.int32, (HEADS, 128), 1) // rest
    head = lax.broadcasted_iota(jnp.int32, (HEADS, 128), 0)
    for g in range(SPAN // rest):
        result = look(packed_low[pl.ds(g, 1), :], packed_high[pl.ds(g, 1), :])
        for first in range(0, WIDE, 128):
            for half in range(2):
                rows = result[half * HEADS : (half + 1) * HEADS, first : first + 128]
                rows = pltpu.roll(rows, 0, axis=1, stride=rest, stride_axis=0)
                for n in range(128 // rest):
                    at = half * HEADS * SPAN + rest * g + first // rest + n
                    spots[pl.ds(at, HEADS, stride=SPAN), :] = jnp.where(block == (head + n) % HEADS, rows, 0.0)
    lane = lax.broadcasted_iota(jnp.int32, (8, 128), 1)
    turn = (lane + rest * lax.broadcasted_iota(jnp.int32, (8, 128), 0)) % 128
    for half in range(2):
        for k in range(0, SPAN, 8):
            total = spots[pl.ds(half * HEADS * SPAN + k, 8), :]
            for h in range(1, HEADS):
                total = total + spots[pl.ds((half * HEADS + h) * SPAN + k, 8), :]
            rest_ref[pl.ds(half * SPAN + k, 8), :] = jnp.take_along_axis(
                total, turn, axis=1, mode="promise_in_bounds"
            )


def lookup(relative_index, encoder_table, decoder_table):
    blocks = -(-encoder_table.shape[1] // WIDE)

    def placed(rows, at):
        return jnp.pad(rows, ((at, SPAN + 2 * HEADS - at - rows.shape[0]), (0, blocks * WIDE - rows.shape[1])))

    inputs = placed(relative_index, 0).astype(f32) + placed(encoder_table, SPAN) + placed(decoder_table, SPAN + HEADS)
    return pl.pallas_call(
        lookup_kernel,
        out_shape=[
            jax.ShapeDtypeStruct((2 * HEADS * SPAN, FIRST), f32),
            jax.ShapeDtypeStruct((2 * SPAN, HEADS * REST), f32),
        ],
        scratch_shapes=[
            pltpu.VMEM((SPAN, 128), f32),
            pltpu.VMEM((SPAN, 128), f32),
            pltpu.VMEM((16, WIDE), f32),
            pltpu.VMEM((16, WIDE), f32),
            pltpu.VMEM((blocks * 3 * 2 * HEADS, WIDE), bf16),
            pltpu.VMEM((2 * HEADS * SPAN, 128), f32),
        ],
        compiler_params=pltpu.CompilerParams(vmem_limit_bytes=32 * 2**20),
        cost_estimate=pl.CostEstimate(flops=3_000_000_000, bytes_accessed=4_000_000, transcendentals=0),
        name="lookup",
    )(inputs)


def coarse_points(qc):
    return [r * 2 * COARSE_COLS + qc * COARSE_COLS + c for r in range(COARSE_ROWS) for c in range(COARSE_COLS)]


def coarse_places():
    places = []
    for q in range(4):
        qr, qc = divmod(q, 2)
        for r in range(HL):
            for c in range(HN):
                row, column = qr * HL + r + HL % 2, qc * HN + c + HN % 2
                at = (row // 2) * 2 * COARSE_COLS + column // 2
                places.append((q * PAIRS + r * HN + c, at, (row % 2) * 2 + column % 2))
    return places


def main_kernel(
    lats, b0, b1, b3, b2, bias_main, bias_rest,
    e_gain, e_offset, e_bias, e_out_bias, d_gain, d_offset, d_bias, d_out_bias, split_bias,
    e_weight, e_out_weight, d_weight, d_out_weight, split,
    o0, o1, o2, o3,
    scratch, coarse, fine, tokens, e_qkv, e_probs, d_qkv, d_probs, dqkv,
):
    def bias_tiles(block):
        def tile(h):
            if h == HEADS:
                return bias_rest[pl.ds(block * SPAN, SPAN), :]
            return bias_main[pl.ds((block * HEADS + h) * SPAN, SPAN), :]

        return tile

    parity = column_parity()
    parts = (b0, b1, b2, b3)
    gather_quadrants(parts, 0, scratch, parity)
    x = whole(scratch)
    tokens[...] = x.astype(bf16)
    blank = mask_bias(parts, lats, parity)
    encoded = block_forward(
        x, blank, bias_tiles(0), e_gain[...], e_offset[...], e_weight,
        e_bias[...].reshape(1, -1), e_out_weight[...], e_out_bias[...], e_qkv, e_probs,
    ).astype(bf16)

    for q, ref in enumerate(parts):
        part = swapped(q // 2, parity)
        for n, at in enumerate(coarse_points(q % 2)):
            for half in range(2):
                coarse[part, pl.ds(2 * at, 2), pl.ds(D * half, D)] = ref[COARSE_AT + POINTS * half + n].astype(f32)
    lowres = whole(coarse).astype(bf16)
    fine[...] = dot(lowres, split[...]) + split_bias[...]
    for t, at, kind in coarse_places():
        scratch[t // (2 * PAIRS), pl.ds(2 * (t % (2 * PAIRS)), 2), :] = fine[pl.ds(2 * at, 2), pl.ds(kind * D, D)]
    x = (encoded.astype(f32) + whole(scratch)).astype(bf16).astype(f32)
    decoded = block_forward(
        x, blank, bias_tiles(1), d_gain[...], d_offset[...], d_weight,
        d_bias[...].reshape(1, -1), d_out_weight[...], d_out_bias[...], d_qkv, d_probs,
    )
    outs = (o0, o1, o2, o3)
    fill(scratch, decoded)
    scatter_quadrants(scratch, outs, 0, parity)
    gather_quadrants(parts, COTANGENT_AT, scratch, parity)
    grad = whole(scratch).astype(bf16)
    dx = block_backward(grad, x, d_gain[...], d_weight[...], d_out_weight[...], d_qkv, d_probs, dqkv)
    grad = dx.astype(bf16)

    fill(scratch, dx)
    fine[...] = jnp.zeros_like(fine)
    for t, at, kind in coarse_places():
        fine[pl.ds(2 * at, 2), pl.ds(kind * D, D)] = scratch[t // (2 * PAIRS), pl.ds(2 * (t % (2 * PAIRS)), 2), :]
    fill(coarse, dot_nt(fine[...].astype(bf16), split[...]))
    for q, ref in enumerate(outs):
        part = swapped(q // 2, parity)
        for n, at in enumerate(coarse_points(q % 2)):
            for half in range(2):
                ref[COARSE_AT + POINTS * half + n] = coarse[part, pl.ds(2 * at, 2), pl.ds(D * half, D)].astype(bf16)

    dx = block_backward(
        grad, tokens[...].astype(f32), e_gain[...], e_weight[...], e_out_weight[...], e_qkv, e_probs, dqkv
    )
    fill(scratch, dx)
    scatter_quadrants(scratch, outs, PAIRS, parity)


def home_kernel(h0, h1, h3, h2, decoded, tokens_gradient, coarse_gradient, total, sems):
    copies = []
    total[...] = jnp.zeros_like(total)
    for q, ref in enumerate((h0, h1, h2, h3)):
        later, right = piece_cut(*divmod(q, 2))
        for n, out in enumerate((decoded, tokens_gradient)):
            for r in range(HL):
                copy = pltpu.make_async_copy(
                    ref.at[pl.ds(PAIRS * n + r * HN, HN)],
                    out.at[HL * later + r, pl.ds(HN * right, HN)],
                    sems.at[len(copies)],
                )
                copy.start()
                copies.append(copy)
        for half in range(2):
            for r in range(COARSE_ROWS):
                for c in range(COARSE_COLS):
                    part = ref[COARSE_AT + POINTS * half + r * COARSE_COLS + c].astype(f32)
                    total[later + r, COARSE_COLS * right + c, :, pl.ds(D * half, D)] += part
    coarse_gradient[...] = total[...].astype(bf16)
    for copy in copies:
        copy.wait()


VM = pl.BlockSpec(memory_space=pltpu.VMEM)


ANY = pl.BlockSpec(memory_space=pl.ANY)


def call(kernel, name, inputs, outs, scratch, flops, in_specs=None, out_specs=None, vmem=32):
    return pl.pallas_call(
        kernel,
        out_shape=outs,
        in_specs=in_specs or [VM] * len(inputs),
        out_specs=out_specs or [VM] * len(outs),
        scratch_shapes=scratch,
        compiler_params=pltpu.CompilerParams(vmem_limit_bytes=vmem * 2**20),
        cost_estimate=pl.CostEstimate(flops=flops, bytes_accessed=flops // 1000, transcendentals=0),
        name=name,
    )(*inputs)


def exchange(pieces, lats, lons, back):
    out = list(pieces)
    for q in (1, 3, 2):
        m, n = divmod(q, 2)
        pairs = []
        for i in range(lats):
            for j in range(lons):
                to = (j - n) % lons
                step = m * (1 if to % 2 else -1)
                pairs.append((i * lons + j, (i + step) % lats * lons + to))
        if back:
            pairs = [(target, source) for source, target in pairs]
        out[q] = lax.ppermute(pieces[q], ("lat", "lon"), pairs)
    return out


def per_device(
    lats, lons,
    tokens, coarse, output_cotangent, token_class, relative_index,
    encoder_gain, encoder_offset, encoder_projection, encoder_projection_bias,
    encoder_output_weight, encoder_output_bias, encoder_table,
    decoder_gain, decoder_offset, decoder_projection, decoder_projection_bias,
    decoder_output_weight, decoder_output_bias, decoder_table,
    split_weight, split_bias,
):
    def row(v):
        return v.reshape(1, -1)

    s = jax.ShapeDtypeStruct
    packed = call(
        pack_kernel,
        "pack",
        [
            jnp.transpose(tokens, (1, 2, 0, 3)),
            jnp.transpose(output_cotangent, (1, 2, 0, 3)),
            jnp.transpose(coarse, (1, 2, 0, 3)),
            jnp.transpose(token_class, (1, 0, 2)),
        ],
        [s((TILES, LEVELS, D), bf16)] * 4,
        [
            pltpu.VMEM((WIN_LAT, WIN_LON, LEVELS, D), bf16),
            pltpu.VMEM((WIN_LAT, WIN_LON, LEVELS, D), bf16),
            pltpu.VMEM((WIN_LAT // 2, WIN_LON // 2, LEVELS, 2 * D), bf16),
            pltpu.VMEM((WIN_LAT, LEVELS, WIN_LON), jnp.int32),
            pltpu.VMEM((4, TILES, LEVELS, D), bf16),
            pltpu.SemaphoreType.DMA((4,)),
            pltpu.SemaphoreType.DMA((4,)),
        ],
        100_000_000,
        [ANY] * 4,
        [ANY] * 4,
        60,
    )
    parts = exchange(packed, lats, lons, False)
    biases = lookup(relative_index, encoder_table, decoder_table)
    points = 4 * LEVELS * POINTS
    outs = call(
        functools.partial(main_kernel, lats),
        "main",
        [
            parts[0], parts[1], parts[3], parts[2], *biases,
            row(encoder_gain), row(encoder_offset), encoder_projection_bias, row(encoder_output_bias),
            row(decoder_gain), row(decoder_offset), decoder_projection_bias, row(decoder_output_bias),
            row(split_bias),
            encoder_projection, encoder_output_weight, decoder_projection, decoder_output_weight, split_weight,
        ],
        [s((CLASS_AT, LEVELS, D), bf16)] * 4,
        [
            pltpu.VMEM((2, SPAN // 2, D), f32),
            pltpu.VMEM((2, points // 2, 2 * D), f32),
            pltpu.VMEM((points, 4 * D), f32),
            pltpu.VMEM((SPAN, D), bf16),
            pltpu.VMEM((SPAN, 3 * D), bf16),
            pltpu.VMEM((SPAN, HEADS * SPAN), bf16),
            pltpu.VMEM((SPAN, 3 * D), bf16),
            pltpu.VMEM((SPAN, HEADS * SPAN), bf16),
            pltpu.VMEM((SPAN, 3 * D), bf16),
        ],
        8_000_000_000,
    )
    home = exchange(outs, lats, lons, True)
    grid = s((WIN_LAT, WIN_LON, LEVELS, D), bf16)
    low = s((WIN_LAT // 2, WIN_LON // 2, LEVELS, 2 * D), bf16)
    results = call(
        home_kernel,
        "home",
        [home[0], home[1], home[3], home[2]],
        [grid, grid, low],
        [
            pltpu.VMEM((WIN_LAT // 2, WIN_LON // 2, LEVELS, 2 * D), f32),
            pltpu.SemaphoreType.DMA((4 * 2 * HL,)),
        ],
        1_000_000,
        None,
        [ANY, ANY, VM],
    )
    return tuple(jnp.transpose(r, (2, 0, 1, 3)) for r in results)


def solution(mesh):
    cut = P(None, "lat", "lon", None)
    in_specs = (cut, cut, cut, P(None, "lat", "lon")) + (P(),) * 17
    return jax.shard_map(
        functools.partial(per_device, mesh.shape["lat"], mesh.shape["lon"]),
        mesh=mesh,
        in_specs=in_specs,
        out_specs=(cut, cut, cut),
        check_vma=False,
    )
```

```python
import functools

import jax
import jax.numpy as jnp
from jax import lax
from jax.experimental import pallas as pl
from jax.experimental.pallas import tpu as pltpu
from jax.sharding import PartitionSpec as P

HEADS = 8
LEVELS = 2
WIN_LAT = 6
WIN_LON = 12
SPAN = LEVELS * WIN_LAT * WIN_LON
D = 512
HEAD = D // HEADS
WIDE = 256
FIRST = 128
REST = SPAN - FIRST
HL, HN = WIN_LAT // 2, WIN_LON // 2
PAIRS = HL * HN
GROUP = 4
BLANK = -1e30
eps = 1e-05

f32, bf16 = jnp.float32, jnp.bfloat16
NT = (((1,), (1,)), ((), ()))
TN = (((0,), (0,)), ((), ()))


def dot(a, b):
    return jnp.dot(a, b, preferred_element_type=f32)


def dot_nt(a, b):
    return lax.dot_general(a, b, NT, preferred_element_type=f32)


def dot_tn(a, b):
    return lax.dot_general(a, b, TN, preferred_element_type=f32)


def column_parity():
    return lax.axis_index("lon") % 2


def swapped(m, parity):
    return m + parity * (1 - 2 * m)


def piece_cut(m, n):
    return swapped(1 - m, swapped(n, column_parity())), 1 - n


def gather_quadrants(refs, base, scratch, parity):
    for q, ref in enumerate(refs):
        m, n = divmod(q, 2)
        rows = ref[pl.ds(base, PAIRS)].reshape(2 * PAIRS, D).astype(f32)
        scratch[swapped(m, parity), pl.ds(2 * PAIRS * n, 2 * PAIRS), :] = rows


def scatter_quadrants(scratch, refs, base, parity):
    for q, ref in enumerate(refs):
        m, n = divmod(q, 2)
        rows = scratch[swapped(m, parity), pl.ds(2 * PAIRS * n, 2 * PAIRS), :]
        ref[pl.ds(base, PAIRS)] = rows.astype(bf16).reshape(PAIRS, LEVELS, D)


def whole(scratch):
    return scratch[...].reshape(-1, scratch.shape[-1])


def fill(scratch, value):
    scratch[...] = value.reshape(scratch.shape)


def token_place(t):
    rest = t % (2 * PAIRS)
    return t // (2 * PAIRS), rest // (2 * HN), rest % (2 * HN) // 2, rest % 2


def normalise(x):
    centred = x - jnp.mean(x, axis=-1, keepdims=True)
    variance = jnp.mean(centred * centred, axis=-1, keepdims=True)
    rstd = lax.rsqrt(variance + eps)
    return centred * rstd, rstd


def head_of(lanes):
    return lax.broadcasted_iota(jnp.int32, (1, lanes), 1) // HEAD


def stack(x):
    lanes = x.shape[1]
    return jnp.concatenate([x * (head_of(lanes) == h).astype(x.dtype) for h in range(lanes // HEAD)], axis=0)


def unstack(y):
    lanes = y.shape[1]
    rows = y.shape[0] // (lanes // HEAD)
    total = y[:rows]
    for h in range(1, lanes // HEAD):
        total = jnp.where(head_of(lanes) == h, y[h * rows : (h + 1) * rows], total)
    return total


def main_lanes(g):
    return pl.ds(g * GROUP * HEAD, GROUP * HEAD)


def columns_of(g):
    return slice(g * GROUP * FIRST, (g + 1) * GROUP * FIRST)


def mask_bias(refs, lats, parity):
    lane = lax.broadcasted_iota(jnp.int32, (1, WIDE + FIRST), 1)
    token = jnp.where(lane < WIDE, lane, FIRST + lane % REST)
    quadrant, r, c, level = token_place(token)
    place = HN * (1 - quadrant % 2) + c
    hot = lax.broadcasted_iota(jnp.int32, (128, WIDE + FIRST), 0) == place
    rows = jnp.concatenate([ref[CLASS_AT + r, :, :128].astype(f32) for ref in refs for r in range(HL)], axis=0)
    spread = dot(rows.astype(bf16), hot.astype(f32).astype(bf16))
    piece = swapped(quadrant // 2, parity) * 2 + quadrant % 2
    row = lax.broadcasted_iota(jnp.int32, (4 * HL * LEVELS, WIDE + FIRST), 0)
    mine = row == (piece * HL + r) * LEVELS + level
    last = lax.axis_index("lat") == jnp.where(parity == 0, lats - 1, 0)
    seam = jnp.where(last, (quadrant // 2).astype(f32), 0.0)
    label = 2.0 * jnp.sum(jnp.where(mine, spread, 0.0), axis=0, keepdims=True) + seam
    eye = lax.broadcasted_iota(jnp.int32, (SPAN, WIDE), 0) == lax.broadcasted_iota(jnp.int32, (SPAN, WIDE), 1)
    column = jnp.sum(jnp.where(eye, label[:, :WIDE], 0.0), axis=1, keepdims=True)
    return [jnp.where(column == queries, 0.0, BLANK) for queries in (label[:, :FIRST], label[:, WIDE:])]


def project(x, gain, offset, weight, bias, qkv_ref):
    xhat, _ = normalise(x)
    normed = (xhat * gain + offset).astype(bf16)
    queries = (dot(normed, weight[:, :D]) + bias[:, :D]).astype(bf16) * jnp.array(HEAD**-0.5, bf16)
    qkv_ref[:, :D] = queries
    qkv_ref[:, D:] = (dot(normed, weight[:, D:]) + bias[:, D:]).astype(bf16)


def attend(x, blank, bias_of, out_weight, out_bias, qkv_ref, probs_ref):
    keys, values = qkv_ref[:, D : 2 * D], qkv_ref[:, 2 * D :]

    def soften(s, tile):
        s = s + bias_of(tile) + blank[tile // HEADS]
        e = jnp.exp(s - jnp.max(s, axis=0, keepdims=True))
        p = e * (1.0 / jnp.sum(e, axis=0, keepdims=True))
        probs_ref[:, pl.ds(tile * FIRST, FIRST)] = p.astype(bf16)

    for g in range(HEADS // GROUP):
        scores = dot_nt(keys[:, g * 256 : (g + 1) * 256], stack(qkv_ref[:FIRST, main_lanes(g)]))
        for h in range(GROUP):
            soften(scores[:, h * FIRST : (h + 1) * FIRST], g * GROUP + h)
    soften(dot_nt(keys, stack(qkv_ref[FIRST:, :D])), HEADS)
    first = [
        unstack(dot_tn(probs_ref[:, columns_of(g)], values[:, g * 256 : (g + 1) * 256])) for g in range(HEADS // GROUP)
    ]
    rest = unstack(dot_tn(probs_ref[:, HEADS * FIRST :], values))
    heads_out = jnp.concatenate([jnp.concatenate(first, axis=1).astype(bf16), rest.astype(bf16)], axis=0)
    return x + dot(heads_out, out_weight) + out_bias


def block_backward(grad, dheads, x, gain, weight, qkv_ref, probs_ref, dqkv_ref):
    keys, values = qkv_ref[:, D : 2 * D], qkv_ref[:, 2 * D :]

    def harden(dprobs, columns):
        pf = probs_ref[:, columns].astype(f32)
        weighted = pf * dprobs
        return (weighted - pf * jnp.sum(weighted, axis=0, keepdims=True)).astype(bf16)

    last = slice(HEADS * FIRST, HEADS * FIRST + HEADS * REST)
    q_rest, do_rest = stack(qkv_ref[FIRST:, :D]), stack(dheads[FIRST:])
    ds_rest = harden(dot_nt(values, do_rest), last)
    dqkv_ref[FIRST:, :D] = (unstack(dot_tn(ds_rest, keys)) * HEAD**-0.5).astype(bf16)
    dk_rest, dv_rest = dot(ds_rest, q_rest), dot(probs_ref[:, last], do_rest)
    for g in range(HEADS // GROUP):
        lanes = slice(g * 256, (g + 1) * 256)
        q4, do4 = stack(qkv_ref[:FIRST, main_lanes(g)]), stack(dheads[:FIRST, lanes])
        ds = harden(dot_nt(values[:, lanes], do4), columns_of(g))
        dq = unstack(dot_tn(ds, keys[:, lanes])) * HEAD**-0.5
        dqkv_ref[:FIRST, lanes] = dq.astype(bf16)
        dqkv_ref[:, pl.ds(D + g * 256, 256)] = (dot(ds, q4) + dk_rest[:, lanes]).astype(bf16)
        dv = dot(probs_ref[:, columns_of(g)], do4) + dv_rest[:, lanes]
        dqkv_ref[:, pl.ds(2 * D + g * 256, 256)] = dv.astype(bf16)
    dnormed = dot_nt(dqkv_ref[...], weight)
    xhat, rstd = normalise(x)
    dxhat = dnormed * gain
    dx = rstd * (
        dxhat
        - jnp.mean(dxhat, axis=-1, keepdims=True)
        - xhat * jnp.mean(dxhat * xhat, axis=-1, keepdims=True)
    )
    return grad.astype(f32) + dx


COARSE_ROWS, COARSE_COLS = HL // 2 + 1, HN // 2
POINTS = COARSE_ROWS * COARSE_COLS
COTANGENT_AT = PAIRS
COARSE_AT = 2 * PAIRS
CLASS_AT = 2 * PAIRS + 2 * POINTS


TILES = CLASS_AT + HL


def pack_kernel(
    tokens_hbm, cotangent_hbm, coarse_hbm, classes_hbm, o0, o1, o2, o3,
    tokens, cotangent, coarse, classes, buffers, in_sems, out_sems,
):
    arrivals = [
        pltpu.make_async_copy(src, dst, in_sems.at[n])
        for n, (src, dst) in enumerate(
            ((tokens_hbm, tokens), (cotangent_hbm, cotangent), (coarse_hbm, coarse), (classes_hbm, classes))
        )
    ]
    for copy in arrivals:
        copy.start()
    buffers[:, pl.ds(CLASS_AT, HL)] = jnp.zeros((4, HL, LEVELS, D), bf16)
    for copy in arrivals:
        copy.wait()
    departures = []
    for q in (1, 3, 2, 0):
        later, right = piece_cut(*divmod(q, 2))
        lat, lon = HL * later, HN * right
        low_lat, low_lon = (coarse.shape[0] - COARSE_ROWS) * later, COARSE_COLS * right
        for r in range(HL):
            buffers[q, pl.ds(r * HN, HN)] = tokens[lat + r, pl.ds(lon, HN)]
            buffers[q, pl.ds(COTANGENT_AT + r * HN, HN)] = cotangent[lat + r, pl.ds(lon, HN)]
            buffers[q, CLASS_AT + r, :, pl.ds(0, WIN_LON)] = classes[lat + r].astype(f32).astype(bf16)
        for r in range(COARSE_ROWS):
            for half in range(2):
                buffers[q, pl.ds(COARSE_AT + POINTS * half + r * COARSE_COLS, COARSE_COLS)] = coarse[
                    low_lat + r, pl.ds(low_lon, COARSE_COLS), :, pl.ds(D * half, D)
                ]
        copy = pltpu.make_async_copy(buffers.at[q], (o0, o1, o2, o3)[q], out_sems.at[q])
        copy.start()
        departures.append(copy)
    for copy in departures:
        copy.wait()


def lookup_kernel(inputs_ref, out_ref, rest_ref, low, high, packed_low, packed_high, parts, spots):
    token = lax.broadcasted_iota(jnp.int32, (SPAN, 1), 0)
    quadrant, r, c, level = token_place(token)
    old = level * (WIN_LAT * WIN_LON) + (quadrant // 2 * HL + r) * WIN_LON + quadrant % 2 * HN + c
    order = (lax.broadcasted_iota(jnp.int32, (SPAN, SPAN), 1) == old).astype(f32).astype(bf16)
    index = inputs_ref[:SPAN, :SPAN].astype(jnp.int32)
    rest = SPAN - 128

    lane = lax.broadcasted_iota(jnp.int32, (rest, WIDE), 1)
    spread = (lane % rest == lax.broadcasted_iota(jnp.int32, (rest, WIDE), 0)).astype(f32).astype(bf16)
    own = (
        lax.broadcasted_iota(jnp.int32, (SPAN, WIDE), 1) // rest
        == lax.broadcasted_iota(jnp.int32, (SPAN, WIDE), 0) % rest
    )
    for part, full, packed in ((index % WIDE, low, packed_low), (index // WIDE, high, packed_high)):
        moved = dot_nt(dot_nt(order, part.astype(f32).astype(bf16)).astype(bf16), order)
        full[...] = moved[:, :128]
        tail = jnp.where(own, dot(moved[:, 128:].astype(bf16), spread), 0.0)
        for g in range(SPAN // rest):
            packed[pl.ds(g, 1), :] = jnp.sum(tail[rest * g : rest * (g + 1)], axis=0, keepdims=True)

    left = inputs_ref[SPAN:]
    blocks = left.shape[1] // WIDE
    for k in range(3):
        piece = left.astype(bf16)
        left = left - piece.astype(f32)
        for b in range(blocks):
            parts[pl.ds((b * 3 + k) * 2 * HEADS, 2 * HEADS), :] = piece[:, b * WIDE : (b + 1) * WIDE]
    entries = parts[...]
    ids = lax.broadcasted_iota(jnp.int32, (16, WIDE), 0).astype(f32)
    ids = [(ids + 16 * n).astype(bf16) for n in range(WIDE // 16)]
    one, zero = jnp.ones((16, WIDE), bf16), jnp.zeros((16, WIDE), bf16)

    def look(low_row, high_row):
        wanted = jnp.broadcast_to(low_row, (16, WIDE)).astype(bf16)
        hot = jnp.concatenate([jnp.where(wanted == i, one, zero) for i in ids], axis=0)
        found = dot(entries, hot)
        sums = []
        for b in range(blocks):
            at = [found[(b * 3 + k) * 2 * HEADS : (b * 3 + k + 1) * 2 * HEADS] for k in range(3)]
            sums.append(at[0] + at[1] + at[2])
        result = sums[0]
        for b in range(1, blocks):
            result = jnp.where(high_row == b, sums[b], result)
        return result

    def two_rows(i):
        def pair(ref):
            return jnp.concatenate([ref[pl.ds(i, 1), :], ref[pl.ds(i + 1, 1), :]], axis=1)

        result = look(pair(low), pair(high))
        for n in range(2):
            for half in range(2):
                out_ref[pl.ds(half * HEADS * SPAN + i + n, HEADS, stride=SPAN), :] = result[
                    half * HEADS : (half + 1) * HEADS, n * 128 : (n + 1) * 128
                ]

    @pl.loop(0, SPAN // 48)
    def _(step):
        for n in range(24):
            two_rows(48 * step + 2 * n)

    block = lax.broadcasted_iota(jnp.int32, (HEADS, 128), 1) // rest
    head = lax.broadcasted_iota(jnp.int32, (HEADS, 128), 0)
    for g in range(SPAN // rest):
        result = look(packed_low[pl.ds(g, 1), :], packed_high[pl.ds(g, 1), :])
        for first in range(0, WIDE, 128):
            for half in range(2):
                rows = result[half * HEADS : (half + 1) * HEADS, first : first + 128]
                rows = pltpu.roll(rows, 0, axis=1, stride=rest, stride_axis=0)
                for n in range(128 // rest):
                    at = half * HEADS * SPAN + rest * g + first // rest + n
                    spots[pl.ds(at, HEADS, stride=SPAN), :] = jnp.where(block == (head + n) % HEADS, rows, 0.0)
    lane = lax.broadcasted_iota(jnp.int32, (8, 128), 1)
    turn = (lane + rest * lax.broadcasted_iota(jnp.int32, (8, 128), 0)) % 128
    for half in range(2):
        for k in range(0, SPAN, 8):
            total = spots[pl.ds(half * HEADS * SPAN + k, 8), :]
            for h in range(1, HEADS):
                total = total + spots[pl.ds((half * HEADS + h) * SPAN + k, 8), :]
            rest_ref[pl.ds(half * SPAN + k, 8), :] = jnp.take_along_axis(
                total, turn, axis=1, mode="promise_in_bounds"
            )


def lookup(relative_index, encoder_table, decoder_table):
    blocks = -(-encoder_table.shape[1] // WIDE)

    def placed(rows, at):
        return jnp.pad(rows, ((at, SPAN + 2 * HEADS - at - rows.shape[0]), (0, blocks * WIDE - rows.shape[1])))

    inputs = placed(relative_index, 0).astype(f32) + placed(encoder_table, SPAN) + placed(decoder_table, SPAN + HEADS)
    return pl.pallas_call(
        lookup_kernel,
        out_shape=[
            jax.ShapeDtypeStruct((2 * HEADS * SPAN, FIRST), f32),
            jax.ShapeDtypeStruct((2 * SPAN, HEADS * REST), f32),
        ],
        scratch_shapes=[
            pltpu.VMEM((SPAN, 128), f32),
            pltpu.VMEM((SPAN, 128), f32),
            pltpu.VMEM((16, WIDE), f32),
            pltpu.VMEM((16, WIDE), f32),
            pltpu.VMEM((blocks * 3 * 2 * HEADS, WIDE), bf16),
            pltpu.VMEM((2 * HEADS * SPAN, 128), f32),
        ],
        compiler_params=pltpu.CompilerParams(vmem_limit_bytes=32 * 2**20),
        cost_estimate=pl.CostEstimate(flops=3_000_000_000, bytes_accessed=4_000_000, transcendentals=0),
        name="lookup",
    )(inputs)


POINT_ROWS = 4 * LEVELS * POINTS


def fine_place(t):
    quadrant, r, c, level = token_place(t)
    row, column = quadrant // 2 * HL + r + HL % 2, quadrant % 2 * HN + c + HN % 2
    point = row // 4 * 2 * POINTS + column // 2 // COARSE_COLS * POINTS
    point = point + row // 2 % 2 * COARSE_COLS + column // 2 % COARSE_COLS
    return (row % 2 * 2 + column % 2) * POINT_ROWS + LEVELS * point + level


def main_kernel(
    lats, b0, b1, b3, b2, bias_main, bias_rest,
    e_gain, e_offset, e_bias, e_out_bias, d_gain, d_offset, d_bias, d_out_bias, split_bias,
    e_weight, e_out_weight, d_weight, d_out_weight, split,
    o0, o1, o2, o3,
    in_tokens, in_cotangent, out_decoded, out_tokens, coarse, coarse_grad,
    e_qkv, e_probs, d_qkv, d_probs, d_dqkv, e_dqkv,
):
    def bias_tiles(block):
        def tile(h):
            if h == HEADS:
                return bias_rest[pl.ds(block * SPAN, SPAN), :]
            return bias_main[pl.ds((block * HEADS + h) * SPAN, SPAN), :]

        return tile

    parity = column_parity()
    parts, outs = (b0, b1, b2, b3), (o0, o1, o2, o3)
    gather_quadrants(parts, 0, in_tokens, parity)
    tokens = whole(in_tokens)
    project(tokens, e_gain[...], e_offset[...], e_weight, e_bias[...].reshape(1, -1), e_qkv)
    blank = mask_bias(parts, lats, parity)

    for q, ref in enumerate(parts):
        m, n = divmod(q, 2)
        for half in range(2):
            rows = ref[pl.ds(COARSE_AT + POINTS * half, POINTS)].reshape(2 * POINTS, D).astype(f32)
            coarse[swapped(m, parity), pl.ds(2 * POINTS * n, 2 * POINTS), pl.ds(D * half, D)] = rows
    fine = dot(whole(coarse).astype(bf16), split[...]) + split_bias[...]
    fine = jnp.concatenate([fine[:, D * k : D * (k + 1)] for k in range(4)], axis=0)
    shape = (SPAN, 4 * POINT_ROWS)
    token = lax.broadcasted_iota(jnp.int32, (SPAN, 1), 0)
    picks = (lax.broadcasted_iota(jnp.int32, shape, 1) == fine_place(token)).astype(f32).astype(bf16)
    high = fine.astype(bf16)
    upsampled = dot(picks, high) + dot(picks, (fine - high.astype(f32)).astype(bf16))

    gather_quadrants(parts, COTANGENT_AT, in_cotangent, parity)
    grad = whole(in_cotangent).astype(bf16)
    dheads = dot_nt(grad, d_out_weight[...]).astype(bf16)

    encoded = attend(tokens, blank, bias_tiles(0), e_out_weight[...], e_out_bias[...], e_qkv, e_probs).astype(bf16)
    joined = (encoded.astype(f32) + upsampled).astype(bf16).astype(f32)
    project(joined, d_gain[...], d_offset[...], d_weight, d_bias[...].reshape(1, -1), d_qkv)
    decoded = attend(joined, blank, bias_tiles(1), d_out_weight[...], d_out_bias[...], d_qkv, d_probs)
    dx = block_backward(grad, dheads, joined, d_gain[...], d_weight[...], d_qkv, d_probs, d_dqkv)
    fill(out_decoded, decoded)
    scatter_quadrants(out_decoded, outs, 0, parity)

    grad = dx.astype(bf16)
    dheads = dot_nt(grad, e_out_weight[...]).astype(bf16)
    token = lax.broadcasted_iota(jnp.int32, (1, SPAN), 1)
    places = (lax.broadcasted_iota(jnp.int32, shape[::-1], 0) == fine_place(token)).astype(f32).astype(bf16)
    spread = dot(places, grad).astype(bf16)
    spread = jnp.concatenate([spread[POINT_ROWS * k : POINT_ROWS * (k + 1)] for k in range(4)], axis=1)
    fill(coarse_grad, dot_nt(spread, split[...]))
    dx = block_backward(grad, dheads, tokens, e_gain[...], e_weight[...], e_qkv, e_probs, e_dqkv)
    for q, ref in enumerate(outs):
        m, n = divmod(q, 2)
        for half in range(2):
            rows = coarse_grad[swapped(m, parity), pl.ds(2 * POINTS * n, 2 * POINTS), pl.ds(D * half, D)]
            ref[pl.ds(COARSE_AT + POINTS * half, POINTS)] = rows.astype(bf16).reshape(POINTS, LEVELS, D)
    fill(out_tokens, dx)
    scatter_quadrants(out_tokens, outs, PAIRS, parity)


def home_kernel(h0, h1, h3, h2, decoded, tokens_gradient, coarse_gradient, total, sems):
    copies = []
    total[...] = jnp.zeros_like(total)
    for q, ref in enumerate((h0, h1, h2, h3)):
        later, right = piece_cut(*divmod(q, 2))
        for n, out in enumerate((decoded, tokens_gradient)):
            for r in range(HL):
                copy = pltpu.make_async_copy(
                    ref.at[pl.ds(PAIRS * n + r * HN, HN)],
                    out.at[HL * later + r, pl.ds(HN * right, HN)],
                    sems.at[len(copies)],
                )
                copy.start()
                copies.append(copy)
        for half in range(2):
            for r in range(COARSE_ROWS):
                for c in range(COARSE_COLS):
                    part = ref[COARSE_AT + POINTS * half + r * COARSE_COLS + c].astype(f32)
                    total[later + r, COARSE_COLS * right + c, :, pl.ds(D * half, D)] += part
    coarse_gradient[...] = total[...].astype(bf16)
    for copy in copies:
        copy.wait()


VM = pl.BlockSpec(memory_space=pltpu.VMEM)


ANY = pl.BlockSpec(memory_space=pl.ANY)


def call(kernel, name, inputs, outs, scratch, flops, in_specs=None, out_specs=None, vmem=32):
    return pl.pallas_call(
        kernel,
        out_shape=outs,
        in_specs=in_specs or [VM] * len(inputs),
        out_specs=out_specs or [VM] * len(outs),
        scratch_shapes=scratch,
        compiler_params=pltpu.CompilerParams(vmem_limit_bytes=vmem * 2**20),
        cost_estimate=pl.CostEstimate(flops=flops, bytes_accessed=flops // 1000, transcendentals=0),
        name=name,
    )(*inputs)


def exchange(pieces, lats, lons, back):
    out = list(pieces)
    for q in (1, 3, 2):
        m, n = divmod(q, 2)
        pairs = []
        for i in range(lats):
            for j in range(lons):
                to = (j - n) % lons
                step = m * (1 if to % 2 else -1)
                pairs.append((i * lons + j, (i + step) % lats * lons + to))
        if back:
            pairs = [(target, source) for source, target in pairs]
        out[q] = lax.ppermute(pieces[q], ("lat", "lon"), pairs)
    return out


def per_device(
    lats, lons,
    tokens, coarse, output_cotangent, token_class, relative_index,
    encoder_gain, encoder_offset, encoder_projection, encoder_projection_bias,
    encoder_output_weight, encoder_output_bias, encoder_table,
    decoder_gain, decoder_offset, decoder_projection, decoder_projection_bias,
    decoder_output_weight, decoder_output_bias, decoder_table,
    split_weight, split_bias,
):
    def row(v):
        return v.reshape(1, -1)

    s = jax.ShapeDtypeStruct
    packed = call(
        pack_kernel,
        "pack",
        [
            jnp.transpose(tokens, (1, 2, 0, 3)),
            jnp.transpose(output_cotangent, (1, 2, 0, 3)),
            jnp.transpose(coarse, (1, 2, 0, 3)),
            jnp.transpose(token_class, (1, 0, 2)),
        ],
        [s((TILES, LEVELS, D), bf16)] * 4,
        [
            pltpu.VMEM((WIN_LAT, WIN_LON, LEVELS, D), bf16),
            pltpu.VMEM((WIN_LAT, WIN_LON, LEVELS, D), bf16),
            pltpu.VMEM((WIN_LAT // 2, WIN_LON // 2, LEVELS, 2 * D), bf16),
            pltpu.VMEM((WIN_LAT, LEVELS, WIN_LON), jnp.int32),
            pltpu.VMEM((4, TILES, LEVELS, D), bf16),
            pltpu.SemaphoreType.DMA((4,)),
            pltpu.SemaphoreType.DMA((4,)),
        ],
        100_000_000,
        [ANY] * 4,
        [ANY] * 4,
        60,
    )
    parts = exchange(packed, lats, lons, False)
    biases = lookup(relative_index, encoder_table, decoder_table)
    outs = call(
        functools.partial(main_kernel, lats),
        "main",
        [
            parts[0], parts[1], parts[3], parts[2], *biases,
            row(encoder_gain), row(encoder_offset), encoder_projection_bias, row(encoder_output_bias),
            row(decoder_gain), row(decoder_offset), decoder_projection_bias, row(decoder_output_bias),
            row(split_bias),
            encoder_projection, encoder_output_weight, decoder_projection, decoder_output_weight, split_weight,
        ],
        [s((CLASS_AT, LEVELS, D), bf16)] * 4,
        [
            pltpu.VMEM((2, SPAN // 2, D), f32),
            pltpu.VMEM((2, SPAN // 2, D), f32),
            pltpu.VMEM((2, SPAN // 2, D), f32),
            pltpu.VMEM((2, SPAN // 2, D), f32),
            pltpu.VMEM((2, POINT_ROWS // 2, 2 * D), f32),
            pltpu.VMEM((2, POINT_ROWS // 2, 2 * D), f32),
            pltpu.VMEM((SPAN, 3 * D), bf16),
            pltpu.VMEM((SPAN, HEADS * SPAN), bf16),
            pltpu.VMEM((SPAN, 3 * D), bf16),
            pltpu.VMEM((SPAN, HEADS * SPAN), bf16),
            pltpu.VMEM((SPAN, 3 * D), bf16),
            pltpu.VMEM((SPAN, 3 * D), bf16),
        ],
        8_000_000_000,
    )
    home = exchange(outs, lats, lons, True)
    grid = s((WIN_LAT, WIN_LON, LEVELS, D), bf16)
    low = s((WIN_LAT // 2, WIN_LON // 2, LEVELS, 2 * D), bf16)
    results = call(
        home_kernel,
        "home",
        [home[0], home[1], home[3], home[2]],
        [grid, grid, low],
        [
            pltpu.VMEM((WIN_LAT // 2, WIN_LON // 2, LEVELS, 2 * D), f32),
            pltpu.SemaphoreType.DMA((4 * 2 * HL,)),
        ],
        1_000_000,
        None,
        [ANY, ANY, VM],
    )
    return tuple(jnp.transpose(r, (2, 0, 1, 3)) for r in results)


def solution(mesh):
    cut = P(None, "lat", "lon", None)
    in_specs = (cut, cut, cut, P(None, "lat", "lon")) + (P(),) * 17
    return jax.shard_map(
        functools.partial(per_device, mesh.shape["lat"], mesh.shape["lon"]),
        mesh=mesh,
        in_specs=in_specs,
        out_specs=(cut, cut, cut),
        check_vma=False,
    )
```

```python
import functools

import jax
import jax.numpy as jnp
from jax import lax
from jax.experimental import pallas as pl
from jax.experimental.pallas import tpu as pltpu
from jax.sharding import PartitionSpec as P

HEADS = 8
LEVELS = 2
WIN_LAT = 6
WIN_LON = 12
SPAN = LEVELS * WIN_LAT * WIN_LON
D = 512
HEAD = D // HEADS
WIDE = 256
FIRST = 128
REST = SPAN - FIRST
HL, HN = WIN_LAT // 2, WIN_LON // 2
PAIRS = HL * HN
GROUP = 4
BLANK = -1e30
eps = 1e-05

f32, bf16 = jnp.float32, jnp.bfloat16
NT = (((1,), (1,)), ((), ()))
TN = (((0,), (0,)), ((), ()))


def dot(a, b):
    return jnp.dot(a, b, preferred_element_type=f32)


def dot_nt(a, b):
    return lax.dot_general(a, b, NT, preferred_element_type=f32)


def dot_tn(a, b):
    return lax.dot_general(a, b, TN, preferred_element_type=f32)


def column_parity():
    return lax.axis_index("lon") % 2


def swapped(m, parity):
    return m + parity * (1 - 2 * m)


def piece_cut(m, n):
    return swapped(1 - m, swapped(n, column_parity())), n


def gather_quadrants(refs, base, scratch, parity):
    for q, ref in enumerate(refs):
        m, n = divmod(q, 2)
        rows = ref[pl.ds(base, PAIRS)].reshape(2 * PAIRS, D).astype(f32)
        scratch[swapped(m, parity), pl.ds(2 * PAIRS * n, 2 * PAIRS), :] = rows


def scatter_quadrants(scratch, refs, base, parity):
    for q, ref in enumerate(refs):
        m, n = divmod(q, 2)
        rows = scratch[swapped(m, parity), pl.ds(2 * PAIRS * n, 2 * PAIRS), :]
        ref[pl.ds(base, PAIRS)] = rows.astype(bf16).reshape(PAIRS, LEVELS, D)


def whole(scratch):
    return scratch[...].reshape(-1, scratch.shape[-1])


def fill(scratch, value):
    scratch[...] = value.reshape(scratch.shape)


def token_place(t):
    rest = t % (2 * PAIRS)
    return t // (2 * PAIRS), rest // (2 * HN), rest % (2 * HN) // 2, rest % 2


def normalise(x):
    centred = x - jnp.mean(x, axis=-1, keepdims=True)
    variance = jnp.mean(centred * centred, axis=-1, keepdims=True)
    rstd = lax.rsqrt(variance + eps)
    return centred * rstd, rstd


def head_of(lanes):
    return lax.broadcasted_iota(jnp.int32, (1, lanes), 1) // HEAD


def stack(x):
    lanes = x.shape[1]
    return jnp.concatenate([x * (head_of(lanes) == h).astype(x.dtype) for h in range(lanes // HEAD)], axis=0)


def unstack(y):
    lanes = y.shape[1]
    rows = y.shape[0] // (lanes // HEAD)
    total = y[:rows]
    for h in range(1, lanes // HEAD):
        total = jnp.where(head_of(lanes) == h, y[h * rows : (h + 1) * rows], total)
    return total


def main_lanes(g):
    return pl.ds(g * GROUP * HEAD, GROUP * HEAD)


def columns_of(g):
    return slice(g * GROUP * FIRST, (g + 1) * GROUP * FIRST)


def mask_bias(refs, lats, parity):
    lane = lax.broadcasted_iota(jnp.int32, (1, WIDE + FIRST), 1)
    token = jnp.where(lane < WIDE, lane, FIRST + lane % REST)
    quadrant, r, c, level = token_place(token)
    place = HN * (quadrant % 2) + c
    hot = lax.broadcasted_iota(jnp.int32, (128, WIDE + FIRST), 0) == place
    rows = jnp.concatenate([ref[CLASS_AT + r, :, :128].astype(f32) for ref in refs for r in range(HL)], axis=0)
    spread = dot(rows.astype(bf16), hot.astype(f32).astype(bf16))
    piece = swapped(quadrant // 2, parity) * 2 + quadrant % 2
    row = lax.broadcasted_iota(jnp.int32, (4 * HL * LEVELS, WIDE + FIRST), 0)
    mine = row == (piece * HL + r) * LEVELS + level
    last = lax.axis_index("lat") == jnp.where(parity == 0, lats - 1, 0)
    seam = jnp.where(last, (quadrant // 2).astype(f32), 0.0)
    label = 2.0 * jnp.sum(jnp.where(mine, spread, 0.0), axis=0, keepdims=True) + seam
    eye = lax.broadcasted_iota(jnp.int32, (SPAN, WIDE), 0) == lax.broadcasted_iota(jnp.int32, (SPAN, WIDE), 1)
    column = jnp.sum(jnp.where(eye, label[:, :WIDE], 0.0), axis=1, keepdims=True)
    return [jnp.where(column == queries, 0.0, BLANK) for queries in (label[:, :FIRST], label[:, WIDE:])]


def project(x, gain, offset, weight, bias, qkv_ref):
    xhat, _ = normalise(x)
    normed = (xhat * gain + offset).astype(bf16)
    queries = (dot(normed, weight[:, :D]) + bias[:, :D]).astype(bf16) * jnp.array(HEAD**-0.5, bf16)
    qkv_ref[:, :D] = queries
    qkv_ref[:, D:] = (dot(normed, weight[:, D:]) + bias[:, D:]).astype(bf16)


def attend(x, blank, bias_of, out_weight, out_bias, qkv_ref, probs_ref):
    keys, values = qkv_ref[:, D : 2 * D], qkv_ref[:, 2 * D :]

    def soften(s, tile):
        s = s + bias_of(tile) + blank[tile // HEADS]
        e = jnp.exp(s - jnp.max(s, axis=0, keepdims=True))
        p = e * (1.0 / jnp.sum(e, axis=0, keepdims=True))
        probs_ref[:, pl.ds(tile * FIRST, FIRST)] = p.astype(bf16)

    for g in range(HEADS // GROUP):
        scores = dot_nt(keys[:, g * 256 : (g + 1) * 256], stack(qkv_ref[:FIRST, main_lanes(g)]))
        for h in range(GROUP):
            soften(scores[:, h * FIRST : (h + 1) * FIRST], g * GROUP + h)
    soften(dot_nt(keys, stack(qkv_ref[FIRST:, :D])), HEADS)
    first = [
        unstack(dot_tn(probs_ref[:, columns_of(g)], values[:, g * 256 : (g + 1) * 256])) for g in range(HEADS // GROUP)
    ]
    rest = unstack(dot_tn(probs_ref[:, HEADS * FIRST :], values))
    heads_out = jnp.concatenate([jnp.concatenate(first, axis=1).astype(bf16), rest.astype(bf16)], axis=0)
    return x + dot(heads_out, out_weight) + out_bias


def block_backward(grad, dheads, x, gain, weight, qkv_ref, probs_ref, dqkv_ref):
    keys, values = qkv_ref[:, D : 2 * D], qkv_ref[:, 2 * D :]

    def harden(dprobs, columns):
        pf = probs_ref[:, columns].astype(f32)
        weighted = pf * dprobs
        return (weighted - pf * jnp.sum(weighted, axis=0, keepdims=True)).astype(bf16)

    last = slice(HEADS * FIRST, HEADS * FIRST + HEADS * REST)
    q_rest, do_rest = stack(qkv_ref[FIRST:, :D]), stack(dheads[FIRST:])
    ds_rest = harden(dot_nt(values, do_rest), last)
    dqkv_ref[FIRST:, :D] = (unstack(dot_tn(ds_rest, keys)) * HEAD**-0.5).astype(bf16)
    dk_rest, dv_rest = dot(ds_rest, q_rest), dot(probs_ref[:, last], do_rest)
    for g in range(HEADS // GROUP):
        lanes = slice(g * 256, (g + 1) * 256)
        q4, do4 = stack(qkv_ref[:FIRST, main_lanes(g)]), stack(dheads[:FIRST, lanes])
        ds = harden(dot_nt(values[:, lanes], do4), columns_of(g))
        dq = unstack(dot_tn(ds, keys[:, lanes])) * HEAD**-0.5
        dqkv_ref[:FIRST, lanes] = dq.astype(bf16)
        dqkv_ref[:, pl.ds(D + g * 256, 256)] = (dot(ds, q4) + dk_rest[:, lanes]).astype(bf16)
        dv = dot(probs_ref[:, columns_of(g)], do4) + dv_rest[:, lanes]
        dqkv_ref[:, pl.ds(2 * D + g * 256, 256)] = dv.astype(bf16)
    dnormed = dot_nt(dqkv_ref[...], weight)
    xhat, rstd = normalise(x)
    dxhat = dnormed * gain
    dx = rstd * (
        dxhat
        - jnp.mean(dxhat, axis=-1, keepdims=True)
        - xhat * jnp.mean(dxhat * xhat, axis=-1, keepdims=True)
    )
    return grad.astype(f32) + dx


COARSE_ROWS, COARSE_COLS = HL // 2 + 1, HN // 2
POINTS = COARSE_ROWS * COARSE_COLS
COTANGENT_AT = PAIRS
COARSE_AT = 2 * PAIRS
CLASS_AT = 2 * PAIRS + 2 * POINTS


TILES = CLASS_AT + HL


def pack_kernel(
    tokens_hbm, cotangent_hbm, coarse_hbm, classes_hbm, o0, o1, o2, o3,
    tokens, cotangent, coarse, classes, buffers, in_sems, out_sems,
):
    arrivals = [
        pltpu.make_async_copy(src, dst, in_sems.at[n])
        for n, (src, dst) in enumerate(
            ((tokens_hbm, tokens), (cotangent_hbm, cotangent), (coarse_hbm, coarse), (classes_hbm, classes))
        )
    ]
    for copy in arrivals:
        copy.start()
    buffers[:, pl.ds(CLASS_AT, HL)] = jnp.zeros((4, HL, LEVELS, D), bf16)
    for copy in arrivals:
        copy.wait()
    departures = []
    for q in (1, 3, 2, 0):
        later, right = piece_cut(*divmod(q, 2))
        lat, lon = HL * later, HN * right
        low_lat, low_lon = (coarse.shape[0] - COARSE_ROWS) * later, COARSE_COLS * right
        for r in range(HL):
            buffers[q, pl.ds(r * HN, HN)] = tokens[lat + r, pl.ds(lon, HN)]
            buffers[q, pl.ds(COTANGENT_AT + r * HN, HN)] = cotangent[lat + r, pl.ds(lon, HN)]
            buffers[q, CLASS_AT + r, :, pl.ds(0, WIN_LON)] = classes[lat + r].astype(f32).astype(bf16)
        for r in range(COARSE_ROWS):
            for half in range(2):
                buffers[q, pl.ds(COARSE_AT + POINTS * half + r * COARSE_COLS, COARSE_COLS)] = coarse[
                    low_lat + r, pl.ds(low_lon, COARSE_COLS), :, pl.ds(D * half, D)
                ]
        copy = pltpu.make_async_copy(buffers.at[q], (o0, o1, o2, o3)[q], out_sems.at[q])
        copy.start()
        departures.append(copy)
    for copy in departures:
        copy.wait()


def lookup_kernel(inputs_ref, out_ref, rest_ref, low, high, packed_low, packed_high, parts, spots):
    token = lax.broadcasted_iota(jnp.int32, (SPAN, 1), 0)
    quadrant, r, c, level = token_place(token)
    old = level * (WIN_LAT * WIN_LON) + (quadrant // 2 * HL + r) * WIN_LON + (1 - quadrant % 2) * HN + c
    order = (lax.broadcasted_iota(jnp.int32, (SPAN, SPAN), 1) == old).astype(f32).astype(bf16)
    index = inputs_ref[:SPAN, :SPAN].astype(jnp.int32)
    rest = SPAN - 128

    lane = lax.broadcasted_iota(jnp.int32, (rest, WIDE), 1)
    spread = (lane % rest == lax.broadcasted_iota(jnp.int32, (rest, WIDE), 0)).astype(f32).astype(bf16)
    own = (
        lax.broadcasted_iota(jnp.int32, (SPAN, WIDE), 1) // rest
        == lax.broadcasted_iota(jnp.int32, (SPAN, WIDE), 0) % rest
    )
    for part, full, packed in ((index % WIDE, low, packed_low), (index // WIDE, high, packed_high)):
        moved = dot_nt(dot_nt(order, part.astype(f32).astype(bf16)).astype(bf16), order)
        full[...] = moved[:, :128]
        tail = jnp.where(own, dot(moved[:, 128:].astype(bf16), spread), 0.0)
        for g in range(SPAN // rest):
            packed[pl.ds(g, 1), :] = jnp.sum(tail[rest * g : rest * (g + 1)], axis=0, keepdims=True)

    left = inputs_ref[SPAN:]
    blocks = left.shape[1] // WIDE
    for k in range(3):
        piece = left.astype(bf16)
        left = left - piece.astype(f32)
        for b in range(blocks):
            parts[pl.ds((b * 3 + k) * 2 * HEADS, 2 * HEADS), :] = piece[:, b * WIDE : (b + 1) * WIDE]
    entries = parts[...]
    ids = lax.broadcasted_iota(jnp.int32, (16, WIDE), 0).astype(f32)
    ids = [(ids + 16 * n).astype(bf16) for n in range(WIDE // 16)]
    one, zero = jnp.ones((16, WIDE), bf16), jnp.zeros((16, WIDE), bf16)

    def look(low_row, high_row):
        wanted = jnp.broadcast_to(low_row, (16, WIDE)).astype(bf16)
        hot = jnp.concatenate([jnp.where(wanted == i, one, zero) for i in ids], axis=0)
        found = dot(entries, hot)
        sums = []
        for b in range(blocks):
            at = [found[(b * 3 + k) * 2 * HEADS : (b * 3 + k + 1) * 2 * HEADS] for k in range(3)]
            sums.append(at[0] + at[1] + at[2])
        result = sums[0]
        for b in range(1, blocks):
            result = jnp.where(high_row == b, sums[b], result)
        return result

    def two_rows(i):
        def pair(ref):
            return jnp.concatenate([ref[pl.ds(i, 1), :], ref[pl.ds(i + 1, 1), :]], axis=1)

        result = look(pair(low), pair(high))
        for n in range(2):
            for half in range(2):
                out_ref[pl.ds(half * HEADS * SPAN + i + n, HEADS, stride=SPAN), :] = result[
                    half * HEADS : (half + 1) * HEADS, n * 128 : (n + 1) * 128
                ]

    @pl.loop(0, SPAN // 48)
    def _(step):
        for n in range(24):
            two_rows(48 * step + 2 * n)

    block = lax.broadcasted_iota(jnp.int32, (HEADS, 128), 1) // rest
    head = lax.broadcasted_iota(jnp.int32, (HEADS, 128), 0)
    for g in range(SPAN // rest):
        result = look(packed_low[pl.ds(g, 1), :], packed_high[pl.ds(g, 1), :])
        for first in range(0, WIDE, 128):
            for half in range(2):
                rows = result[half * HEADS : (half + 1) * HEADS, first : first + 128]
                rows = pltpu.roll(rows, 0, axis=1, stride=rest, stride_axis=0)
                for n in range(128 // rest):
                    at = half * HEADS * SPAN + rest * g + first // rest + n
                    spots[pl.ds(at, HEADS, stride=SPAN), :] = jnp.where(block == (head + n) % HEADS, rows, 0.0)
    lane = lax.broadcasted_iota(jnp.int32, (8, 128), 1)
    turn = (lane + rest * lax.broadcasted_iota(jnp.int32, (8, 128), 0)) % 128
    for half in range(2):
        for k in range(0, SPAN, 8):
            total = spots[pl.ds(half * HEADS * SPAN + k, 8), :]
            for h in range(1, HEADS):
                total = total + spots[pl.ds((half * HEADS + h) * SPAN + k, 8), :]
            rest_ref[pl.ds(half * SPAN + k, 8), :] = jnp.take_along_axis(
                total, turn, axis=1, mode="promise_in_bounds"
            )


def lookup(relative_index, encoder_table, decoder_table):
    blocks = -(-encoder_table.shape[1] // WIDE)

    def placed(rows, at):
        return jnp.pad(rows, ((at, SPAN + 2 * HEADS - at - rows.shape[0]), (0, blocks * WIDE - rows.shape[1])))

    inputs = placed(relative_index, 0).astype(f32) + placed(encoder_table, SPAN) + placed(decoder_table, SPAN + HEADS)
    return pl.pallas_call(
        lookup_kernel,
        out_shape=[
            jax.ShapeDtypeStruct((2 * HEADS * SPAN, FIRST), f32),
            jax.ShapeDtypeStruct((2 * SPAN, HEADS * REST), f32),
        ],
        scratch_shapes=[
            pltpu.VMEM((SPAN, 128), f32),
            pltpu.VMEM((SPAN, 128), f32),
            pltpu.VMEM((16, WIDE), f32),
            pltpu.VMEM((16, WIDE), f32),
            pltpu.VMEM((blocks * 3 * 2 * HEADS, WIDE), bf16),
            pltpu.VMEM((2 * HEADS * SPAN, 128), f32),
        ],
        compiler_params=pltpu.CompilerParams(vmem_limit_bytes=32 * 2**20),
        cost_estimate=pl.CostEstimate(flops=3_000_000_000, bytes_accessed=4_000_000, transcendentals=0),
        name="lookup",
    )(inputs)


POINT_ROWS = 4 * LEVELS * POINTS


def fine_place(t):
    quadrant, r, c, level = token_place(t)
    row, column = quadrant // 2 * HL + r + HL % 2, quadrant % 2 * HN + c + HN % 2
    point = row // 4 * 2 * POINTS + column // 2 // COARSE_COLS * POINTS
    point = point + row // 2 % 2 * COARSE_COLS + column // 2 % COARSE_COLS
    return (row % 2 * 2 + column % 2) * POINT_ROWS + LEVELS * point + level


def main_kernel(
    lats, b0, b1, b3, b2, bias_main, bias_rest,
    e_gain, e_offset, e_bias, e_out_bias, d_gain, d_offset, d_bias, d_out_bias, split_bias,
    e_weight, e_out_weight, d_weight, d_out_weight, split,
    o0, o1, o2, o3,
    in_tokens, in_cotangent, out_decoded, out_tokens, coarse, coarse_grad,
    e_qkv, e_probs, d_qkv, d_probs, d_dqkv, e_dqkv,
):
    def bias_tiles(block):
        def tile(h):
            if h == HEADS:
                return bias_rest[pl.ds(block * SPAN, SPAN), :]
            return bias_main[pl.ds((block * HEADS + h) * SPAN, SPAN), :]

        return tile

    parity = column_parity()
    parts, outs = (b0, b1, b2, b3), (o0, o1, o2, o3)
    gather_quadrants(parts, 0, in_tokens, parity)
    tokens = whole(in_tokens)
    project(tokens, e_gain[...], e_offset[...], e_weight, e_bias[...].reshape(1, -1), e_qkv)
    blank = mask_bias(parts, lats, parity)

    for q, ref in enumerate(parts):
        m, n = divmod(q, 2)
        for half in range(2):
            rows = ref[pl.ds(COARSE_AT + POINTS * half, POINTS)].reshape(2 * POINTS, D).astype(f32)
            coarse[swapped(m, parity), pl.ds(2 * POINTS * n, 2 * POINTS), pl.ds(D * half, D)] = rows
    fine = dot(whole(coarse).astype(bf16), split[...]) + split_bias[...]
    fine = jnp.concatenate([fine[:, D * k : D * (k + 1)] for k in range(4)], axis=0)
    shape = (SPAN, 4 * POINT_ROWS)
    token = lax.broadcasted_iota(jnp.int32, (SPAN, 1), 0)
    picks = (lax.broadcasted_iota(jnp.int32, shape, 1) == fine_place(token)).astype(f32).astype(bf16)
    high = fine.astype(bf16)
    upsampled = dot(picks, high) + dot(picks, (fine - high.astype(f32)).astype(bf16))

    gather_quadrants(parts, COTANGENT_AT, in_cotangent, parity)
    grad = whole(in_cotangent).astype(bf16)
    dheads = dot_nt(grad, d_out_weight[...]).astype(bf16)

    encoded = attend(tokens, blank, bias_tiles(0), e_out_weight[...], e_out_bias[...], e_qkv, e_probs).astype(bf16)
    joined = (encoded.astype(f32) + upsampled).astype(bf16).astype(f32)
    project(joined, d_gain[...], d_offset[...], d_weight, d_bias[...].reshape(1, -1), d_qkv)
    decoded = attend(joined, blank, bias_tiles(1), d_out_weight[...], d_out_bias[...], d_qkv, d_probs)
    dx = block_backward(grad, dheads, joined, d_gain[...], d_weight[...], d_qkv, d_probs, d_dqkv)
    fill(out_decoded, decoded)
    scatter_quadrants(out_decoded, outs, 0, parity)

    grad = dx.astype(bf16)
    dheads = dot_nt(grad, e_out_weight[...]).astype(bf16)
    token = lax.broadcasted_iota(jnp.int32, (1, SPAN), 1)
    places = (lax.broadcasted_iota(jnp.int32, shape[::-1], 0) == fine_place(token)).astype(f32).astype(bf16)
    spread = dot(places, grad).astype(bf16)
    spread = jnp.concatenate([spread[POINT_ROWS * k : POINT_ROWS * (k + 1)] for k in range(4)], axis=1)
    fill(coarse_grad, dot_nt(spread, split[...]))
    dx = block_backward(grad, dheads, tokens, e_gain[...], e_weight[...], e_qkv, e_probs, e_dqkv)
    for q, ref in enumerate(outs):
        m, n = divmod(q, 2)
        for half in range(2):
            rows = coarse_grad[swapped(m, parity), pl.ds(2 * POINTS * n, 2 * POINTS), pl.ds(D * half, D)]
            ref[pl.ds(COARSE_AT + POINTS * half, POINTS)] = rows.astype(bf16).reshape(POINTS, LEVELS, D)
    fill(out_tokens, dx)
    scatter_quadrants(out_tokens, outs, PAIRS, parity)


def home_kernel(h0, h1, h3, h2, decoded, tokens_gradient, coarse_gradient, total, sems):
    copies = []
    total[...] = jnp.zeros_like(total)
    for q, ref in enumerate((h0, h1, h2, h3)):
        later, right = piece_cut(*divmod(q, 2))
        for n, out in enumerate((decoded, tokens_gradient)):
            for r in range(HL):
                copy = pltpu.make_async_copy(
                    ref.at[pl.ds(PAIRS * n + r * HN, HN)],
                    out.at[HL * later + r, pl.ds(HN * right, HN)],
                    sems.at[len(copies)],
                )
                copy.start()
                copies.append(copy)
        for half in range(2):
            for r in range(COARSE_ROWS):
                for c in range(COARSE_COLS):
                    part = ref[COARSE_AT + POINTS * half + r * COARSE_COLS + c].astype(f32)
                    total[later + r, COARSE_COLS * right + c, :, pl.ds(D * half, D)] += part
    coarse_gradient[...] = total[...].astype(bf16)
    for copy in copies:
        copy.wait()


VM = pl.BlockSpec(memory_space=pltpu.VMEM)


ANY = pl.BlockSpec(memory_space=pl.ANY)


def call(kernel, name, inputs, outs, scratch, flops, in_specs=None, out_specs=None, vmem=32):
    return pl.pallas_call(
        kernel,
        out_shape=outs,
        in_specs=in_specs or [VM] * len(inputs),
        out_specs=out_specs or [VM] * len(outs),
        scratch_shapes=scratch,
        compiler_params=pltpu.CompilerParams(vmem_limit_bytes=vmem * 2**20),
        cost_estimate=pl.CostEstimate(flops=flops, bytes_accessed=flops // 1000, transcendentals=0),
        name=name,
    )(*inputs)


def exchange(pieces, lats, lons, back):
    out = list(pieces)
    for q in (1, 3, 2):
        m, n = divmod(q, 2)
        pairs = []
        for i in range(lats):
            for j in range(lons):
                to = (j + n) % lons
                step = m * (1 if to % 2 else -1)
                pairs.append((i * lons + j, (i + step) % lats * lons + to))
        if back:
            pairs = [(target, source) for source, target in pairs]
        out[q] = lax.ppermute(pieces[q], ("lat", "lon"), pairs)
    return out


def per_device(
    lats, lons,
    tokens, coarse, output_cotangent, token_class, relative_index,
    encoder_gain, encoder_offset, encoder_projection, encoder_projection_bias,
    encoder_output_weight, encoder_output_bias, encoder_table,
    decoder_gain, decoder_offset, decoder_projection, decoder_projection_bias,
    decoder_output_weight, decoder_output_bias, decoder_table,
    split_weight, split_bias,
):
    def row(v):
        return v.reshape(1, -1)

    s = jax.ShapeDtypeStruct
    packed = call(
        pack_kernel,
        "pack",
        [
            jnp.transpose(tokens, (1, 2, 0, 3)),
            jnp.transpose(output_cotangent, (1, 2, 0, 3)),
            jnp.transpose(coarse, (1, 2, 0, 3)),
            jnp.transpose(token_class, (1, 0, 2)),
        ],
        [s((TILES, LEVELS, D), bf16)] * 4,
        [
            pltpu.VMEM((WIN_LAT, WIN_LON, LEVELS, D), bf16),
            pltpu.VMEM((WIN_LAT, WIN_LON, LEVELS, D), bf16),
            pltpu.VMEM((WIN_LAT // 2, WIN_LON // 2, LEVELS, 2 * D), bf16),
            pltpu.VMEM((WIN_LAT, LEVELS, WIN_LON), jnp.int32),
            pltpu.VMEM((4, TILES, LEVELS, D), bf16),
            pltpu.SemaphoreType.DMA((4,)),
            pltpu.SemaphoreType.DMA((4,)),
        ],
        100_000_000,
        [ANY] * 4,
        [ANY] * 4,
        60,
    )
    parts = exchange(packed, lats, lons, False)
    biases = lookup(relative_index, encoder_table, decoder_table)
    outs = call(
        functools.partial(main_kernel, lats),
        "main",
        [
            parts[0], parts[1], parts[3], parts[2], *biases,
            row(encoder_gain), row(encoder_offset), encoder_projection_bias, row(encoder_output_bias),
            row(decoder_gain), row(decoder_offset), decoder_projection_bias, row(decoder_output_bias),
            row(split_bias),
            encoder_projection, encoder_output_weight, decoder_projection, decoder_output_weight, split_weight,
        ],
        [s((CLASS_AT, LEVELS, D), bf16)] * 4,
        [
            pltpu.VMEM((2, SPAN // 2, D), f32),
            pltpu.VMEM((2, SPAN // 2, D), f32),
            pltpu.VMEM((2, SPAN // 2, D), f32),
            pltpu.VMEM((2, SPAN // 2, D), f32),
            pltpu.VMEM((2, POINT_ROWS // 2, 2 * D), f32),
            pltpu.VMEM((2, POINT_ROWS // 2, 2 * D), f32),
            pltpu.VMEM((SPAN, 3 * D), bf16),
            pltpu.VMEM((SPAN, HEADS * SPAN), bf16),
            pltpu.VMEM((SPAN, 3 * D), bf16),
            pltpu.VMEM((SPAN, HEADS * SPAN), bf16),
            pltpu.VMEM((SPAN, 3 * D), bf16),
            pltpu.VMEM((SPAN, 3 * D), bf16),
        ],
        8_000_000_000,
    )
    home = exchange(outs, lats, lons, True)
    grid = s((WIN_LAT, WIN_LON, LEVELS, D), bf16)
    low = s((WIN_LAT // 2, WIN_LON // 2, LEVELS, 2 * D), bf16)
    results = call(
        home_kernel,
        "home",
        [home[0], home[1], home[3], home[2]],
        [grid, grid, low],
        [
            pltpu.VMEM((WIN_LAT // 2, WIN_LON // 2, LEVELS, 2 * D), f32),
            pltpu.SemaphoreType.DMA((4 * 2 * HL,)),
        ],
        1_000_000,
        None,
        [ANY, ANY, VM],
    )
    return tuple(jnp.transpose(r, (2, 0, 1, 3)) for r in results)


def solution(mesh):
    cut = P(None, "lat", "lon", None)
    in_specs = (cut, cut, cut, P(None, "lat", "lon")) + (P(),) * 17
    return jax.shard_map(
        functools.partial(per_device, mesh.shape["lat"], mesh.shape["lon"]),
        mesh=mesh,
        in_specs=in_specs,
        out_specs=(cut, cut, cut),
        check_vma=False,
    )
```

```python
import functools

import jax
import jax.numpy as jnp
from jax import lax
from jax.experimental import pallas as pl
from jax.experimental.pallas import tpu as pltpu
from jax.sharding import PartitionSpec as P

HEADS = 8
LEVELS = 2
WIN_LAT = 6
WIN_LON = 12
SPAN = LEVELS * WIN_LAT * WIN_LON
D = 512
HEAD = D // HEADS
WIDE = 256
FIRST = 128
REST = SPAN - FIRST
HL, HN = WIN_LAT // 2, WIN_LON // 2
PAIRS = HL * HN
GROUP = 4
BLANK = -1e30
eps = 1e-05

f32, bf16 = jnp.float32, jnp.bfloat16
NT = (((1,), (1,)), ((), ()))
TN = (((0,), (0,)), ((), ()))


def dot(a, b):
    return jnp.dot(a, b, preferred_element_type=f32)


def dot_nt(a, b):
    return lax.dot_general(a, b, NT, preferred_element_type=f32)


def dot_tn(a, b):
    return lax.dot_general(a, b, TN, preferred_element_type=f32)


def column_parity():
    return lax.axis_index("lon") % 2


def swapped(m, parity):
    return m + parity * (1 - 2 * m)


def piece_cut(m, n):
    return swapped(1 - m, swapped(n, column_parity())), n


def gather_quadrants(refs, base, scratch, parity):
    for q, ref in enumerate(refs):
        m, n = divmod(q, 2)
        rows = ref[pl.ds(base, PAIRS)].reshape(2 * PAIRS, D).astype(f32)
        scratch[swapped(m, parity), pl.ds(2 * PAIRS * n, 2 * PAIRS), :] = rows


def scatter_quadrants(scratch, refs, base, parity):
    for q, ref in enumerate(refs):
        m, n = divmod(q, 2)
        rows = scratch[swapped(m, parity), pl.ds(2 * PAIRS * n, 2 * PAIRS), :]
        ref[pl.ds(base, PAIRS)] = rows.astype(bf16).reshape(PAIRS, LEVELS, D)


def whole(scratch):
    return scratch[...].reshape(-1, scratch.shape[-1])


def fill(scratch, value):
    scratch[...] = value.reshape(scratch.shape)


def token_place(t):
    rest = t % (2 * PAIRS)
    return t // (2 * PAIRS), rest // (2 * HN), rest % (2 * HN) // 2, rest % 2


def normalise(x):
    centred = x - jnp.mean(x, axis=-1, keepdims=True)
    variance = jnp.mean(centred * centred, axis=-1, keepdims=True)
    rstd = lax.rsqrt(variance + eps)
    return centred * rstd, rstd


def head_of(lanes):
    return lax.broadcasted_iota(jnp.int32, (1, lanes), 1) // HEAD


def stack(x):
    lanes = x.shape[1]
    return jnp.concatenate([x * (head_of(lanes) == h).astype(x.dtype) for h in range(lanes // HEAD)], axis=0)


def unstack(y):
    lanes = y.shape[1]
    rows = y.shape[0] // (lanes // HEAD)
    total = y[:rows]
    for h in range(1, lanes // HEAD):
        total = jnp.where(head_of(lanes) == h, y[h * rows : (h + 1) * rows], total)
    return total


def main_lanes(g):
    return pl.ds(g * GROUP * HEAD, GROUP * HEAD)


def columns_of(g):
    return slice(g * GROUP * FIRST, (g + 1) * GROUP * FIRST)


def mask_bias(refs, lats, parity):
    lane = lax.broadcasted_iota(jnp.int32, (1, WIDE + FIRST), 1)
    token = jnp.where(lane < WIDE, lane, FIRST + lane % REST)
    quadrant, r, c, level = token_place(token)
    place = HN * (quadrant % 2) + c
    hot = lax.broadcasted_iota(jnp.int32, (128, WIDE + FIRST), 0) == place
    rows = jnp.concatenate([ref[CLASS_AT + r, :, :128].astype(f32) for ref in refs for r in range(HL)], axis=0)
    spread = dot(rows.astype(bf16), hot.astype(f32).astype(bf16))
    piece = swapped(quadrant // 2, parity) * 2 + quadrant % 2
    row = lax.broadcasted_iota(jnp.int32, (4 * HL * LEVELS, WIDE + FIRST), 0)
    mine = row == (piece * HL + r) * LEVELS + level
    last = lax.axis_index("lat") == jnp.where(parity == 0, lats - 1, 0)
    seam = jnp.where(last, (quadrant // 2).astype(f32), 0.0)
    label = 2.0 * jnp.sum(jnp.where(mine, spread, 0.0), axis=0, keepdims=True) + seam
    eye = lax.broadcasted_iota(jnp.int32, (SPAN, WIDE), 0) == lax.broadcasted_iota(jnp.int32, (SPAN, WIDE), 1)
    column = jnp.sum(jnp.where(eye, label[:, :WIDE], 0.0), axis=1, keepdims=True)
    return [jnp.where(column == queries, 0.0, BLANK) for queries in (label[:, :FIRST], label[:, WIDE:])]


def project(x, gain, offset, weight, bias, qkv_ref):
    xhat, _ = normalise(x)
    normed = (xhat * gain + offset).astype(bf16)
    queries = (dot(normed, weight[:, :D]) + bias[:, :D]).astype(bf16) * jnp.array(HEAD**-0.5, bf16)
    qkv_ref[:, :D] = queries
    qkv_ref[:, D:] = (dot(normed, weight[:, D:]) + bias[:, D:]).astype(bf16)


def attend(x, blank, bias_of, out_weight, out_bias, qkv_ref, probs_ref):
    keys, values = qkv_ref[:, D : 2 * D], qkv_ref[:, 2 * D :]

    def soften(s, tile):
        s = s + bias_of(tile) + blank[tile // HEADS]
        e = jnp.exp(s - jnp.max(s, axis=0, keepdims=True))
        p = e * (1.0 / jnp.sum(e, axis=0, keepdims=True))
        probs_ref[:, pl.ds(tile * FIRST, FIRST)] = p.astype(bf16)

    for g in range(HEADS // GROUP):
        scores = dot_nt(keys[:, g * 256 : (g + 1) * 256], stack(qkv_ref[:FIRST, main_lanes(g)]))
        for h in range(GROUP):
            soften(scores[:, h * FIRST : (h + 1) * FIRST], g * GROUP + h)
    soften(dot_nt(keys, stack(qkv_ref[FIRST:, :D])), HEADS)
    first = [
        unstack(dot_tn(probs_ref[:, columns_of(g)], values[:, g * 256 : (g + 1) * 256])) for g in range(HEADS // GROUP)
    ]
    rest = unstack(dot_tn(probs_ref[:, HEADS * FIRST :], values))
    heads_out = jnp.concatenate([jnp.concatenate(first, axis=1).astype(bf16), rest.astype(bf16)], axis=0)
    return x + dot(heads_out, out_weight) + out_bias


def block_backward(grad, dheads, x, gain, weight, qkv_ref, probs_ref, dqkv_ref):
    keys, values = qkv_ref[:, D : 2 * D], qkv_ref[:, 2 * D :]

    def harden(dprobs, columns):
        pf = probs_ref[:, columns].astype(f32)
        weighted = pf * dprobs
        return (weighted - pf * jnp.sum(weighted, axis=0, keepdims=True)).astype(bf16)

    last = slice(HEADS * FIRST, HEADS * FIRST + HEADS * REST)
    q_rest, do_rest = stack(qkv_ref[FIRST:, :D]), stack(dheads[FIRST:])
    ds_rest = harden(dot_nt(values, do_rest), last)
    dqkv_ref[FIRST:, :D] = (unstack(dot_tn(ds_rest, keys)) * HEAD**-0.5).astype(bf16)
    dk_rest, dv_rest = dot(ds_rest, q_rest), dot(probs_ref[:, last], do_rest)
    for g in range(HEADS // GROUP):
        lanes = slice(g * 256, (g + 1) * 256)
        q4, do4 = stack(qkv_ref[:FIRST, main_lanes(g)]), stack(dheads[:FIRST, lanes])
        ds = harden(dot_nt(values[:, lanes], do4), columns_of(g))
        dq = unstack(dot_tn(ds, keys[:, lanes])) * HEAD**-0.5
        dqkv_ref[:FIRST, lanes] = dq.astype(bf16)
        dqkv_ref[:, pl.ds(D + g * 256, 256)] = (dot(ds, q4) + dk_rest[:, lanes]).astype(bf16)
        dv = dot(probs_ref[:, columns_of(g)], do4) + dv_rest[:, lanes]
        dqkv_ref[:, pl.ds(2 * D + g * 256, 256)] = dv.astype(bf16)
    dnormed = dot_nt(dqkv_ref[...], weight)
    xhat, rstd = normalise(x)
    dxhat = dnormed * gain
    dx = rstd * (
        dxhat
        - jnp.mean(dxhat, axis=-1, keepdims=True)
        - xhat * jnp.mean(dxhat * xhat, axis=-1, keepdims=True)
    )
    return grad.astype(f32) + dx


COARSE_ROWS, COARSE_COLS = HL // 2 + 1, HN // 2
POINTS = COARSE_ROWS * COARSE_COLS
COTANGENT_AT = PAIRS
COARSE_AT = 2 * PAIRS
CLASS_AT = 2 * PAIRS + 2 * POINTS


TILES = CLASS_AT + HL


def pack_kernel(
    tokens_hbm, cotangent_hbm, coarse_hbm, classes_hbm, o0, o1, o2, o3,
    tokens, cotangent, coarse, classes, buffers, in_sems, out_sems,
):
    arrivals = [
        pltpu.make_async_copy(src, dst, in_sems.at[n])
        for n, (src, dst) in enumerate(
            ((tokens_hbm, tokens), (cotangent_hbm, cotangent), (coarse_hbm, coarse), (classes_hbm, classes))
        )
    ]
    for copy in arrivals:
        copy.start()
    buffers[:, pl.ds(CLASS_AT, HL)] = jnp.zeros((4, HL, LEVELS, D), bf16)
    for copy in arrivals:
        copy.wait()
    departures = []
    for q in (1, 3, 2, 0):
        later, right = piece_cut(*divmod(q, 2))
        lat, lon = HL * later, HN * right
        low_lat, low_lon = (coarse.shape[0] - COARSE_ROWS) * later, COARSE_COLS * right
        for r in range(HL):
            buffers[q, pl.ds(r * HN, HN)] = tokens[lat + r, pl.ds(lon, HN)]
            buffers[q, pl.ds(COTANGENT_AT + r * HN, HN)] = cotangent[lat + r, pl.ds(lon, HN)]
            buffers[q, CLASS_AT + r, :, pl.ds(0, WIN_LON)] = classes[lat + r].astype(f32).astype(bf16)
        for r in range(COARSE_ROWS):
            for half in range(2):
                buffers[q, pl.ds(COARSE_AT + POINTS * half + r * COARSE_COLS, COARSE_COLS)] = coarse[
                    low_lat + r, pl.ds(low_lon, COARSE_COLS), :, pl.ds(D * half, D)
                ]
        copy = pltpu.make_async_copy(buffers.at[q], (o0, o1, o2, o3)[q], out_sems.at[q])
        copy.start()
        departures.append(copy)
    for copy in departures:
        copy.wait()


def lookup_kernel(inputs_ref, out_ref, rest_ref, low, high, packed_low, packed_high, parts, spots):
    token = lax.broadcasted_iota(jnp.int32, (SPAN, 1), 0)
    quadrant, r, c, level = token_place(token)
    old = level * (WIN_LAT * WIN_LON) + (quadrant // 2 * HL + r) * WIN_LON + (1 - quadrant % 2) * HN + c
    order = (lax.broadcasted_iota(jnp.int32, (SPAN, SPAN), 1) == old).astype(f32).astype(bf16)
    index = inputs_ref[:SPAN, :SPAN].astype(jnp.int32)
    rest = SPAN - 128

    lane = lax.broadcasted_iota(jnp.int32, (rest, WIDE), 1)
    spread = (lane % rest == lax.broadcasted_iota(jnp.int32, (rest, WIDE), 0)).astype(f32).astype(bf16)
    own = (
        lax.broadcasted_iota(jnp.int32, (SPAN, WIDE), 1) // rest
        == lax.broadcasted_iota(jnp.int32, (SPAN, WIDE), 0) % rest
    )
    for part, full, packed in ((index % WIDE, low, packed_low), (index // WIDE, high, packed_high)):
        moved = dot_nt(dot_nt(order, part.astype(f32).astype(bf16)).astype(bf16), order)
        full[...] = moved[:, :128]
        tail = jnp.where(own, dot(moved[:, 128:].astype(bf16), spread), 0.0)
        for g in range(SPAN // rest):
            packed[pl.ds(g, 1), :] = jnp.sum(tail[rest * g : rest * (g + 1)], axis=0, keepdims=True)

    left = inputs_ref[SPAN:]
    blocks = left.shape[1] // WIDE
    for k in range(3):
        piece = left.astype(bf16)
        left = left - piece.astype(f32)
        for b in range(blocks):
            parts[pl.ds((b * 3 + k) * 2 * HEADS, 2 * HEADS), :] = piece[:, b * WIDE : (b + 1) * WIDE]
    entries = parts[...]
    ids = lax.broadcasted_iota(jnp.int32, (16, WIDE), 0).astype(f32)
    ids = [(ids + 16 * n).astype(bf16) for n in range(WIDE // 16)]
    one, zero = jnp.ones((16, WIDE), bf16), jnp.zeros((16, WIDE), bf16)

    def look(low_row, high_row):
        wanted = jnp.broadcast_to(low_row, (16, WIDE)).astype(bf16)
        hot = jnp.concatenate([jnp.where(wanted == i, one, zero) for i in ids], axis=0)
        found = dot(entries, hot)
        sums = []
        for b in range(blocks):
            at = [found[(b * 3 + k) * 2 * HEADS : (b * 3 + k + 1) * 2 * HEADS] for k in range(3)]
            sums.append(at[0] + at[1] + at[2])
        result = sums[0]
        for b in range(1, blocks):
            result = jnp.where(high_row == b, sums[b], result)
        return result

    def two_rows(i):
        def pair(ref):
            return jnp.concatenate([ref[pl.ds(i, 1), :], ref[pl.ds(i + 1, 1), :]], axis=1)

        result = look(pair(low), pair(high))
        for n in range(2):
            for half in range(2):
                out_ref[pl.ds(half * HEADS * SPAN + i + n, HEADS, stride=SPAN), :] = result[
                    half * HEADS : (half + 1) * HEADS, n * 128 : (n + 1) * 128
                ]

    @pl.loop(0, SPAN // 48)
    def _(step):
        for n in range(24):
            two_rows(48 * step + 2 * n)

    block = lax.broadcasted_iota(jnp.int32, (HEADS, 128), 1) // rest
    head = lax.broadcasted_iota(jnp.int32, (HEADS, 128), 0)
    for g in range(SPAN // rest):
        result = look(packed_low[pl.ds(g, 1), :], packed_high[pl.ds(g, 1), :])
        for first in range(0, WIDE, 128):
            for half in range(2):
                rows = result[half * HEADS : (half + 1) * HEADS, first : first + 128]
                rows = pltpu.roll(rows, 0, axis=1, stride=rest, stride_axis=0)
                for n in range(128 // rest):
                    at = half * HEADS * SPAN + rest * g + first // rest + n
                    spots[pl.ds(at, HEADS, stride=SPAN), :] = jnp.where(block == (head + n) % HEADS, rows, 0.0)
    lane = lax.broadcasted_iota(jnp.int32, (8, 128), 1)
    turn = (lane + rest * lax.broadcasted_iota(jnp.int32, (8, 128), 0)) % 128
    for half in range(2):
        for k in range(0, SPAN, 8):
            total = spots[pl.ds(half * HEADS * SPAN + k, 8), :]
            for h in range(1, HEADS):
                total = total + spots[pl.ds((half * HEADS + h) * SPAN + k, 8), :]
            rest_ref[pl.ds(half * SPAN + k, 8), :] = jnp.take_along_axis(
                total, turn, axis=1, mode="promise_in_bounds"
            )


def lookup(relative_index, encoder_table, decoder_table):
    blocks = -(-encoder_table.shape[1] // WIDE)

    def placed(rows, at):
        return jnp.pad(rows, ((at, SPAN + 2 * HEADS - at - rows.shape[0]), (0, blocks * WIDE - rows.shape[1])))

    inputs = placed(relative_index, 0).astype(f32) + placed(encoder_table, SPAN) + placed(decoder_table, SPAN + HEADS)
    return pl.pallas_call(
        lookup_kernel,
        out_shape=[
            jax.ShapeDtypeStruct((2 * HEADS * SPAN, FIRST), f32),
            jax.ShapeDtypeStruct((2 * SPAN, HEADS * REST), f32),
        ],
        scratch_shapes=[
            pltpu.VMEM((SPAN, 128), f32),
            pltpu.VMEM((SPAN, 128), f32),
            pltpu.VMEM((16, WIDE), f32),
            pltpu.VMEM((16, WIDE), f32),
            pltpu.VMEM((blocks * 3 * 2 * HEADS, WIDE), bf16),
            pltpu.VMEM((2 * HEADS * SPAN, 128), f32),
        ],
        compiler_params=pltpu.CompilerParams(vmem_limit_bytes=32 * 2**20),
        cost_estimate=pl.CostEstimate(flops=3_000_000_000, bytes_accessed=4_000_000, transcendentals=0),
        name="lookup",
    )(inputs)


POINT_ROWS = 4 * LEVELS * POINTS


def fine_place(t):
    quadrant, r, c, level = token_place(t)
    row, column = quadrant // 2 * HL + r + HL % 2, quadrant % 2 * HN + c + HN % 2
    point = row // 4 * 2 * POINTS + column // 2 // COARSE_COLS * POINTS
    point = point + row // 2 % 2 * COARSE_COLS + column // 2 % COARSE_COLS
    return (row % 2 * 2 + column % 2) * POINT_ROWS + LEVELS * point + level


def main_kernel(
    lats, b0, b1, b3, b2, bias_main, bias_rest,
    e_gain, e_offset, e_bias, e_out_bias, d_gain, d_offset, d_bias, d_out_bias, split_bias,
    e_weight, e_out_weight, d_weight, d_out_weight, split,
    o0, o1, o2, o3,
    in_tokens, in_cotangent, out_decoded, out_tokens, coarse, coarse_grad,
    e_qkv, e_probs, d_qkv, d_probs, d_dqkv, e_dqkv,
):
    def bias_tiles(block):
        def tile(h):
            if h == HEADS:
                return bias_rest[pl.ds(block * SPAN, SPAN), :]
            return bias_main[pl.ds((block * HEADS + h) * SPAN, SPAN), :]

        return tile

    parity = column_parity()
    parts, outs = (b0, b1, b2, b3), (o0, o1, o2, o3)
    gather_quadrants(parts, 0, in_tokens, parity)
    tokens = whole(in_tokens)
    project(tokens, e_gain[...], e_offset[...], e_weight, e_bias[...].reshape(1, -1), e_qkv)
    blank = mask_bias(parts, lats, parity)

    for q, ref in enumerate(parts):
        m, n = divmod(q, 2)
        for half in range(2):
            rows = ref[pl.ds(COARSE_AT + POINTS * half, POINTS)].reshape(2 * POINTS, D).astype(f32)
            coarse[swapped(m, parity), pl.ds(2 * POINTS * n, 2 * POINTS), pl.ds(D * half, D)] = rows
    fine = dot(whole(coarse).astype(bf16), split[...]) + split_bias[...]
    fine = jnp.concatenate([fine[:, D * k : D * (k + 1)] for k in range(4)], axis=0)
    shape = (SPAN, 4 * POINT_ROWS)
    token = lax.broadcasted_iota(jnp.int32, (SPAN, 1), 0)
    picks = (lax.broadcasted_iota(jnp.int32, shape, 1) == fine_place(token)).astype(f32).astype(bf16)
    high = fine.astype(bf16)
    upsampled = dot(picks, high) + dot(picks, (fine - high.astype(f32)).astype(bf16))

    gather_quadrants(parts, COTANGENT_AT, in_cotangent, parity)
    grad = whole(in_cotangent).astype(bf16)
    dheads = dot_nt(grad, d_out_weight[...]).astype(bf16)

    encoded = attend(tokens, blank, bias_tiles(0), e_out_weight[...], e_out_bias[...], e_qkv, e_probs).astype(bf16)
    joined = (encoded.astype(f32) + upsampled).astype(bf16).astype(f32)
    project(joined, d_gain[...], d_offset[...], d_weight, d_bias[...].reshape(1, -1), d_qkv)
    decoded = attend(joined, blank, bias_tiles(1), d_out_weight[...], d_out_bias[...], d_qkv, d_probs)
    dx = block_backward(grad, dheads, joined, d_gain[...], d_weight[...], d_qkv, d_probs, d_dqkv)
    fill(out_decoded, decoded)
    scatter_quadrants(out_decoded, outs, 0, parity)

    grad = dx.astype(bf16)
    dheads = dot_nt(grad, e_out_weight[...]).astype(bf16)
    token = lax.broadcasted_iota(jnp.int32, (1, SPAN), 1)
    places = (lax.broadcasted_iota(jnp.int32, shape[::-1], 0) == fine_place(token)).astype(f32).astype(bf16)
    spread = dot(places, grad).astype(bf16)
    spread = jnp.concatenate([spread[POINT_ROWS * k : POINT_ROWS * (k + 1)] for k in range(4)], axis=1)
    fill(coarse_grad, dot_nt(spread, split[...]))
    dx = block_backward(grad, dheads, tokens, e_gain[...], e_weight[...], e_qkv, e_probs, e_dqkv)
    for q, ref in enumerate(outs):
        m, n = divmod(q, 2)
        for half in range(2):
            rows = coarse_grad[swapped(m, parity), pl.ds(2 * POINTS * n, 2 * POINTS), pl.ds(D * half, D)]
            ref[pl.ds(COARSE_AT + POINTS * half, POINTS)] = rows.astype(bf16).reshape(POINTS, LEVELS, D)
    fill(out_tokens, dx)
    scatter_quadrants(out_tokens, outs, PAIRS, parity)


def home_kernel(h0, h1, h3, h2, decoded, tokens_gradient, coarse_gradient, total, rounded, sems):
    refs = (h0, h1, h2, h3)
    copies = []

    def send(src, dst):
        copy = pltpu.make_async_copy(src, dst, sems.at[len(copies)])
        copy.start()
        copies.append(copy)

    for q, ref in enumerate(refs):
        later, right = piece_cut(*divmod(q, 2))
        for n, out in enumerate((decoded, tokens_gradient)):
            for r in range(HL):
                send(ref.at[pl.ds(PAIRS * n + r * HN, HN)], out.at[HL * later + r, pl.ds(HN * right, HN)])
    total[...] = jnp.zeros_like(total)
    for q, ref in enumerate(refs):
        later, right = piece_cut(*divmod(q, 2))
        for half in range(2):
            for r in range(COARSE_ROWS):
                part = ref[pl.ds(COARSE_AT + POINTS * half + r * COARSE_COLS, COARSE_COLS)].astype(f32)
                total[later + r, pl.ds(COARSE_COLS * right, COARSE_COLS), :, pl.ds(D * half, D)] += part
    rounded[...] = total[...].astype(bf16)
    send(rounded, coarse_gradient)
    for copy in copies:
        copy.wait()


VM = pl.BlockSpec(memory_space=pltpu.VMEM)


ANY = pl.BlockSpec(memory_space=pl.ANY)


def call(kernel, name, inputs, outs, scratch, flops, in_specs=None, out_specs=None, vmem=32):
    return pl.pallas_call(
        kernel,
        out_shape=outs,
        in_specs=in_specs or [VM] * len(inputs),
        out_specs=out_specs or [VM] * len(outs),
        scratch_shapes=scratch,
        compiler_params=pltpu.CompilerParams(vmem_limit_bytes=vmem * 2**20),
        cost_estimate=pl.CostEstimate(flops=flops, bytes_accessed=flops // 1000, transcendentals=0),
        name=name,
    )(*inputs)


def exchange(pieces, lats, lons, back):
    out = list(pieces)
    for q in (1, 3, 2):
        m, n = divmod(q, 2)
        pairs = []
        for i in range(lats):
            for j in range(lons):
                to = (j + n) % lons
                step = m * (1 if to % 2 else -1)
                pairs.append((i * lons + j, (i + step) % lats * lons + to))
        if back:
            pairs = [(target, source) for source, target in pairs]
        out[q] = lax.ppermute(pieces[q], ("lat", "lon"), pairs)
    return out


def per_device(
    lats, lons,
    tokens, coarse, output_cotangent, token_class, relative_index,
    encoder_gain, encoder_offset, encoder_projection, encoder_projection_bias,
    encoder_output_weight, encoder_output_bias, encoder_table,
    decoder_gain, decoder_offset, decoder_projection, decoder_projection_bias,
    decoder_output_weight, decoder_output_bias, decoder_table,
    split_weight, split_bias,
):
    def row(v):
        return v.reshape(1, -1)

    s = jax.ShapeDtypeStruct
    packed = call(
        pack_kernel,
        "pack",
        [
            jnp.transpose(tokens, (1, 2, 0, 3)),
            jnp.transpose(output_cotangent, (1, 2, 0, 3)),
            jnp.transpose(coarse, (1, 2, 0, 3)),
            jnp.transpose(token_class, (1, 0, 2)),
        ],
        [s((TILES, LEVELS, D), bf16)] * 4,
        [
            pltpu.VMEM((WIN_LAT, WIN_LON, LEVELS, D), bf16),
            pltpu.VMEM((WIN_LAT, WIN_LON, LEVELS, D), bf16),
            pltpu.VMEM((WIN_LAT // 2, WIN_LON // 2, LEVELS, 2 * D), bf16),
            pltpu.VMEM((WIN_LAT, LEVELS, WIN_LON), jnp.int32),
            pltpu.VMEM((4, TILES, LEVELS, D), bf16),
            pltpu.SemaphoreType.DMA((4,)),
            pltpu.SemaphoreType.DMA((4,)),
        ],
        100_000_000,
        [ANY] * 4,
        [ANY] * 4,
        60,
    )
    parts = exchange(packed, lats, lons, False)
    biases = lookup(relative_index, encoder_table, decoder_table)
    outs = call(
        functools.partial(main_kernel, lats),
        "main",
        [
            parts[0], parts[1], parts[3], parts[2], *biases,
            row(encoder_gain), row(encoder_offset), encoder_projection_bias, row(encoder_output_bias),
            row(decoder_gain), row(decoder_offset), decoder_projection_bias, row(decoder_output_bias),
            row(split_bias),
            encoder_projection, encoder_output_weight, decoder_projection, decoder_output_weight, split_weight,
        ],
        [s((CLASS_AT, LEVELS, D), bf16)] * 4,
        [
            pltpu.VMEM((2, SPAN // 2, D), f32),
            pltpu.VMEM((2, SPAN // 2, D), f32),
            pltpu.VMEM((2, SPAN // 2, D), f32),
            pltpu.VMEM((2, SPAN // 2, D), f32),
            pltpu.VMEM((2, POINT_ROWS // 2, 2 * D), f32),
            pltpu.VMEM((2, POINT_ROWS // 2, 2 * D), f32),
            pltpu.VMEM((SPAN, 3 * D), bf16),
            pltpu.VMEM((SPAN, HEADS * SPAN), bf16),
            pltpu.VMEM((SPAN, 3 * D), bf16),
            pltpu.VMEM((SPAN, HEADS * SPAN), bf16),
            pltpu.VMEM((SPAN, 3 * D), bf16),
            pltpu.VMEM((SPAN, 3 * D), bf16),
        ],
        8_000_000_000,
    )
    home = exchange(outs, lats, lons, True)
    grid = s((WIN_LAT, WIN_LON, LEVELS, D), bf16)
    low = s((WIN_LAT // 2, WIN_LON // 2, LEVELS, 2 * D), bf16)
    results = call(
        home_kernel,
        "home",
        [home[0], home[1], home[3], home[2]],
        [grid, grid, low],
        [
            pltpu.VMEM((WIN_LAT // 2, WIN_LON // 2, LEVELS, 2 * D), f32),
            pltpu.VMEM((WIN_LAT // 2, WIN_LON // 2, LEVELS, 2 * D), bf16),
            pltpu.SemaphoreType.DMA((4 * 2 * HL + 1,)),
        ],
        1_000_000,
        None,
        [ANY] * 3,
    )
    return tuple(jnp.transpose(r, (2, 0, 1, 3)) for r in results)


def solution(mesh):
    cut = P(None, "lat", "lon", None)
    in_specs = (cut, cut, cut, P(None, "lat", "lon")) + (P(),) * 17
    return jax.shard_map(
        functools.partial(per_device, mesh.shape["lat"], mesh.shape["lon"]),
        mesh=mesh,
        in_specs=in_specs,
        out_specs=(cut, cut, cut),
        check_vma=False,
    )
```

```python
import functools

import jax
import jax.numpy as jnp
from jax import lax
from jax.experimental import pallas as pl
from jax.experimental.pallas import tpu as pltpu
from jax.sharding import PartitionSpec as P

HEADS = 8
LEVELS = 2
WIN_LAT = 6
WIN_LON = 12
SPAN = LEVELS * WIN_LAT * WIN_LON
D = 512
HEAD = D // HEADS
WIDE = 256
FIRST = 128
REST = SPAN - FIRST
HL, HN = WIN_LAT // 2, WIN_LON // 2
PAIRS = HL * HN
GROUP = 4
BLANK = -1e30
eps = 1e-05

f32, bf16 = jnp.float32, jnp.bfloat16
NT = (((1,), (1,)), ((), ()))
TN = (((0,), (0,)), ((), ()))


def dot(a, b):
    return jnp.dot(a, b, preferred_element_type=f32)


def dot_nt(a, b):
    return lax.dot_general(a, b, NT, preferred_element_type=f32)


def dot_tn(a, b):
    return lax.dot_general(a, b, TN, preferred_element_type=f32)


def column_parity():
    return lax.axis_index("lon") % 2


def swapped(m, parity):
    return m + parity * (1 - 2 * m)


def piece_cut(m, n):
    return swapped(1 - m, swapped(n, column_parity())), n


def gather_quadrants(refs, base, scratch, parity):
    for q, ref in enumerate(refs):
        m, n = divmod(q, 2)
        rows = ref[pl.ds(base, PAIRS)].reshape(2 * PAIRS, D).astype(f32)
        scratch[swapped(m, parity), pl.ds(2 * PAIRS * n, 2 * PAIRS), :] = rows


def scatter_quadrants(scratch, refs, base, parity):
    for q, ref in enumerate(refs):
        m, n = divmod(q, 2)
        rows = scratch[swapped(m, parity), pl.ds(2 * PAIRS * n, 2 * PAIRS), :]
        ref[pl.ds(base, PAIRS)] = rows.astype(bf16).reshape(PAIRS, LEVELS, D)


def whole(scratch):
    return scratch[...].reshape(-1, scratch.shape[-1])


def fill(scratch, value):
    scratch[...] = value.reshape(scratch.shape)


def token_place(t):
    rest = t % (2 * PAIRS)
    return t // (2 * PAIRS), rest // (2 * HN), rest % (2 * HN) // 2, rest % 2


def normalise(x):
    centred = x - jnp.mean(x, axis=-1, keepdims=True)
    variance = jnp.mean(centred * centred, axis=-1, keepdims=True)
    rstd = lax.rsqrt(variance + eps)
    return centred * rstd, rstd


def head_of(lanes):
    return lax.broadcasted_iota(jnp.int32, (1, lanes), 1) // HEAD


def stack(x):
    lanes = x.shape[1]
    return jnp.concatenate([x * (head_of(lanes) == h).astype(x.dtype) for h in range(lanes // HEAD)], axis=0)


def unstack(y):
    lanes = y.shape[1]
    rows = y.shape[0] // (lanes // HEAD)
    total = y[:rows]
    for h in range(1, lanes // HEAD):
        total = jnp.where(head_of(lanes) == h, y[h * rows : (h + 1) * rows], total)
    return total


def main_lanes(g):
    return pl.ds(g * GROUP * HEAD, GROUP * HEAD)


def columns_of(g):
    return slice(g * GROUP * FIRST, (g + 1) * GROUP * FIRST)


def mask_bias(refs, lats, parity):
    lane = lax.broadcasted_iota(jnp.int32, (1, WIDE + FIRST), 1)
    token = jnp.where(lane < WIDE, lane, FIRST + lane % REST)
    quadrant, r, c, level = token_place(token)
    place = HN * (quadrant % 2) + c
    hot = lax.broadcasted_iota(jnp.int32, (128, WIDE + FIRST), 0) == place
    rows = jnp.concatenate([ref[CLASS_AT + r, :, :128].astype(f32) for ref in refs for r in range(HL)], axis=0)
    spread = dot(rows.astype(bf16), hot.astype(f32).astype(bf16))
    piece = swapped(quadrant // 2, parity) * 2 + quadrant % 2
    row = lax.broadcasted_iota(jnp.int32, (4 * HL * LEVELS, WIDE + FIRST), 0)
    mine = row == (piece * HL + r) * LEVELS + level
    last = lax.axis_index("lat") == jnp.where(parity == 0, lats - 1, 0)
    seam = jnp.where(last, (quadrant // 2).astype(f32), 0.0)
    label = 2.0 * jnp.sum(jnp.where(mine, spread, 0.0), axis=0, keepdims=True) + seam
    eye = lax.broadcasted_iota(jnp.int32, (SPAN, WIDE), 0) == lax.broadcasted_iota(jnp.int32, (SPAN, WIDE), 1)
    column = jnp.sum(jnp.where(eye, label[:, :WIDE], 0.0), axis=1, keepdims=True)
    return [jnp.where(column == queries, 0.0, BLANK) for queries in (label[:, :FIRST], label[:, WIDE:])]


def project(x, gain, offset, weight, bias, qkv_ref, xhat_ref, rstd_ref):
    xhat, rstd = normalise(x)
    xhat_ref[...] = xhat
    rstd_ref[...] = rstd
    normed = (xhat * gain + offset).astype(bf16)
    queries = (dot(normed, weight[:, :D]) + bias[:, :D]).astype(bf16) * jnp.array(HEAD**-0.5, bf16)
    qkv_ref[:, :D] = queries
    qkv_ref[:, D:] = (dot(normed, weight[:, D:]) + bias[:, D:]).astype(bf16)


def attend(x, blank, bias_of, out_weight, out_bias, qkv_ref, probs_ref):
    keys, values = qkv_ref[:, D : 2 * D], qkv_ref[:, 2 * D :]

    def soften(s, tile):
        s = s + bias_of(tile) + blank[tile // HEADS]
        e = jnp.exp(s - jnp.max(s, axis=0, keepdims=True))
        p = e * (1.0 / jnp.sum(e, axis=0, keepdims=True))
        probs_ref[:, pl.ds(tile * FIRST, FIRST)] = p.astype(bf16)

    for g in range(HEADS // GROUP):
        scores = dot_nt(keys[:, g * 256 : (g + 1) * 256], stack(qkv_ref[:FIRST, main_lanes(g)]))
        for h in range(GROUP):
            soften(scores[:, h * FIRST : (h + 1) * FIRST], g * GROUP + h)
    soften(dot_nt(keys, stack(qkv_ref[FIRST:, :D])), HEADS)
    first = [
        unstack(dot_tn(probs_ref[:, columns_of(g)], values[:, g * 256 : (g + 1) * 256])) for g in range(HEADS // GROUP)
    ]
    rest = unstack(dot_tn(probs_ref[:, HEADS * FIRST :], values))
    heads_out = jnp.concatenate([jnp.concatenate(first, axis=1).astype(bf16), rest.astype(bf16)], axis=0)
    return x + dot(heads_out, out_weight) + out_bias


def block_backward(grad, dheads, gain, weight, qkv_ref, probs_ref, dqkv_ref, xhat_ref, rstd_ref):
    keys, values = qkv_ref[:, D : 2 * D], qkv_ref[:, 2 * D :]

    def harden(dprobs, columns):
        pf = probs_ref[:, columns].astype(f32)
        weighted = pf * dprobs
        return (weighted - pf * jnp.sum(weighted, axis=0, keepdims=True)).astype(bf16)

    last = slice(HEADS * FIRST, HEADS * FIRST + HEADS * REST)
    q_rest, do_rest = stack(qkv_ref[FIRST:, :D]), stack(dheads[FIRST:])
    ds_rest = harden(dot_nt(values, do_rest), last)
    dqkv_ref[FIRST:, :D] = (unstack(dot_tn(ds_rest, keys)) * HEAD**-0.5).astype(bf16)
    dk_rest, dv_rest = dot(ds_rest, q_rest), dot(probs_ref[:, last], do_rest)
    for g in range(HEADS // GROUP):
        lanes = slice(g * 256, (g + 1) * 256)
        q4, do4 = stack(qkv_ref[:FIRST, main_lanes(g)]), stack(dheads[:FIRST, lanes])
        ds = harden(dot_nt(values[:, lanes], do4), columns_of(g))
        dq = unstack(dot_tn(ds, keys[:, lanes])) * HEAD**-0.5
        dqkv_ref[:FIRST, lanes] = dq.astype(bf16)
        dqkv_ref[:, pl.ds(D + g * 256, 256)] = (dot(ds, q4) + dk_rest[:, lanes]).astype(bf16)
        dv = dot(probs_ref[:, columns_of(g)], do4) + dv_rest[:, lanes]
        dqkv_ref[:, pl.ds(2 * D + g * 256, 256)] = dv.astype(bf16)
    dnormed = dot_nt(dqkv_ref[...], weight)
    xhat = xhat_ref[...]
    dxhat = dnormed * gain
    dx = rstd_ref[...] * (
        dxhat
        - jnp.mean(dxhat, axis=-1, keepdims=True)
        - xhat * jnp.mean(dxhat * xhat, axis=-1, keepdims=True)
    )
    return grad.astype(f32) + dx


COARSE_ROWS, COARSE_COLS = HL // 2 + 1, HN // 2
POINTS = COARSE_ROWS * COARSE_COLS
COTANGENT_AT = PAIRS
COARSE_AT = 2 * PAIRS
CLASS_AT = 2 * PAIRS + 2 * POINTS


TILES = CLASS_AT + HL


def pack_kernel(
    tokens_hbm, cotangent_hbm, coarse_hbm, classes_hbm, o0, o1, o2, o3,
    tokens, cotangent, coarse, classes, buffers, in_sems, out_sems,
):
    arrivals = [
        pltpu.make_async_copy(src, dst, in_sems.at[n])
        for n, (src, dst) in enumerate(
            ((tokens_hbm, tokens), (cotangent_hbm, cotangent), (coarse_hbm, coarse), (classes_hbm, classes))
        )
    ]
    for copy in arrivals:
        copy.start()
    buffers[:, pl.ds(CLASS_AT, HL)] = jnp.zeros((4, HL, LEVELS, D), bf16)
    for copy in arrivals:
        copy.wait()
    departures = []
    for q in (1, 3, 2, 0):
        later, right = piece_cut(*divmod(q, 2))
        lat, lon = HL * later, HN * right
        low_lat, low_lon = (coarse.shape[0] - COARSE_ROWS) * later, COARSE_COLS * right
        for r in range(HL):
            buffers[q, pl.ds(r * HN, HN)] = tokens[lat + r, pl.ds(lon, HN)]
            buffers[q, pl.ds(COTANGENT_AT + r * HN, HN)] = cotangent[lat + r, pl.ds(lon, HN)]
            buffers[q, CLASS_AT + r, :, pl.ds(0, WIN_LON)] = classes[lat + r].astype(f32).astype(bf16)
        for r in range(COARSE_ROWS):
            for half in range(2):
                buffers[q, pl.ds(COARSE_AT + POINTS * half + r * COARSE_COLS, COARSE_COLS)] = coarse[
                    low_lat + r, pl.ds(low_lon, COARSE_COLS), :, pl.ds(D * half, D)
                ]
        copy = pltpu.make_async_copy(buffers.at[q], (o0, o1, o2, o3)[q], out_sems.at[q])
        copy.start()
        departures.append(copy)
    for copy in departures:
        copy.wait()


def lookup_kernel(inputs_ref, out_ref, rest_ref, low, high, packed_low, packed_high, parts, spots):
    token = lax.broadcasted_iota(jnp.int32, (SPAN, 1), 0)
    quadrant, r, c, level = token_place(token)
    old = level * (WIN_LAT * WIN_LON) + (quadrant // 2 * HL + r) * WIN_LON + (1 - quadrant % 2) * HN + c
    order = (lax.broadcasted_iota(jnp.int32, (SPAN, SPAN), 1) == old).astype(f32).astype(bf16)
    index = inputs_ref[:SPAN, :SPAN].astype(jnp.int32)
    rest = SPAN - 128

    lane = lax.broadcasted_iota(jnp.int32, (rest, WIDE), 1)
    spread = (lane % rest == lax.broadcasted_iota(jnp.int32, (rest, WIDE), 0)).astype(f32).astype(bf16)
    own = (
        lax.broadcasted_iota(jnp.int32, (SPAN, WIDE), 1) // rest
        == lax.broadcasted_iota(jnp.int32, (SPAN, WIDE), 0) % rest
    )
    for part, full, packed in ((index % WIDE, low, packed_low), (index // WIDE, high, packed_high)):
        moved = dot_nt(dot_nt(order, part.astype(f32).astype(bf16)).astype(bf16), order)
        full[...] = moved[:, :128]
        tail = jnp.where(own, dot(moved[:, 128:].astype(bf16), spread), 0.0)
        for g in range(SPAN // rest):
            packed[pl.ds(g, 1), :] = jnp.sum(tail[rest * g : rest * (g + 1)], axis=0, keepdims=True)

    left = inputs_ref[SPAN:]
    blocks = left.shape[1] // WIDE
    for k in range(3):
        piece = left.astype(bf16)
        left = left - piece.astype(f32)
        for b in range(blocks):
            parts[pl.ds((b * 3 + k) * 2 * HEADS, 2 * HEADS), :] = piece[:, b * WIDE : (b + 1) * WIDE]
    entries = parts[...]
    ids = lax.broadcasted_iota(jnp.int32, (16, WIDE), 0).astype(f32)
    ids = [(ids + 16 * n).astype(bf16) for n in range(WIDE // 16)]
    one, zero = jnp.ones((16, WIDE), bf16), jnp.zeros((16, WIDE), bf16)

    def look(low_row, high_row):
        wanted = jnp.broadcast_to(low_row, (16, WIDE)).astype(bf16)
        hot = jnp.concatenate([jnp.where(wanted == i, one, zero) for i in ids], axis=0)
        found = dot(entries, hot)
        sums = []
        for b in range(blocks):
            at = [found[(b * 3 + k) * 2 * HEADS : (b * 3 + k + 1) * 2 * HEADS] for k in range(3)]
            sums.append(at[0] + at[1] + at[2])
        result = sums[0]
        for b in range(1, blocks):
            result = jnp.where(high_row == b, sums[b], result)
        return result

    def two_rows(i):
        def pair(ref):
            return jnp.concatenate([ref[pl.ds(i, 1), :], ref[pl.ds(i + 1, 1), :]], axis=1)

        result = look(pair(low), pair(high))
        for n in range(2):
            for half in range(2):
                out_ref[pl.ds(half * HEADS * SPAN + i + n, HEADS, stride=SPAN), :] = result[
                    half * HEADS : (half + 1) * HEADS, n * 128 : (n + 1) * 128
                ]

    @pl.loop(0, SPAN // 48)
    def _(step):
        for n in range(24):
            two_rows(48 * step + 2 * n)

    block = lax.broadcasted_iota(jnp.int32, (HEADS, 128), 1) // rest
    head = lax.broadcasted_iota(jnp.int32, (HEADS, 128), 0)
    for g in range(SPAN // rest):
        result = look(packed_low[pl.ds(g, 1), :], packed_high[pl.ds(g, 1), :])
        for first in range(0, WIDE, 128):
            for half in range(2):
                rows = result[half * HEADS : (half + 1) * HEADS, first : first + 128]
                rows = pltpu.roll(rows, 0, axis=1, stride=rest, stride_axis=0)
                for n in range(128 // rest):
                    at = half * HEADS * SPAN + rest * g + first // rest + n
                    spots[pl.ds(at, HEADS, stride=SPAN), :] = jnp.where(block == (head + n) % HEADS, rows, 0.0)
    lane = lax.broadcasted_iota(jnp.int32, (8, 128), 1)
    turn = (lane + rest * lax.broadcasted_iota(jnp.int32, (8, 128), 0)) % 128
    for half in range(2):
        for k in range(0, SPAN, 8):
            total = spots[pl.ds(half * HEADS * SPAN + k, 8), :]
            for h in range(1, HEADS):
                total = total + spots[pl.ds((half * HEADS + h) * SPAN + k, 8), :]
            rest_ref[pl.ds(half * SPAN + k, 8), :] = jnp.take_along_axis(
                total, turn, axis=1, mode="promise_in_bounds"
            )


def lookup(relative_index, encoder_table, decoder_table):
    blocks = -(-encoder_table.shape[1] // WIDE)

    def placed(rows, at):
        return jnp.pad(rows, ((at, SPAN + 2 * HEADS - at - rows.shape[0]), (0, blocks * WIDE - rows.shape[1])))

    inputs = placed(relative_index, 0).astype(f32) + placed(encoder_table, SPAN) + placed(decoder_table, SPAN + HEADS)
    return pl.pallas_call(
        lookup_kernel,
        out_shape=[
            jax.ShapeDtypeStruct((2 * HEADS * SPAN, FIRST), f32),
            jax.ShapeDtypeStruct((2 * SPAN, HEADS * REST), f32),
        ],
        scratch_shapes=[
            pltpu.VMEM((SPAN, 128), f32),
            pltpu.VMEM((SPAN, 128), f32),
            pltpu.VMEM((16, WIDE), f32),
            pltpu.VMEM((16, WIDE), f32),
            pltpu.VMEM((blocks * 3 * 2 * HEADS, WIDE), bf16),
            pltpu.VMEM((2 * HEADS * SPAN, 128), f32),
        ],
        compiler_params=pltpu.CompilerParams(vmem_limit_bytes=32 * 2**20),
        cost_estimate=pl.CostEstimate(flops=3_000_000_000, bytes_accessed=4_000_000, transcendentals=0),
        name="lookup",
    )(inputs)


POINT_ROWS = 4 * LEVELS * POINTS


def fine_place(t):
    quadrant, r, c, level = token_place(t)
    row, column = quadrant // 2 * HL + r + HL % 2, quadrant % 2 * HN + c + HN % 2
    point = row // 4 * 2 * POINTS + column // 2 // COARSE_COLS * POINTS
    point = point + row // 2 % 2 * COARSE_COLS + column // 2 % COARSE_COLS
    return (row % 2 * 2 + column % 2) * POINT_ROWS + LEVELS * point + level


def main_kernel(
    lats, b0, b1, b3, b2, bias_main, bias_rest,
    e_gain, e_offset, e_bias, e_out_bias, d_gain, d_offset, d_bias, d_out_bias, split_bias,
    e_weight, e_out_weight, d_weight, d_out_weight, split,
    o0, o1, o2, o3,
    in_tokens, in_cotangent, out_decoded, out_tokens, coarse, coarse_grad,
    e_qkv, e_probs, d_qkv, d_probs, d_dqkv, e_dqkv, e_xhat, d_xhat, e_rstd, d_rstd,
):
    def bias_tiles(block):
        def tile(h):
            if h == HEADS:
                return bias_rest[pl.ds(block * SPAN, SPAN), :]
            return bias_main[pl.ds((block * HEADS + h) * SPAN, SPAN), :]

        return tile

    parity = column_parity()
    parts, outs = (b0, b1, b2, b3), (o0, o1, o2, o3)
    gather_quadrants(parts, 0, in_tokens, parity)
    tokens = whole(in_tokens)
    project(tokens, e_gain[...], e_offset[...], e_weight, e_bias[...].reshape(1, -1), e_qkv, e_xhat, e_rstd)
    blank = mask_bias(parts, lats, parity)

    for q, ref in enumerate(parts):
        m, n = divmod(q, 2)
        for half in range(2):
            rows = ref[pl.ds(COARSE_AT + POINTS * half, POINTS)].reshape(2 * POINTS, D).astype(f32)
            coarse[swapped(m, parity), pl.ds(2 * POINTS * n, 2 * POINTS), pl.ds(D * half, D)] = rows
    fine = dot(whole(coarse).astype(bf16), split[...]) + split_bias[...]
    fine = jnp.concatenate([fine[:, D * k : D * (k + 1)] for k in range(4)], axis=0)
    shape = (SPAN, 4 * POINT_ROWS)
    token = lax.broadcasted_iota(jnp.int32, (SPAN, 1), 0)
    picks = (lax.broadcasted_iota(jnp.int32, shape, 1) == fine_place(token)).astype(f32).astype(bf16)
    high = fine.astype(bf16)
    upsampled = dot(picks, high) + dot(picks, (fine - high.astype(f32)).astype(bf16))

    gather_quadrants(parts, COTANGENT_AT, in_cotangent, parity)
    grad = whole(in_cotangent).astype(bf16)
    dheads = dot_nt(grad, d_out_weight[...]).astype(bf16)

    encoded = attend(tokens, blank, bias_tiles(0), e_out_weight[...], e_out_bias[...], e_qkv, e_probs).astype(bf16)
    joined = (encoded.astype(f32) + upsampled).astype(bf16).astype(f32)
    project(joined, d_gain[...], d_offset[...], d_weight, d_bias[...].reshape(1, -1), d_qkv, d_xhat, d_rstd)
    decoded = attend(joined, blank, bias_tiles(1), d_out_weight[...], d_out_bias[...], d_qkv, d_probs)
    dx = block_backward(grad, dheads, d_gain[...], d_weight[...], d_qkv, d_probs, d_dqkv, d_xhat, d_rstd)
    fill(out_decoded, decoded)
    scatter_quadrants(out_decoded, outs, 0, parity)

    grad = dx.astype(bf16)
    dheads = dot_nt(grad, e_out_weight[...]).astype(bf16)
    token = lax.broadcasted_iota(jnp.int32, (1, SPAN), 1)
    places = (lax.broadcasted_iota(jnp.int32, shape[::-1], 0) == fine_place(token)).astype(f32).astype(bf16)
    spread = dot(places, grad).astype(bf16)
    spread = jnp.concatenate([spread[POINT_ROWS * k : POINT_ROWS * (k + 1)] for k in range(4)], axis=1)
    fill(coarse_grad, dot_nt(spread, split[...]))
    dx = block_backward(grad, dheads, e_gain[...], e_weight[...], e_qkv, e_probs, e_dqkv, e_xhat, e_rstd)
    for q, ref in enumerate(outs):
        m, n = divmod(q, 2)
        for half in range(2):
            rows = coarse_grad[swapped(m, parity), pl.ds(2 * POINTS * n, 2 * POINTS), pl.ds(D * half, D)]
            ref[pl.ds(COARSE_AT + POINTS * half, POINTS)] = rows.astype(bf16).reshape(POINTS, LEVELS, D)
    fill(out_tokens, dx)
    scatter_quadrants(out_tokens, outs, PAIRS, parity)


def home_kernel(h0, h1, h3, h2, decoded, tokens_gradient, coarse_gradient, total, rounded, sems):
    refs = (h0, h1, h2, h3)
    copies = []

    def send(src, dst):
        copy = pltpu.make_async_copy(src, dst, sems.at[len(copies)])
        copy.start()
        copies.append(copy)

    for q, ref in enumerate(refs):
        later, right = piece_cut(*divmod(q, 2))
        for n, out in enumerate((decoded, tokens_gradient)):
            for r in range(HL):
                send(ref.at[pl.ds(PAIRS * n + r * HN, HN)], out.at[HL * later + r, pl.ds(HN * right, HN)])
    total[...] = jnp.zeros_like(total)
    for q, ref in enumerate(refs):
        later, right = piece_cut(*divmod(q, 2))
        for half in range(2):
            for r in range(COARSE_ROWS):
                part = ref[pl.ds(COARSE_AT + POINTS * half + r * COARSE_COLS, COARSE_COLS)].astype(f32)
                total[later + r, pl.ds(COARSE_COLS * right, COARSE_COLS), :, pl.ds(D * half, D)] += part
    rounded[...] = total[...].astype(bf16)
    send(rounded, coarse_gradient)
    for copy in copies:
        copy.wait()


VM = pl.BlockSpec(memory_space=pltpu.VMEM)


ANY = pl.BlockSpec(memory_space=pl.ANY)


def call(kernel, name, inputs, outs, scratch, flops, in_specs=None, out_specs=None, vmem=32):
    return pl.pallas_call(
        kernel,
        out_shape=outs,
        in_specs=in_specs or [VM] * len(inputs),
        out_specs=out_specs or [VM] * len(outs),
        scratch_shapes=scratch,
        compiler_params=pltpu.CompilerParams(vmem_limit_bytes=vmem * 2**20),
        cost_estimate=pl.CostEstimate(flops=flops, bytes_accessed=flops // 1000, transcendentals=0),
        name=name,
    )(*inputs)


def exchange(pieces, lats, lons, back):
    out = list(pieces)
    for q in (1, 3, 2):
        m, n = divmod(q, 2)
        pairs = []
        for i in range(lats):
            for j in range(lons):
                to = (j + n) % lons
                step = m * (1 if to % 2 else -1)
                pairs.append((i * lons + j, (i + step) % lats * lons + to))
        if back:
            pairs = [(target, source) for source, target in pairs]
        out[q] = lax.ppermute(pieces[q], ("lat", "lon"), pairs)
    return out


def per_device(
    lats, lons,
    tokens, coarse, output_cotangent, token_class, relative_index,
    encoder_gain, encoder_offset, encoder_projection, encoder_projection_bias,
    encoder_output_weight, encoder_output_bias, encoder_table,
    decoder_gain, decoder_offset, decoder_projection, decoder_projection_bias,
    decoder_output_weight, decoder_output_bias, decoder_table,
    split_weight, split_bias,
):
    def row(v):
        return v.reshape(1, -1)

    s = jax.ShapeDtypeStruct
    packed = call(
        pack_kernel,
        "pack",
        [
            jnp.transpose(tokens, (1, 2, 0, 3)),
            jnp.transpose(output_cotangent, (1, 2, 0, 3)),
            jnp.transpose(coarse, (1, 2, 0, 3)),
            jnp.transpose(token_class, (1, 0, 2)),
        ],
        [s((TILES, LEVELS, D), bf16)] * 4,
        [
            pltpu.VMEM((WIN_LAT, WIN_LON, LEVELS, D), bf16),
            pltpu.VMEM((WIN_LAT, WIN_LON, LEVELS, D), bf16),
            pltpu.VMEM((WIN_LAT // 2, WIN_LON // 2, LEVELS, 2 * D), bf16),
            pltpu.VMEM((WIN_LAT, LEVELS, WIN_LON), jnp.int32),
            pltpu.VMEM((4, TILES, LEVELS, D), bf16),
            pltpu.SemaphoreType.DMA((4,)),
            pltpu.SemaphoreType.DMA((4,)),
        ],
        100_000_000,
        [ANY] * 4,
        [ANY] * 4,
        60,
    )
    parts = exchange(packed, lats, lons, False)
    biases = lookup(relative_index, encoder_table, decoder_table)
    outs = call(
        functools.partial(main_kernel, lats),
        "main",
        [
            parts[0], parts[1], parts[3], parts[2], *biases,
            row(encoder_gain), row(encoder_offset), encoder_projection_bias, row(encoder_output_bias),
            row(decoder_gain), row(decoder_offset), decoder_projection_bias, row(decoder_output_bias),
            row(split_bias),
            encoder_projection, encoder_output_weight, decoder_projection, decoder_output_weight, split_weight,
        ],
        [s((CLASS_AT, LEVELS, D), bf16)] * 4,
        [
            pltpu.VMEM((2, SPAN // 2, D), f32),
            pltpu.VMEM((2, SPAN // 2, D), f32),
            pltpu.VMEM((2, SPAN // 2, D), f32),
            pltpu.VMEM((2, SPAN // 2, D), f32),
            pltpu.VMEM((2, POINT_ROWS // 2, 2 * D), f32),
            pltpu.VMEM((2, POINT_ROWS // 2, 2 * D), f32),
            pltpu.VMEM((SPAN, 3 * D), bf16),
            pltpu.VMEM((SPAN, HEADS * SPAN), bf16),
            pltpu.VMEM((SPAN, 3 * D), bf16),
            pltpu.VMEM((SPAN, HEADS * SPAN), bf16),
            pltpu.VMEM((SPAN, 3 * D), bf16),
            pltpu.VMEM((SPAN, 3 * D), bf16),
            pltpu.VMEM((SPAN, D), f32),
            pltpu.VMEM((SPAN, D), f32),
            pltpu.VMEM((SPAN, 1), f32),
            pltpu.VMEM((SPAN, 1), f32),
        ],
        8_000_000_000,
    )
    home = exchange(outs, lats, lons, True)
    grid = s((WIN_LAT, WIN_LON, LEVELS, D), bf16)
    low = s((WIN_LAT // 2, WIN_LON // 2, LEVELS, 2 * D), bf16)
    results = call(
        home_kernel,
        "home",
        [home[0], home[1], home[3], home[2]],
        [grid, grid, low],
        [
            pltpu.VMEM((WIN_LAT // 2, WIN_LON // 2, LEVELS, 2 * D), f32),
            pltpu.VMEM((WIN_LAT // 2, WIN_LON // 2, LEVELS, 2 * D), bf16),
            pltpu.SemaphoreType.DMA((4 * 2 * HL + 1,)),
        ],
        1_000_000,
        None,
        [ANY] * 3,
    )
    return tuple(jnp.transpose(r, (2, 0, 1, 3)) for r in results)


def solution(mesh):
    cut = P(None, "lat", "lon", None)
    in_specs = (cut, cut, cut, P(None, "lat", "lon")) + (P(),) * 17
    return jax.shard_map(
        functools.partial(per_device, mesh.shape["lat"], mesh.shape["lon"]),
        mesh=mesh,
        in_specs=in_specs,
        out_specs=(cut, cut, cut),
        check_vma=False,
    )
```

```python
import functools

import jax
import jax.numpy as jnp
from jax import lax
from jax.experimental import pallas as pl
from jax.experimental.pallas import tpu as pltpu
from jax.sharding import PartitionSpec as P

HEADS = 8
LEVELS = 2
WIN_LAT = 6
WIN_LON = 12
SPAN = LEVELS * WIN_LAT * WIN_LON
D = 512
HEAD = D // HEADS
WIDE = 256
FIRST = 128
REST = SPAN - FIRST
HL, HN = WIN_LAT // 2, WIN_LON // 2
PAIRS = HL * HN
GROUP = 4
BLANK = -1e30
eps = 1e-05

f32, bf16 = jnp.float32, jnp.bfloat16
NT = (((1,), (1,)), ((), ()))
TN = (((0,), (0,)), ((), ()))


def dot(a, b):
    return jnp.dot(a, b, preferred_element_type=f32)


def dot_nt(a, b):
    return lax.dot_general(a, b, NT, preferred_element_type=f32)


def dot_tn(a, b):
    return lax.dot_general(a, b, TN, preferred_element_type=f32)


def column_parity():
    return lax.axis_index("lon") % 2


def swapped(m, parity):
    return m + parity * (1 - 2 * m)


def piece_cut(m, n):
    return swapped(1 - m, swapped(n, column_parity())), n


def gather_quadrants(refs, base, scratch, parity):
    for q, ref in enumerate(refs):
        m, n = divmod(q, 2)
        rows = ref[pl.ds(base, PAIRS)].reshape(2 * PAIRS, D).astype(f32)
        scratch[swapped(m, parity), pl.ds(2 * PAIRS * n, 2 * PAIRS), :] = rows


def scatter_quadrants(scratch, refs, base, parity):
    for q, ref in enumerate(refs):
        m, n = divmod(q, 2)
        rows = scratch[swapped(m, parity), pl.ds(2 * PAIRS * n, 2 * PAIRS), :]
        ref[pl.ds(base, PAIRS)] = rows.astype(bf16).reshape(PAIRS, LEVELS, D)


def whole(scratch):
    return scratch[...].reshape(-1, scratch.shape[-1])


def fill(scratch, value):
    scratch[...] = value.reshape(scratch.shape)


def token_place(t):
    rest = t % (2 * PAIRS)
    return t // (2 * PAIRS), rest // (2 * HN), rest % (2 * HN) // 2, rest % 2


def normalise(x):
    centred = x - jnp.mean(x, axis=-1, keepdims=True)
    variance = jnp.mean(centred * centred, axis=-1, keepdims=True)
    rstd = lax.rsqrt(variance + eps)
    return centred * rstd, rstd


def head_of(lanes):
    return lax.broadcasted_iota(jnp.int32, (1, lanes), 1) // HEAD


def stack(x):
    lanes = x.shape[1]
    return jnp.concatenate([x * (head_of(lanes) == h).astype(x.dtype) for h in range(lanes // HEAD)], axis=0)


def unstack(y):
    lanes = y.shape[1]
    rows = y.shape[0] // (lanes // HEAD)
    total = y[:rows]
    for h in range(1, lanes // HEAD):
        total = jnp.where(head_of(lanes) == h, y[h * rows : (h + 1) * rows], total)
    return total


def main_lanes(g):
    return pl.ds(g * GROUP * HEAD, GROUP * HEAD)


def columns_of(g):
    return slice(g * GROUP * FIRST, (g + 1) * GROUP * FIRST)


def mask_bias(refs, lats, parity):
    lane = lax.broadcasted_iota(jnp.int32, (1, WIDE + FIRST), 1)
    token = jnp.where(lane < WIDE, lane, FIRST + lane % REST)
    quadrant, r, c, level = token_place(token)
    place = HN * (quadrant % 2) + c
    hot = lax.broadcasted_iota(jnp.int32, (128, WIDE + FIRST), 0) == place
    rows = jnp.concatenate([ref[CLASS_AT + r, :, :128].astype(f32) for ref in refs for r in range(HL)], axis=0)
    spread = dot(rows.astype(bf16), hot.astype(f32).astype(bf16))
    piece = swapped(quadrant // 2, parity) * 2 + quadrant % 2
    row = lax.broadcasted_iota(jnp.int32, (4 * HL * LEVELS, WIDE + FIRST), 0)
    mine = row == (piece * HL + r) * LEVELS + level
    last = lax.axis_index("lat") == jnp.where(parity == 0, lats - 1, 0)
    seam = jnp.where(last, (quadrant // 2).astype(f32), 0.0)
    label = 2.0 * jnp.sum(jnp.where(mine, spread, 0.0), axis=0, keepdims=True) + seam
    eye = lax.broadcasted_iota(jnp.int32, (SPAN, WIDE), 0) == lax.broadcasted_iota(jnp.int32, (SPAN, WIDE), 1)
    column = jnp.sum(jnp.where(eye, label[:, :WIDE], 0.0), axis=1, keepdims=True)
    return [jnp.where(column == queries, 0.0, BLANK) for queries in (label[:, :FIRST], label[:, WIDE:])]


def project(x, gain, offset, weight, bias, qkv_ref, xhat_ref, rstd_ref):
    xhat, rstd = normalise(x)
    xhat_ref[...] = xhat
    rstd_ref[...] = rstd
    normed = (xhat * gain + offset).astype(bf16)
    queries = (dot(normed, weight[:, :D]) + bias[:, :D]).astype(bf16) * jnp.array(HEAD**-0.5, bf16)
    qkv_ref[:, :D] = queries
    qkv_ref[:, D:] = (dot(normed, weight[:, D:]) + bias[:, D:]).astype(bf16)


def attend(x, blank, bias_of, out_weight, out_bias, qkv_ref, probs_ref):
    keys, values = qkv_ref[:, D : 2 * D], qkv_ref[:, 2 * D :]

    def soften(s, tile):
        s = s + bias_of(tile) + blank[tile // HEADS]
        e = jnp.exp(s - jnp.max(s, axis=0, keepdims=True))
        p = e * (1.0 / jnp.sum(e, axis=0, keepdims=True))
        probs_ref[:, pl.ds(tile * FIRST, FIRST)] = p.astype(bf16)

    for g in range(HEADS // GROUP):
        scores = dot_nt(keys[:, g * 256 : (g + 1) * 256], stack(qkv_ref[:FIRST, main_lanes(g)]))
        for h in range(GROUP):
            soften(scores[:, h * FIRST : (h + 1) * FIRST], g * GROUP + h)
    soften(dot_nt(keys, stack(qkv_ref[FIRST:, :D])), HEADS)
    first = [
        unstack(dot_tn(probs_ref[:, columns_of(g)], values[:, g * 256 : (g + 1) * 256])) for g in range(HEADS // GROUP)
    ]
    rest = unstack(dot_tn(probs_ref[:, HEADS * FIRST :], values))
    heads_out = jnp.concatenate([jnp.concatenate(first, axis=1).astype(bf16), rest.astype(bf16)], axis=0)
    return x + dot(heads_out, out_weight) + out_bias


def block_backward(grad, dheads, gain, weight, qkv_ref, probs_ref, dqkv_ref, xhat_ref, rstd_ref):
    keys, values = qkv_ref[:, D : 2 * D], qkv_ref[:, 2 * D :]

    def harden(dprobs, columns):
        pf = probs_ref[:, columns].astype(f32)
        weighted = pf * dprobs
        return (weighted - pf * jnp.sum(weighted, axis=0, keepdims=True)).astype(bf16)

    last = slice(HEADS * FIRST, HEADS * FIRST + HEADS * REST)
    q_rest, do_rest = stack(qkv_ref[FIRST:, :D]), stack(dheads[FIRST:])
    ds_rest = harden(dot_nt(values, do_rest), last)
    dqkv_ref[FIRST:, :D] = (unstack(dot_tn(ds_rest, keys)) * HEAD**-0.5).astype(bf16)
    dk_rest, dv_rest = dot(ds_rest, q_rest), dot(probs_ref[:, last], do_rest)
    for g in range(HEADS // GROUP):
        lanes = slice(g * 256, (g + 1) * 256)
        q4, do4 = stack(qkv_ref[:FIRST, main_lanes(g)]), stack(dheads[:FIRST, lanes])
        ds = harden(dot_nt(values[:, lanes], do4), columns_of(g))
        dq = unstack(dot_tn(ds, keys[:, lanes])) * HEAD**-0.5
        dqkv_ref[:FIRST, lanes] = dq.astype(bf16)
        dqkv_ref[:, pl.ds(D + g * 256, 256)] = (dot(ds, q4) + dk_rest[:, lanes]).astype(bf16)
        dv = dot(probs_ref[:, columns_of(g)], do4) + dv_rest[:, lanes]
        dqkv_ref[:, pl.ds(2 * D + g * 256, 256)] = dv.astype(bf16)
    dnormed = dot_nt(dqkv_ref[...], weight)
    xhat = xhat_ref[...]
    dxhat = dnormed * gain
    dx = rstd_ref[...] * (
        dxhat
        - jnp.mean(dxhat, axis=-1, keepdims=True)
        - xhat * jnp.mean(dxhat * xhat, axis=-1, keepdims=True)
    )
    return grad.astype(f32) + dx


COARSE_ROWS, COARSE_COLS = HL // 2 + 1, HN // 2
POINTS = COARSE_ROWS * COARSE_COLS
COTANGENT_AT = PAIRS
COARSE_AT = 2 * PAIRS
CLASS_AT = 2 * PAIRS + 2 * POINTS


TILES = CLASS_AT + HL


def pack_kernel(
    tokens_hbm, cotangent_hbm, coarse_hbm, classes_hbm, o0, o1, o2, o3,
    tokens, cotangent, coarse, classes, buffers, in_sems, out_sems,
):
    arrivals = [
        pltpu.make_async_copy(src, dst, in_sems.at[n])
        for n, (src, dst) in enumerate(
            ((tokens_hbm, tokens), (cotangent_hbm, cotangent), (coarse_hbm, coarse), (classes_hbm, classes))
        )
    ]
    for copy in arrivals:
        copy.start()
    buffers[:, pl.ds(CLASS_AT, HL)] = jnp.zeros((4, HL, LEVELS, D), bf16)
    for copy in arrivals:
        copy.wait()
    departures = []
    for q in (1, 3, 2, 0):
        later, right = piece_cut(*divmod(q, 2))
        lat, lon = HL * later, HN * right
        low_lat, low_lon = (coarse.shape[0] - COARSE_ROWS) * later, COARSE_COLS * right
        for r in range(HL):
            buffers[q, pl.ds(r * HN, HN)] = tokens[lat + r, pl.ds(lon, HN)]
            buffers[q, pl.ds(COTANGENT_AT + r * HN, HN)] = cotangent[lat + r, pl.ds(lon, HN)]
            buffers[q, CLASS_AT + r, :, pl.ds(0, WIN_LON)] = classes[lat + r].astype(f32).astype(bf16)
        for r in range(COARSE_ROWS):
            for half in range(2):
                buffers[q, pl.ds(COARSE_AT + POINTS * half + r * COARSE_COLS, COARSE_COLS)] = coarse[
                    low_lat + r, pl.ds(low_lon, COARSE_COLS), :, pl.ds(D * half, D)
                ]
        copy = pltpu.make_async_copy(buffers.at[q], (o0, o1, o2, o3)[q], out_sems.at[q])
        copy.start()
        departures.append(copy)
    for copy in departures:
        copy.wait()


def lookup_kernel(inputs_ref, out_ref, rest_ref, low, high, packed_low, packed_high, parts, spots):
    token = lax.broadcasted_iota(jnp.int32, (SPAN, 1), 0)
    quadrant, r, c, level = token_place(token)
    old = level * (WIN_LAT * WIN_LON) + (quadrant // 2 * HL + r) * WIN_LON + (1 - quadrant % 2) * HN + c
    order = (lax.broadcasted_iota(jnp.int32, (SPAN, SPAN), 1) == old).astype(f32).astype(bf16)
    index = inputs_ref[:SPAN, :SPAN].astype(jnp.int32)
    rest = SPAN - 128

    lane = lax.broadcasted_iota(jnp.int32, (rest, WIDE), 1)
    spread = (lane % rest == lax.broadcasted_iota(jnp.int32, (rest, WIDE), 0)).astype(f32).astype(bf16)
    own = (
        lax.broadcasted_iota(jnp.int32, (SPAN, WIDE), 1) // rest
        == lax.broadcasted_iota(jnp.int32, (SPAN, WIDE), 0) % rest
    )
    for part, full, packed in ((index % WIDE, low, packed_low), (index // WIDE, high, packed_high)):
        moved = dot_nt(dot_nt(order, part.astype(f32).astype(bf16)).astype(bf16), order)
        full[...] = moved[:, :128]
        tail = jnp.where(own, dot(moved[:, 128:].astype(bf16), spread), 0.0)
        for g in range(SPAN // rest):
            packed[pl.ds(g, 1), :] = jnp.sum(tail[rest * g : rest * (g + 1)], axis=0, keepdims=True)

    left = inputs_ref[SPAN:]
    blocks = left.shape[1] // WIDE
    for k in range(3):
        piece = left.astype(bf16)
        left = left - piece.astype(f32)
        for b in range(blocks):
            parts[pl.ds((b * 3 + k) * 2 * HEADS, 2 * HEADS), :] = piece[:, b * WIDE : (b + 1) * WIDE]
    entries = parts[...]
    ids = lax.broadcasted_iota(jnp.int32, (16, WIDE), 0).astype(f32)
    ids = [(ids + 16 * n).astype(bf16) for n in range(WIDE // 16)]
    one, zero = jnp.ones((16, WIDE), bf16), jnp.zeros((16, WIDE), bf16)

    def look(low_row, high_row):
        wanted = jnp.broadcast_to(low_row, (16, WIDE)).astype(bf16)
        hot = jnp.concatenate([jnp.where(wanted == i, one, zero) for i in ids], axis=0)
        found = dot(entries, hot)
        sums = []
        for b in range(blocks):
            at = [found[(b * 3 + k) * 2 * HEADS : (b * 3 + k + 1) * 2 * HEADS] for k in range(3)]
            sums.append(at[0] + at[1] + at[2])
        result = sums[0]
        for b in range(1, blocks):
            result = jnp.where(high_row == b, sums[b], result)
        return result

    def two_rows(i):
        def pair(ref):
            return jnp.concatenate([ref[pl.ds(i, 1), :], ref[pl.ds(i + 1, 1), :]], axis=1)

        result = look(pair(low), pair(high))
        for n in range(2):
            for half in range(2):
                out_ref[pl.ds(half * HEADS * SPAN + i + n, HEADS, stride=SPAN), :] = result[
                    half * HEADS : (half + 1) * HEADS, n * 128 : (n + 1) * 128
                ]

    @pl.loop(0, SPAN // 48)
    def _(step):
        for n in range(24):
            two_rows(48 * step + 2 * n)

    block = lax.broadcasted_iota(jnp.int32, (HEADS, 128), 1) // rest
    head = lax.broadcasted_iota(jnp.int32, (HEADS, 128), 0)
    for g in range(SPAN // rest):
        result = look(packed_low[pl.ds(g, 1), :], packed_high[pl.ds(g, 1), :])
        for first in range(0, WIDE, 128):
            for half in range(2):
                rows = result[half * HEADS : (half + 1) * HEADS, first : first + 128]
                rows = pltpu.roll(rows, 0, axis=1, stride=rest, stride_axis=0)
                for n in range(128 // rest):
                    at = half * HEADS * SPAN + rest * g + first // rest + n
                    spots[pl.ds(at, HEADS, stride=SPAN), :] = jnp.where(block == (head + n) % HEADS, rows, 0.0)
    lane = lax.broadcasted_iota(jnp.int32, (8, 128), 1)
    turn = (lane + rest * lax.broadcasted_iota(jnp.int32, (8, 128), 0)) % 128
    for half in range(2):
        for k in range(0, SPAN, 8):
            total = spots[pl.ds(half * HEADS * SPAN + k, 8), :]
            for h in range(1, HEADS):
                total = total + spots[pl.ds((half * HEADS + h) * SPAN + k, 8), :]
            rest_ref[pl.ds(half * SPAN + k, 8), :] = jnp.take_along_axis(
                total, turn, axis=1, mode="promise_in_bounds"
            )


def lookup(relative_index, encoder_table, decoder_table):
    blocks = -(-encoder_table.shape[1] // WIDE)

    def placed(rows, at):
        return jnp.pad(rows, ((at, SPAN + 2 * HEADS - at - rows.shape[0]), (0, blocks * WIDE - rows.shape[1])))

    inputs = placed(relative_index, 0).astype(f32) + placed(encoder_table, SPAN) + placed(decoder_table, SPAN + HEADS)
    return pl.pallas_call(
        lookup_kernel,
        out_shape=[
            jax.ShapeDtypeStruct((2 * HEADS * SPAN, FIRST), f32),
            jax.ShapeDtypeStruct((2 * SPAN, HEADS * REST), f32),
        ],
        scratch_shapes=[
            pltpu.VMEM((SPAN, 128), f32),
            pltpu.VMEM((SPAN, 128), f32),
            pltpu.VMEM((16, WIDE), f32),
            pltpu.VMEM((16, WIDE), f32),
            pltpu.VMEM((blocks * 3 * 2 * HEADS, WIDE), bf16),
            pltpu.VMEM((2 * HEADS * SPAN, 128), f32),
        ],
        compiler_params=pltpu.CompilerParams(vmem_limit_bytes=32 * 2**20),
        cost_estimate=pl.CostEstimate(flops=3_000_000_000, bytes_accessed=4_000_000, transcendentals=0),
        name="lookup",
    )(inputs)


POINT_ROWS = 4 * LEVELS * POINTS


def fine_place(t):
    quadrant, r, c, level = token_place(t)
    row, column = quadrant // 2 * HL + r + HL % 2, quadrant % 2 * HN + c + HN % 2
    point = row // 4 * 2 * POINTS + column // 2 // COARSE_COLS * POINTS
    point = point + row // 2 % 2 * COARSE_COLS + column // 2 % COARSE_COLS
    return (row % 2 * 2 + column % 2) * POINT_ROWS + LEVELS * point + level


def main_kernel(
    lats, b0, b1, b3, b2, bias_main, bias_rest,
    e_gain, e_offset, e_bias, e_out_bias, d_gain, d_offset, d_bias, d_out_bias, split_bias,
    e_weight, e_out_weight, d_weight, d_out_weight, split,
    o0, o1, o2, o3,
    in_tokens, in_cotangent, out_decoded, out_tokens, coarse, coarse_grad,
    e_qkv, e_probs, d_qkv, d_probs, d_dqkv, e_dqkv, e_xhat, d_xhat, e_rstd, d_rstd,
):
    def bias_tiles(block):
        def tile(h):
            if h == HEADS:
                return bias_rest[pl.ds(block * SPAN, SPAN), :]
            return bias_main[pl.ds((block * HEADS + h) * SPAN, SPAN), :]

        return tile

    parity = column_parity()
    parts, outs = (b0, b1, b2, b3), (o0, o1, o2, o3)
    gather_quadrants(parts, 0, in_tokens, parity)
    tokens = whole(in_tokens)
    project(tokens, e_gain[...], e_offset[...], e_weight, e_bias[...].reshape(1, -1), e_qkv, e_xhat, e_rstd)
    blank = mask_bias(parts, lats, parity)

    for q, ref in enumerate(parts):
        m, n = divmod(q, 2)
        for half in range(2):
            rows = ref[pl.ds(COARSE_AT + POINTS * half, POINTS)].reshape(2 * POINTS, D).astype(f32)
            coarse[swapped(m, parity), pl.ds(2 * POINTS * n, 2 * POINTS), pl.ds(D * half, D)] = rows
    fine = dot(whole(coarse).astype(bf16), split[...]) + split_bias[...]
    fine = jnp.concatenate([fine[:, D * k : D * (k + 1)] for k in range(4)], axis=0)
    shape = (SPAN, 4 * POINT_ROWS)
    token = lax.broadcasted_iota(jnp.int32, (SPAN, 1), 0)
    picks = (lax.broadcasted_iota(jnp.int32, shape, 1) == fine_place(token)).astype(f32).astype(bf16)
    high = fine.astype(bf16)
    upsampled = dot(picks, high) + dot(picks, (fine - high.astype(f32)).astype(bf16))

    gather_quadrants(parts, COTANGENT_AT, in_cotangent, parity)
    grad = whole(in_cotangent).astype(bf16)
    dheads = dot_nt(grad, d_out_weight[...]).astype(bf16)

    encoded = attend(tokens, blank, bias_tiles(0), e_out_weight[...], e_out_bias[...], e_qkv, e_probs).astype(bf16)
    joined = (encoded.astype(f32) + upsampled).astype(bf16).astype(f32)
    project(joined, d_gain[...], d_offset[...], d_weight, d_bias[...].reshape(1, -1), d_qkv, d_xhat, d_rstd)
    decoded = attend(joined, blank, bias_tiles(1), d_out_weight[...], d_out_bias[...], d_qkv, d_probs)
    dx = block_backward(grad, dheads, d_gain[...], d_weight[...], d_qkv, d_probs, d_dqkv, d_xhat, d_rstd)
    fill(out_decoded, decoded)
    scatter_quadrants(out_decoded, outs, 0, parity)

    grad = dx.astype(bf16)
    dheads = dot_nt(grad, e_out_weight[...]).astype(bf16)
    token = lax.broadcasted_iota(jnp.int32, (1, SPAN), 1)
    places = (lax.broadcasted_iota(jnp.int32, shape[::-1], 0) == fine_place(token)).astype(f32).astype(bf16)
    spread = dot(places, grad).astype(bf16)
    spread = jnp.concatenate([spread[POINT_ROWS * k : POINT_ROWS * (k + 1)] for k in range(4)], axis=1)
    fill(coarse_grad, dot_nt(spread, split[...]))
    dx = block_backward(grad, dheads, e_gain[...], e_weight[...], e_qkv, e_probs, e_dqkv, e_xhat, e_rstd)
    for q, ref in enumerate(outs):
        m, n = divmod(q, 2)
        for half in range(2):
            rows = coarse_grad[swapped(m, parity), pl.ds(2 * POINTS * n, 2 * POINTS), pl.ds(D * half, D)]
            ref[pl.ds(COARSE_AT + POINTS * half, POINTS)] = rows.astype(bf16).reshape(POINTS, LEVELS, D)
    fill(out_tokens, dx)
    scatter_quadrants(out_tokens, outs, PAIRS, parity)


def home_kernel(h0, h1, h2, h3, decoded, tokens_gradient, coarse_gradient, total, rounded, sems):
    refs = (h0, h1, h2, h3)
    copies = []

    def send(src, dst):
        copy = pltpu.make_async_copy(src, dst, sems.at[len(copies)])
        copy.start()
        copies.append(copy)

    for q, ref in enumerate(refs):
        later, right = piece_cut(*divmod(q, 2))
        for n, out in enumerate((decoded, tokens_gradient)):
            for r in range(HL):
                send(ref.at[pl.ds(PAIRS * n + r * HN, HN)], out.at[HL * later + r, pl.ds(HN * right, HN)])
    total[...] = jnp.zeros_like(total)
    for q, ref in enumerate(refs):
        later, right = piece_cut(*divmod(q, 2))
        for half in range(2):
            for r in range(COARSE_ROWS):
                part = ref[pl.ds(COARSE_AT + POINTS * half + r * COARSE_COLS, COARSE_COLS)].astype(f32)
                total[later + r, pl.ds(COARSE_COLS * right, COARSE_COLS), :, pl.ds(D * half, D)] += part
    rounded[...] = total[...].astype(bf16)
    send(rounded, coarse_gradient)
    for copy in copies:
        copy.wait()


VM = pl.BlockSpec(memory_space=pltpu.VMEM)


ANY = pl.BlockSpec(memory_space=pl.ANY)


def call(kernel, name, inputs, outs, scratch, flops, in_specs=None, out_specs=None, vmem=32):
    return pl.pallas_call(
        kernel,
        out_shape=outs,
        in_specs=in_specs or [VM] * len(inputs),
        out_specs=out_specs or [VM] * len(outs),
        scratch_shapes=scratch,
        compiler_params=pltpu.CompilerParams(vmem_limit_bytes=vmem * 2**20),
        cost_estimate=pl.CostEstimate(flops=flops, bytes_accessed=flops // 1000, transcendentals=0),
        name=name,
    )(*inputs)


def exchange(pieces, lats, lons, back):
    out = list(pieces)
    for q in (1, 3, 2):
        m, n = divmod(q, 2)
        pairs = []
        for i in range(lats):
            for j in range(lons):
                to = (j + n) % lons
                step = m * (1 if to % 2 else -1)
                pairs.append((i * lons + j, (i + step) % lats * lons + to))
        if back:
            pairs = [(target, source) for source, target in pairs]
        out[q] = lax.ppermute(pieces[q], ("lat", "lon"), pairs)
    return out


def per_device(
    lats, lons,
    tokens, coarse, output_cotangent, token_class, relative_index,
    encoder_gain, encoder_offset, encoder_projection, encoder_projection_bias,
    encoder_output_weight, encoder_output_bias, encoder_table,
    decoder_gain, decoder_offset, decoder_projection, decoder_projection_bias,
    decoder_output_weight, decoder_output_bias, decoder_table,
    split_weight, split_bias,
):
    def row(v):
        return v.reshape(1, -1)

    s = jax.ShapeDtypeStruct
    packed = call(
        pack_kernel,
        "pack",
        [
            jnp.transpose(tokens, (1, 2, 0, 3)),
            jnp.transpose(output_cotangent, (1, 2, 0, 3)),
            jnp.transpose(coarse, (1, 2, 0, 3)),
            jnp.transpose(token_class, (1, 0, 2)),
        ],
        [s((TILES, LEVELS, D), bf16)] * 4,
        [
            pltpu.VMEM((WIN_LAT, WIN_LON, LEVELS, D), bf16),
            pltpu.VMEM((WIN_LAT, WIN_LON, LEVELS, D), bf16),
            pltpu.VMEM((WIN_LAT // 2, WIN_LON // 2, LEVELS, 2 * D), bf16),
            pltpu.VMEM((WIN_LAT, LEVELS, WIN_LON), jnp.int32),
            pltpu.VMEM((4, TILES, LEVELS, D), bf16),
            pltpu.SemaphoreType.DMA((4,)),
            pltpu.SemaphoreType.DMA((4,)),
        ],
        100_000_000,
        [ANY] * 4,
        [ANY] * 4,
        60,
    )
    parts = exchange(packed, lats, lons, False)
    biases = lookup(relative_index, encoder_table, decoder_table)
    outs = call(
        functools.partial(main_kernel, lats),
        "main",
        [
            parts[0], parts[1], parts[3], parts[2], *biases,
            row(encoder_gain), row(encoder_offset), encoder_projection_bias, row(encoder_output_bias),
            row(decoder_gain), row(decoder_offset), decoder_projection_bias, row(decoder_output_bias),
            row(split_bias),
            encoder_projection, encoder_output_weight, decoder_projection, decoder_output_weight, split_weight,
        ],
        [s((CLASS_AT, LEVELS, D), bf16)] * 4,
        [
            pltpu.VMEM((2, SPAN // 2, D), f32),
            pltpu.VMEM((2, SPAN // 2, D), f32),
            pltpu.VMEM((2, SPAN // 2, D), f32),
            pltpu.VMEM((2, SPAN // 2, D), f32),
            pltpu.VMEM((2, POINT_ROWS // 2, 2 * D), f32),
            pltpu.VMEM((2, POINT_ROWS // 2, 2 * D), f32),
            pltpu.VMEM((SPAN, 3 * D), bf16),
            pltpu.VMEM((SPAN, HEADS * SPAN), bf16),
            pltpu.VMEM((SPAN, 3 * D), bf16),
            pltpu.VMEM((SPAN, HEADS * SPAN), bf16),
            pltpu.VMEM((SPAN, 3 * D), bf16),
            pltpu.VMEM((SPAN, 3 * D), bf16),
            pltpu.VMEM((SPAN, D), f32),
            pltpu.VMEM((SPAN, D), f32),
            pltpu.VMEM((SPAN, 1), f32),
            pltpu.VMEM((SPAN, 1), f32),
        ],
        8_000_000_000,
    )
    home = exchange(outs, lats, lons, True)
    grid = s((WIN_LAT, WIN_LON, LEVELS, D), bf16)
    low = s((WIN_LAT // 2, WIN_LON // 2, LEVELS, 2 * D), bf16)
    results = call(
        home_kernel,
        "home",
        list(home),
        [grid, grid, low],
        [
            pltpu.VMEM((WIN_LAT // 2, WIN_LON // 2, LEVELS, 2 * D), f32),
            pltpu.VMEM((WIN_LAT // 2, WIN_LON // 2, LEVELS, 2 * D), bf16),
            pltpu.SemaphoreType.DMA((4 * 2 * HL + 1,)),
        ],
        1_000_000,
        None,
        [ANY] * 3,
    )
    return tuple(jnp.transpose(r, (2, 0, 1, 3)) for r in results)


def solution(mesh):
    cut = P(None, "lat", "lon", None)
    in_specs = (cut, cut, cut, P(None, "lat", "lon")) + (P(),) * 17
    return jax.shard_map(
        functools.partial(per_device, mesh.shape["lat"], mesh.shape["lon"]),
        mesh=mesh,
        in_specs=in_specs,
        out_specs=(cut, cut, cut),
        check_vma=False,
    )
```
